32 devices in a mesh: band: 8 (over z, x), wgrp: 4 (over y, core).
Axes of the slice: x: 2, y: 2, z: 4, core: 2. Of those that a mesh axis runs over, the one named last changes fastest.
Arguments:
- visibilities: bfloat16 [4, 512, 512], P('wgrp', 'band'), may hold values from -6 to 6
- coordinates: bfloat16 [4, 512, 512], P('wgrp', 'band'), may hold values from -16 to 16
- block_index: int32 [4, 512], P('wgrp', 'band'), may hold values from 0 to 63
- counts: int32 [4, 64], P('wgrp', 'band'), may hold values from 1 to 8, as said below
- col_offset: int32 [4, 512], P('wgrp', 'band'), may hold values from 0 to 8160
Outputs:
- image_rows: float32 [4, 2, 256, 8192], P('wgrp', None, 'band')
The draws below stay inside these ranges and needn't reach their ends.
Inputs may be any that keep to these rules, and one draw needn't show every extreme that they name: Entry d of a device's row counts the live slots of its list for band d; every device's entry for band 8 // 2 is exactly 8. `block_index`: slots past a list's count read a block too; their subgrids are zero. `col_offset`: A subgrid lies inside its band's rows and the grid's columns.
All inputs are finite; a program needn't handle non-finite values.
Results may differ from the reference program's by a relative error of at most 0.0036.
Values may be sent and summed in bfloat16 or wider, within the bound.
No kernel may reach another device: no remote copies, remote signals or barrier semaphores. Data moves between devices by JAX's collectives and lax.ppermute only.
A program may use at most 128 MiB of HBM per device.

```python
import math
import jax
import jax.numpy as jnp
from jax import lax

S = 32
G = 8192
K = 256
NBLK = 64
CAP = 8
NW = 4
N_BAND = 8
N_WGRP = 4


def draw_counts(key, part):
    values = jax.random.randint(key, (N_WGRP, N_BAND * N_BAND), 1, CAP + 1)
    column = jnp.arange(N_BAND * N_BAND) % N_BAND
    return jnp.where(column[None, :] == N_BAND // 2, CAP, values).astype(jnp.int32)


def touch_ends(result, rng, smallest, largest):
    longest = result.shape.index(max(result.shape))
    spots = []
    for shift in (0, 1):
        where = [jax.random.randint(jax.random.fold_in(rng, axis), (), 0, length) for axis, length in enumerate(result.shape)]
        where[longest] = (where[longest] + shift) % result.shape[longest]
        spots.append(tuple(where))
    return result.at[spots[0]].set(smallest).at[spots[1]].set(largest)


def steps_of(key, extent, shards, least, high):
    def one(dim, blocks):
        steps = jax.random.uniform(jax.random.fold_in(jax.random.fold_in(key, 6), dim), (blocks,), jnp.float32, least / len(shards), high / len(shards))
        return jnp.repeat(jnp.exp(steps), extent[dim] // blocks).reshape((-1,) + (1,) * (len(extent) - dim - 1))

    level = one(*shards[0])
    for cut in shards[1:]:
        level = level * one(*cut)
    return level


def noise(own_key, shape, spread, limit, split=(), kind=jnp.bfloat16):
    drawn = jax.random.normal(own_key, shape, jnp.float32) * spread
    if len(split) > 0:
        drawn = steps_of(own_key, shape, split, -0.22, 0.18) * drawn
    return jnp.clip(drawn, min=-limit, max=limit).astype(kind)


def setup_inputs(seed: int = 0) -> dict:
    keys = jax.random.split(jax.random.key(seed), 6)
    visibilities = noise(keys[0], (NW, N_BAND * NBLK, 2 * K), 1.0, 6.0, ((0, 4), (1, 8)))
    coordinates = jnp.clip(jax.random.uniform(keys[1], (NW, N_BAND * NBLK, 2 * K), jnp.float32, -16.0, 16.0) * steps_of(keys[1], (NW, N_BAND * NBLK, 2 * K), ((0, 4), (1, 8)), -0.4, 0.0), -16.0, 16.0).astype(jnp.bfloat16)
    block_index = touch_ends(jax.random.randint(keys[2], (NW, N_BAND * N_BAND * CAP), 0, NBLK), jax.random.fold_in(keys[2], 1), 0, NBLK - 1).astype(jnp.int32)
    counts = draw_counts(jax.random.fold_in(keys[5], 71), 0)
    col_offset = touch_ends(jax.random.randint(keys[4], (NW, N_BAND * N_BAND * CAP), 0, G - S + 1), jax.random.fold_in(keys[4], 1), 0, G - S).astype(jnp.int32)
    return dict(visibilities=visibilities, coordinates=coordinates, block_index=block_index, counts=counts, col_offset=col_offset)


TWO_PI = 2.0 * math.pi

def phase_tables(coord_rows):
    samples = coord_rows.shape[1] // 2
    pixel_pos = (jnp.arange(S, dtype=jnp.float32) - S / 2.0) * (TWO_PI / S)
    coords = coord_rows.astype(jnp.float32)
    angle_x = coords[:, None, :samples] * pixel_pos[None, :, None]
    angle_y = coords[:, None, samples:] * pixel_pos[None, :, None]
    return (angle_x, angle_y)

def weighted_rows(vis_rows, angle_x, angle_y):
    samples = vis_rows.shape[1] // 2
    vis_re = vis_rows[:, None, :samples].astype(jnp.float32)
    vis_im = vis_rows[:, None, samples:].astype(jnp.float32)
    cos_x = jnp.cos(angle_x)
    sin_x = jnp.sin(angle_x)
    weighted_re = (vis_re * cos_x - vis_im * sin_x).astype(jnp.bfloat16)
    weighted_im = (vis_re * sin_x + vis_im * cos_x).astype(jnp.bfloat16)
    cos_y = jnp.cos(angle_y).astype(jnp.bfloat16)
    sin_y = jnp.sin(angle_y).astype(jnp.bfloat16)
    return (weighted_re, weighted_im, cos_y, sin_y)

def product(left, right):
    return jnp.einsum('nyk,nxk->nyx', left.astype(jnp.float32), right.astype(jnp.float32))

def make_subgrids(vis_rows, coord_rows):
    angle_x, angle_y = phase_tables(coord_rows)
    weighted_re, weighted_im, cos_y, sin_y = weighted_rows(vis_rows, angle_x, angle_y)
    sub_re = product(cos_y, weighted_re) - product(sin_y, weighted_im)
    sub_im = product(cos_y, weighted_im) + product(sin_y, weighted_re)
    return jnp.stack([sub_re, sub_im], axis=1)

def reference(visibilities, coordinates, block_index, counts, col_offset):
    slot_total = N_BAND * CAP

    def one_group(arrays):
        vis_group, coord_group, block_group, count_group, offset_group = arrays

        def add_source(slab, source):
            vis_store = lax.dynamic_slice_in_dim(vis_group, source * NBLK, NBLK, 0)
            coord_store = lax.dynamic_slice_in_dim(coord_group, source * NBLK, NBLK, 0)
            blocks = lax.dynamic_slice_in_dim(block_group, source * slot_total, slot_total, 0)
            counts_row = lax.dynamic_slice_in_dim(count_group, source * N_BAND, N_BAND, 0)
            offsets = lax.dynamic_slice_in_dim(offset_group, source * slot_total, slot_total, 0)
            slot_live = (jnp.arange(CAP, dtype=jnp.int32)[None, :] < counts_row[:, None]).reshape(-1)
            chosen_vis = jnp.take(vis_store, blocks, axis=0)
            chosen_coord = jnp.take(coord_store, blocks, axis=0)
            subgrids = make_subgrids(chosen_vis, chosen_coord)
            subgrids = subgrids * slot_live.astype(jnp.float32)[:, None, None, None]
            dest_band = (jnp.arange(slot_total, dtype=jnp.int32) // CAP).astype(jnp.int32)
            pixel_index = jnp.arange(S, dtype=jnp.int32)
            row_index = (dest_band[:, None] * S + pixel_index[None, :]).astype(jnp.int32)
            column_index = (offsets[:, None] + pixel_index[None, :]).astype(jnp.int32)
            slab = slab.at[:, row_index[:, :, None], column_index[:, None, :]].add(jnp.transpose(subgrids, (1, 0, 2, 3)))
            return (slab, None)
        empty_slab = jnp.zeros((2, N_BAND * S, G), jnp.float32)
        slab, unused = lax.scan(add_source, empty_slab, jnp.arange(N_BAND, dtype=jnp.int32))
        return slab
    grid = lax.map(one_group, (visibilities, coordinates, block_index, counts, col_offset))
    norm_scale = 1.0 / math.sqrt(G * K)

    def fold_transform(group_index):
        own_slab = grid[group_index]
        mirror_slab = grid[N_WGRP - 1 - group_index][:, ::-1, ::-1]
        folded_re = own_slab[0] + mirror_slab[0]
        folded_im = own_slab[1] - mirror_slab[1]
        spectrum = jnp.fft.fft(lax.complex(folded_re, folded_im), axis=-1)
        return jnp.stack([jnp.real(spectrum), jnp.imag(spectrum)]) * norm_scale
    return lax.map(fold_transform, jnp.arange(N_WGRP, dtype=jnp.int32))
```

```python
import functools
import math

import jax
import jax.numpy as jnp
import numpy as np
from jax import lax
from jax.experimental import pallas as pl
from jax.experimental.pallas import tpu as pltpu
from jax.sharding import PartitionSpec as P

S = 32
G = 8192
K = 256
CAP = 8
HALF = S // 2
N1 = 128
N2 = 64
DATA = 4 * K
ROW = DATA + 128
LO = 64
PI = math.pi

SIN_TERMS = (1.0, -1 / 6, 1 / 120, -1 / 5040, 1 / 362880, -1 / 39916800)
COS_TERMS = (1.0, -1 / 2, 1 / 24, -1 / 720, 1 / 40320, -1 / 3628800, 1 / 479001600)


def transform_tables():
    n1, n2 = np.arange(N1), np.arange(N2)
    outer = np.exp(-2j * np.pi * (np.outer(n1, n1) % N1) / N1)
    inner = np.exp(-2j * np.pi * (np.outer(n2, n2) % N2) / N2)
    twist = np.exp(-2j * np.pi * np.outer(n1, n2) / G) / math.sqrt(G * K)
    pair = np.kron(np.eye(2), inner)

    def real_form(m):
        return np.block([[m.real, -m.imag], [m.imag, m.real]])

    twist = np.concatenate([twist, twist], axis=1)
    return (
        jnp.asarray(real_form(outer), jnp.bfloat16),
        jnp.asarray(real_form(pair), jnp.bfloat16),
        jnp.asarray(np.stack([twist.real, twist.imag]), jnp.float32),
    )


def dot_last(left, right):
    return lax.dot_general(
        left, right, (((1,), (1,)), ((), ())), preferred_element_type=jnp.float32
    )


def dot_first(left, right):
    return lax.dot_general(
        left, right, (((0,), (0,)), ((), ())), preferred_element_type=jnp.float32
    )


def own_base(band_count, group_count):
    low = lax.axis_index("wgrp") < group_count // 2
    return jnp.where(low, 0, band_count), jnp.where(low, band_count, 0)


def pack_kernel(band_count, group_count, vis_ref, coord_ref, block_ref, count_ref, offset_ref, out_ref):
    own, mirror = own_base(band_count, group_count)
    slots = block_ref.shape[1]
    blocks = vis_ref.shape[0]
    lane = lax.broadcasted_iota(jnp.int32, (1, slots), 1)
    list_of = lane // CAP
    within = lane % CAP
    band_row = lax.broadcasted_iota(jnp.int32, (band_count, slots), 0)
    in_list = (band_row == list_of).astype(jnp.float32)
    counts = jnp.broadcast_to(count_ref[...].astype(jnp.float32), (8, band_count))
    live_count = jnp.dot(counts, in_list, preferred_element_type=jnp.float32)[0:1]
    live = (within.astype(jnp.float32) < live_count).astype(jnp.float32)
    chosen = (
        lax.broadcasted_iota(jnp.int32, (blocks, slots), 0) == block_ref[...]
    ).astype(jnp.float32)
    vis = dot_first((chosen * live).astype(jnp.bfloat16), vis_ref[...])
    coord = dot_first(chosen.astype(jnp.bfloat16), coord_ref[...])
    offsets = offset_ref[...]
    here = lax.broadcasted_iota(jnp.int32, (CAP, slots), 0) == within
    high = jnp.where(here, (offsets >> 7).astype(jnp.float32), 0.0).astype(jnp.bfloat16)
    low = jnp.where(here, (offsets & 127).astype(jnp.float32), 0.0).astype(jnp.bfloat16)
    slot_row = lax.broadcasted_iota(jnp.int32, (slots, 128), 0) // CAP
    column = lax.broadcasted_iota(jnp.int32, (slots, 128), 1)
    to_high = (slot_row == column).astype(jnp.bfloat16)
    to_low = (slot_row + LO == column).astype(jnp.bfloat16)
    meta = jnp.dot(high, to_high, preferred_element_type=jnp.float32) + jnp.dot(
        low, to_low, preferred_element_type=jnp.float32
    )
    for d in range(band_count):
        rows = slice(d * CAP, (d + 1) * CAP)
        message = jnp.concatenate([vis[rows], coord[rows], meta], axis=1).astype(jnp.bfloat16)
        out_ref[own + d] = message
        out_ref[mirror + band_count - 1 - d] = message


def square(z):
    re, im = z
    return re * re - im * im, 2.0 * (re * im)


def times(z, w):
    return z[0] * w[0] - z[1] * w[1], z[0] * w[1] + z[1] * w[0]


def unit_phasor(cycles):
    half = (cycles - jnp.round(cycles)) * PI
    x = half * half
    sine = jnp.full_like(x, SIN_TERMS[-1])
    for term in SIN_TERMS[-2::-1]:
        sine = sine * x + term
    cosine = jnp.full_like(x, COS_TERMS[-1])
    for term in COS_TERMS[-2::-1]:
        cosine = cosine * x + term
    sine = sine * half
    return 1.0 - 2.0 * (sine * sine), 2.0 * (sine * cosine)


def grid_kernel(
    band_count,
    group_count,
    recv_ref,
    outer_ref,
    inner_ref,
    twist_ref,
    out_ref,
    offset_vmem,
    offset_smem,
    tab_re,
    tab_im,
    eight_re,
    eight_im,
    grid_ref,
    rows_ref,
    offset_sem,
    out_sem,
):
    own, mirror = own_base(band_count, group_count)
    band = lax.axis_index("band")
    peers = 2 * band_count

    meta = recv_ref[:, :, DATA:].astype(jnp.float32).reshape(peers * CAP, 128)
    pick_row = lax.broadcasted_iota(jnp.int32, (8, 128), 0)
    pick_col = lax.broadcasted_iota(jnp.int32, (8, 128), 1)
    flipped = band_count - 1 - band
    wanted = jnp.where(
        pick_row == 0,
        band,
        jnp.where(pick_row == 1, band + LO, jnp.where(pick_row == 2, flipped, flipped + LO)),
    )
    pick = (pick_col == wanted).astype(jnp.bfloat16)
    picked = dot_last(pick, meta.astype(jnp.bfloat16))
    offset_vmem[0:1] = (picked[0:1] * 128.0 + picked[1:2]).astype(jnp.int32)
    offset_vmem[1:2] = (G - S) - (picked[2:3] * 128.0 + picked[3:4]).astype(jnp.int32)
    to_smem = pltpu.make_async_copy(offset_vmem, offset_smem, offset_sem)
    to_smem.start()

    def clear(step, _):
        grid_ref[pl.ds(pl.multiple_of(step * 2 * S, 2 * S), 2 * S), :] = jnp.zeros(
            (2 * S, 128), jnp.float32
        )
        return 0

    lax.fori_loop(0, (N1 + 2) // 2, clear, 0)
    to_smem.wait()

    lane = lax.broadcasted_iota(jnp.int32, (HALF, 128), 1)
    first_half = lane < N2
    lane_in = lane & (N2 - 1)
    empty = jnp.zeros((S, 2 * K), jnp.bfloat16)
    chunks = 2 * K // 128

    def one_list(peer, mirrored):
        block = recv_ref[peer].astype(jnp.float32)
        vis = (block[:, 0:K], block[:, K : 2 * K])
        e1 = unit_phasor(block[:, 2 * K : 4 * K] * (1.0 / S))
        e2 = square(e1)
        e3 = times(e2, e1)
        e4 = square(e2)
        one = (jnp.ones_like(e1[0]), jnp.zeros_like(e1[0]))
        steps = (one, e1, e2, e3, e4, times(e4, e1), square(e3), times(e4, e3))
        e8 = square(e4)
        for b, e in enumerate(steps):
            place = CAP - 1 - b if mirrored else b
            weighted = vis if b == 0 else times(vis, (e[0][:, :K], e[1][:, :K]))
            for tab, z, e_part in ((tab_re, weighted[0], e[0]), (tab_im, weighted[1], e[1])):
                whole = jnp.concatenate([z, e_part[:, K:]], axis=1)
                for q in range(chunks):
                    tab[pl.ds(q * 8 * CAP + place, CAP, stride=8), :] = whole[:, q * 128 : (q + 1) * 128]
        eight_re[...] = e8[0]
        eight_im[...] = e8[1]
        for c in range(CAP):
            base = tuple(
                jnp.concatenate(
                    [tab[(q * CAP + c) * 8 : (q * CAP + c + 1) * 8, :] for q in range(chunks)], axis=1
                )
                for tab in (tab_re, tab_im)
            )
            c8 = jnp.broadcast_to(eight_re[c : c + 1, :], (8, 2 * K))
            s8 = jnp.broadcast_to(eight_im[c : c + 1, :], (8, 2 * K))
            cc, ss, cs, sc = base[0] * c8, base[1] * s8, base[0] * s8, base[1] * c8
            up = (cc - ss, sc + cs)
            down = (cc + ss, sc - cs)
            down2 = (down[0] * c8 + down[1] * s8, down[1] * c8 - down[0] * s8)
            order = (up, base, down, down2) if mirrored else (down2, down, base, up)
            re = jnp.concatenate([z[0] for z in order], axis=0).astype(jnp.bfloat16)
            im = jnp.concatenate([z[1] for z in order], axis=0).astype(jnp.bfloat16)
            left = jnp.concatenate([re[:, K:], im[:, K:]], axis=1)
            right = jnp.concatenate(
                [
                    jnp.concatenate([re[:, :K], -im[:, :K]], axis=1),
                    empty,
                    jnp.concatenate([im[:, :K], re[:, :K]], axis=1),
                    empty,
                ],
                axis=0,
            )
            cells = dot_last(left, right)
            offset = offset_smem[1 if mirrored else 0, peer * CAP + c]
            row = pl.multiple_of((offset >> 6) * S, S)
            shift = offset & (N2 - 1)
            upper, lower = cells[:HALF], cells[HALF:]
            upper1 = pltpu.roll(upper, shift, 1)
            upper2 = pltpu.roll(upper, shift + N2, 1)
            lower1 = pltpu.roll(lower, shift, 1)
            lower2 = pltpu.roll(lower, shift + N2, 1)
            even = jnp.where(first_half, upper1, lower2)
            odd = jnp.where(first_half, upper2, lower1)
            stays = lane_in >= shift
            sign = -1.0 if mirrored else 1.0
            grid_ref[pl.ds(row, HALF), :] += jnp.where(stays, even, 0.0)
            grid_ref[pl.ds(row + HALF, HALF), :] += sign * jnp.where(stays, odd, 0.0)
            grid_ref[pl.ds(row + S, HALF), :] += jnp.where(stays, 0.0, odd)
            grid_ref[pl.ds(row + S + HALF, HALF), :] += sign * jnp.where(stays, 0.0, even)

    def both(b, _):
        one_list(own + b, False)
        one_list(mirror + b, True)
        return 0

    lax.fori_loop(0, band_count, both, 0)

    def out_copy(part, group):
        rows = pl.ds(group * 8 * N2, 8 * N2)
        return pltpu.make_async_copy(
            rows_ref.at[part, rows, :], out_ref.at[part, rows, :], out_sem.at[part, group]
        )

    twist_re, twist_im = twist_ref[0], twist_ref[1]
    for pair in range(HALF // 2):
        lines = (2 * pair, 2 * pair + 1)
        field = jnp.concatenate(
            [
                jnp.concatenate(
                    [
                        grid_ref[pl.ds(part * HALF + y, N1, stride=S), :].astype(jnp.bfloat16)
                        for y in lines
                    ],
                    axis=1,
                )
                for part in range(2)
            ],
            axis=0,
        )
        section = jnp.dot(outer_ref[...], field, preferred_element_type=jnp.float32)
        twisted = []
        for p in range(2):
            re = section[:N1, p * 128 : (p + 1) * 128]
            im = section[N1:, p * 128 : (p + 1) * 128]
            twisted.append(
                jnp.concatenate(
                    [re * twist_re - im * twist_im, re * twist_im + im * twist_re], axis=1
                ).astype(jnp.bfloat16)
            )
        spectrum = dot_last(inner_ref[...], jnp.concatenate(twisted, axis=0))
        for part in range(2):
            for half in range(2):
                for p, y in enumerate(lines):
                    start = (part * 2 + half) * N2
                    line = half * HALF + y
                    rows_ref[part, pl.ds((line // 8) * 8 * N2 + line % 8, N2, stride=8), :] = spectrum[
                        start : start + N2, p * 128 : (p + 1) * 128
                    ]
        if lines[1] % 8 == 7:
            for part in range(2):
                for half in range(2):
                    out_copy(part, half * (HALF // 8) + lines[1] // 8).start()
    for part in range(2):
        for group in range(S // 8):
            out_copy(part, group).wait()


def shards(visibilities, coordinates, block_index, counts, col_offset):
    band_count = lax.axis_size("band")
    group_count = lax.axis_size("wgrp")
    peers = 2 * band_count
    vmem = pl.BlockSpec(memory_space=pltpu.VMEM)
    message = pl.pallas_call(
        functools.partial(pack_kernel, band_count, group_count),
        out_shape=jax.ShapeDtypeStruct((peers, CAP, ROW), jnp.bfloat16),
        in_specs=[vmem] * 5,
        out_specs=vmem,
        compiler_params=pltpu.CompilerParams(vmem_limit_bytes=40 * 2**20),
        name="pack_blocks",
    )(visibilities[0], coordinates[0], block_index, counts, col_offset)
    groups = [
        [b * group_count + q for b in range(band_count)]
        + [b * group_count + group_count - 1 - q for b in range(band_count)]
        for q in range(group_count // 2)
    ]
    received = lax.all_to_all(
        message, ("band", "wgrp"), 0, 0, axis_index_groups=groups, tiled=True
    )
    outer, inner, twist = transform_tables()
    slots = peers * CAP
    rows = pl.pallas_call(
        functools.partial(grid_kernel, band_count, group_count),
        out_shape=jax.ShapeDtypeStruct((2, S * N2, N1), jnp.float32),
        in_specs=[vmem] * 4,
        out_specs=pl.BlockSpec(memory_space=pl.ANY),
        scratch_shapes=[
            pltpu.VMEM((8, slots), jnp.int32),
            pltpu.SMEM((8, slots), jnp.int32),
            pltpu.VMEM((2 * K // 128 * 8 * CAP, 128), jnp.float32),
            pltpu.VMEM((2 * K // 128 * 8 * CAP, 128), jnp.float32),
            pltpu.VMEM((CAP, 2 * K), jnp.float32),
            pltpu.VMEM((CAP, 2 * K), jnp.float32),
            pltpu.VMEM(((N1 + 2) * S, 128), jnp.float32),
            pltpu.VMEM((2, S * N2, N1), jnp.float32),
            pltpu.SemaphoreType.DMA(()),
            pltpu.SemaphoreType.DMA((2, S // 8)),
        ],
        compiler_params=pltpu.CompilerParams(vmem_limit_bytes=40 * 2**20),
        name="grid_and_transform",
    )(received, outer, inner, twist)
    lines = rows.reshape(1, 2, S // 8, N2, 8, N1).transpose(0, 1, 2, 4, 3, 5)
    return lines.reshape(1, 2, S, G)


def solution(mesh):
    placed = (
        P("wgrp", "band", None),
        P("wgrp", "band", None),
        P("wgrp", "band"),
        P("wgrp", "band"),
        P("wgrp", "band"),
    )
    return jax.shard_map(
        shards, mesh=mesh, in_specs=placed, out_specs=P("wgrp", None, "band", None), check_vma=False
    )
```

```python
import functools
import math

import jax
import jax.numpy as jnp
import numpy as np
from jax import lax
from jax.experimental import pallas as pl
from jax.experimental.pallas import tpu as pltpu
from jax.sharding import PartitionSpec as P

S = 32
G = 8192
K = 256
GROUP = 4
CAP = 8
HALF = S // 2
N1 = 128
N2 = 64
DATA = 4 * K
ROW = DATA + 128
LO = 64
PI = math.pi

SIN_TERMS = (1.0, -1 / 6, 1 / 120, -1 / 5040, 1 / 362880, -1 / 39916800)
COS_TERMS = (1.0, -1 / 2, 1 / 24, -1 / 720, 1 / 40320, -1 / 3628800, 1 / 479001600)


def transform_tables():
    n1, n2 = np.arange(N1), np.arange(N2)
    outer = np.exp(-2j * np.pi * (np.outer(n1, n1) % N1) / N1)
    inner = np.exp(-2j * np.pi * (np.outer(n2, n2) % N2) / N2)
    twist = np.exp(-2j * np.pi * np.outer(n1, n2) / G) / math.sqrt(G * K)
    pair = np.kron(np.eye(2), inner)

    def real_form(m):
        return np.block([[m.real, -m.imag], [m.imag, m.real]])

    twist = np.concatenate([twist, twist], axis=1)
    return (
        jnp.asarray(real_form(outer), jnp.bfloat16),
        jnp.asarray(real_form(pair), jnp.bfloat16),
        jnp.asarray(np.stack([twist.real, twist.imag]), jnp.float32),
    )


def dot_last(left, right):
    return lax.dot_general(
        left, right, (((1,), (1,)), ((), ())), preferred_element_type=jnp.float32
    )


def dot_first(left, right):
    return lax.dot_general(
        left, right, (((0,), (0,)), ((), ())), preferred_element_type=jnp.float32
    )


def own_base(band_count, group_count):
    low = lax.axis_index("wgrp") < group_count // 2
    return jnp.where(low, 0, band_count), jnp.where(low, band_count, 0)


def pack_kernel(band_count, group_count, *refs):
    sources, out_ref, targets, sems = refs[:5], refs[5], refs[6:11], refs[11]
    copies = [
        pltpu.make_async_copy(source, target, sems.at[i])
        for i, (source, target) in enumerate(zip(sources, targets))
    ]
    for copy in copies:
        copy.start()
    vis_ref, coord_ref, block_ref, count_ref, offset_ref = targets
    own, mirror = own_base(band_count, group_count)
    for copy in copies:
        copy.wait()
    slots = block_ref.shape[1]
    blocks = vis_ref.shape[0]
    lane = lax.broadcasted_iota(jnp.int32, (1, slots), 1)
    list_of = lane // CAP
    within = lane % CAP
    band_row = lax.broadcasted_iota(jnp.int32, (band_count, slots), 0)
    in_list = (band_row == list_of).astype(jnp.float32)
    counts = jnp.broadcast_to(count_ref[...].astype(jnp.float32), (8, band_count))
    live_count = jnp.dot(counts, in_list, preferred_element_type=jnp.float32)[0:1]
    live = (within.astype(jnp.float32) < live_count).astype(jnp.float32)
    chosen = (
        lax.broadcasted_iota(jnp.int32, (blocks, slots), 0) == block_ref[...]
    ).astype(jnp.float32)
    vis = dot_first((chosen * live).astype(jnp.bfloat16), vis_ref[...])
    coord = dot_first(chosen.astype(jnp.bfloat16), coord_ref[...])
    offsets = offset_ref[...]
    here = lax.broadcasted_iota(jnp.int32, (CAP, slots), 0) == within
    high = jnp.where(here, (offsets >> 7).astype(jnp.float32), 0.0).astype(jnp.bfloat16)
    low = jnp.where(here, (offsets & 127).astype(jnp.float32), 0.0).astype(jnp.bfloat16)
    slot_row = lax.broadcasted_iota(jnp.int32, (slots, 128), 0) // CAP
    column = lax.broadcasted_iota(jnp.int32, (slots, 128), 1)
    to_high = (slot_row == column).astype(jnp.bfloat16)
    to_low = (slot_row + LO == column).astype(jnp.bfloat16)
    meta = jnp.dot(high, to_high, preferred_element_type=jnp.float32) + jnp.dot(
        low, to_low, preferred_element_type=jnp.float32
    )
    for d in range(band_count):
        rows = slice(d * CAP, (d + 1) * CAP)
        message = jnp.concatenate([vis[rows], coord[rows], meta], axis=1).astype(jnp.bfloat16)
        out_ref[own + d] = message
        out_ref[mirror + band_count - 1 - d] = message


def square(z):
    re, im = z
    return re * re - im * im, 2.0 * (re * im)


def times(z, w):
    return z[0] * w[0] - z[1] * w[1], z[0] * w[1] + z[1] * w[0]


def unit_phasor(cycles):
    half = (cycles - jnp.round(cycles)) * PI
    x = half * half
    sine = jnp.full_like(x, SIN_TERMS[-1])
    for term in SIN_TERMS[-2::-1]:
        sine = sine * x + term
    cosine = jnp.full_like(x, COS_TERMS[-1])
    for term in COS_TERMS[-2::-1]:
        cosine = cosine * x + term
    sine = sine * half
    return 1.0 - 2.0 * (sine * sine), 2.0 * (sine * cosine)


def grid_kernel(
    band_count,
    group_count,
    recv_ref,
    outer_hbm,
    inner_hbm,
    twist_hbm,
    out_ref,
    outer_ref,
    inner_ref,
    twist_ref,
    offset_vmem,
    offset_smem,
    own_phasors,
    mirror_phasors,
    own_cells,
    mirror_cells,
    grid_ref,
    rows_ref,
    offset_sem,
    table_sem,
    out_sem,
):
    tables = [
        pltpu.make_async_copy(source, target, table_sem.at[i])
        for i, (source, target) in enumerate(
            ((outer_hbm, outer_ref), (inner_hbm, inner_ref), (twist_hbm, twist_ref))
        )
    ]
    for table in tables:
        table.start()
    own, mirror = own_base(band_count, group_count)
    band = lax.axis_index("band")
    peers = 2 * band_count

    meta = recv_ref[:, :, DATA:].astype(jnp.float32).reshape(peers * CAP, 128)
    pick_row = lax.broadcasted_iota(jnp.int32, (8, 128), 0)
    pick_col = lax.broadcasted_iota(jnp.int32, (8, 128), 1)
    flipped = band_count - 1 - band
    wanted = jnp.where(
        pick_row == 0,
        band,
        jnp.where(pick_row == 1, band + LO, jnp.where(pick_row == 2, flipped, flipped + LO)),
    )
    pick = (pick_col == wanted).astype(jnp.bfloat16)
    picked = dot_last(pick, meta.astype(jnp.bfloat16))
    offset_vmem[0:1] = (picked[0:1] * 128.0 + picked[1:2]).astype(jnp.int32)
    offset_vmem[1:2] = (G - S) - (picked[2:3] * 128.0 + picked[3:4]).astype(jnp.int32)
    to_smem = pltpu.make_async_copy(offset_vmem, offset_smem, offset_sem)
    to_smem.start()

    def clear(step, _):
        for block in range(S // 8):
            grid_ref[block, pl.ds(pl.multiple_of(step * 16, 16), 16), :] = jnp.zeros(
                (16, 128), jnp.float32
            )
        return 0

    lax.fori_loop(0, (N1 + 2) // 2, clear, 0)

    lane = lax.broadcasted_iota(jnp.int32, (8, 128), 1)
    first_half = lane < N2
    lane_in = lane & (N2 - 1)
    chunks = 2 * K // 128
    phasors, cells_ref = (own_phasors, mirror_phasors), (own_cells, mirror_cells)

    def add_cells(cells, start, offset, negate):
        row = pl.multiple_of((offset >> 6) * 8, 8)
        shift = offset & (N2 - 1)
        near, far = (shift + 128 - start) & 127, (shift + N2 - start) & 127
        stays = (lane_in >= shift) & (lane_in < shift + S)
        wraps = lane_in < shift - (N2 - S)
        for block in range(HALF // 8):
            upper = cells[block * 8 : block * 8 + 8]
            lower = cells[HALF + block * 8 : HALF + block * 8 + 8]
            even = jnp.where(first_half, pltpu.roll(upper, near, 1), pltpu.roll(lower, far, 1))
            odd = jnp.where(first_half, pltpu.roll(upper, far, 1), pltpu.roll(lower, near, 1))
            for part, here, over in ((0, even, odd), (1, odd, even)):
                for at, piece in ((row, jnp.where(stays, here, 0.0)), (row + 8, jnp.where(wraps, over, 0.0))):
                    rows = pl.ds(at, 8)
                    old = grid_ref[part * (HALF // 8) + block, rows, :]
                    grid_ref[part * (HALF // 8) + block, rows, :] = (
                        old - piece if part == 1 and negate else old + piece
                    )

    def make_tables(peer, mirrored):
        tab_re, tab_im, eight_re, eight_im = phasors[mirrored]
        block = recv_ref[peer].astype(jnp.float32)
        vis = (block[:, 0:K], block[:, K : 2 * K])
        e1 = unit_phasor(block[:, 2 * K : 4 * K] * (1.0 / S))
        e2 = square(e1)
        e3 = times(e2, e1)
        e4 = square(e2)
        one = (jnp.ones_like(e1[0]), jnp.zeros_like(e1[0]))
        steps = (one, e1, e2, e3, e4, times(e4, e1), square(e3), times(e4, e3))
        e8 = square(e4)
        for b, e in enumerate(steps):
            at = CAP - 1 - b if mirrored else b
            weighted = vis if b == 0 else times(vis, (e[0][:, :K], e[1][:, :K]))
            for tab, z, e_part in ((tab_re, weighted[0], e[0]), (tab_im, weighted[1], e[1])):
                whole = jnp.concatenate([z, e_part[:, K:]], axis=1)
                for q in range(chunks):
                    tab[pl.ds(q * 8 * CAP + at, CAP, stride=8), :] = whole[:, q * 128 : (q + 1) * 128]
        eight_re[...] = e8[0]
        eight_im[...] = e8[1]

    def multiply(mirrored):
        tab_re, tab_im, eight_re, eight_im = phasors[mirrored]
        for first in range(0, CAP, GROUP):
            left, real, imag = [], [], []
            for c in range(first, first + GROUP):
                base = tuple(
                    jnp.concatenate(
                        [tab[(q * CAP + c) * 8 : (q * CAP + c + 1) * 8, :] for q in range(chunks)],
                        axis=1,
                    )
                    for tab in (tab_re, tab_im)
                )
                c8 = jnp.broadcast_to(eight_re[c : c + 1, :], (8, 2 * K))
                s8 = jnp.broadcast_to(eight_im[c : c + 1, :], (8, 2 * K))
                cc, ss, cs, sc = base[0] * c8, base[1] * s8, base[0] * s8, base[1] * c8
                up = (cc - ss, sc + cs)
                down = (cc + ss, sc - cs)
                down2 = (down[0] * c8 + down[1] * s8, down[1] * c8 - down[0] * s8)
                order = (up, base, down, down2) if mirrored else (down2, down, base, up)
                re = jnp.concatenate([z[0] for z in order], axis=0).astype(jnp.bfloat16)
                im = jnp.concatenate([z[1] for z in order], axis=0).astype(jnp.bfloat16)
                left.append(jnp.concatenate([re[:, K:], im[:, K:]], axis=1))
                real.append(jnp.concatenate([re[:, :K], -im[:, :K]], axis=1))
                imag.append(jnp.concatenate([im[:, :K], re[:, :K]], axis=1))
            right = []
            for c in range(0, GROUP, 2):
                right += real[c : c + 2] + imag[c : c + 2]
            cells = dot_last(jnp.concatenate(left, axis=0), jnp.concatenate(right, axis=0))
            for c in range(GROUP):
                tile = c // 2 * 128
                cells_ref[mirrored][(first + c) * S : (first + c + 1) * S, :] = cells[
                    c * S : (c + 1) * S, tile : tile + 128
                ]

    def add_list(peer, mirrored):
        for c in range(CAP):
            add_cells(
                cells_ref[mirrored][c * S : (c + 1) * S, :],
                c % 2 * S,
                offset_smem[mirrored, peer * CAP + c],
                mirrored == 1,
            )

    make_tables(own, 0)
    to_smem.wait()
    cells_ref[1][...] = jnp.zeros_like(cells_ref[1])

    def turn(b, _):
        multiply(0)
        add_list(mirror + jnp.maximum(b - 1, 0), 1)
        make_tables(mirror + b, 1)
        multiply(1)
        add_list(own + b, 0)
        make_tables(own + jnp.minimum(b + 1, band_count - 1), 0)
        return 0

    lax.fori_loop(0, band_count, turn, 0)
    add_list(mirror + band_count - 1, 1)

    for table in tables:
        table.wait()

    def out_copy(part, group):
        rows = pl.ds(group * 8 * N2, 8 * N2)
        return pltpu.make_async_copy(
            rows_ref.at[part, rows, :], out_ref.at[part, rows, :], out_sem.at[part, group]
        )

    twist_re, twist_im = twist_ref[0], twist_ref[1]
    for pair in range(HALF // 2):
        lines = (2 * pair, 2 * pair + 1)
        field = jnp.concatenate(
            [
                jnp.concatenate(
                    [
                        grid_ref[
                            part * (HALF // 8) + y // 8, pl.ds(y % 8, N1, stride=8), :
                        ].astype(jnp.bfloat16)
                        for y in lines
                    ],
                    axis=1,
                )
                for part in range(2)
            ],
            axis=0,
        )
        section = jnp.dot(outer_ref[...], field, preferred_element_type=jnp.float32)
        twisted = []
        for p in range(2):
            re = section[:N1, p * 128 : (p + 1) * 128]
            im = section[N1:, p * 128 : (p + 1) * 128]
            twisted.append(
                jnp.concatenate(
                    [re * twist_re - im * twist_im, re * twist_im + im * twist_re], axis=1
                ).astype(jnp.bfloat16)
            )
        spectrum = dot_last(inner_ref[...], jnp.concatenate(twisted, axis=0))
        for part in range(2):
            for half in range(2):
                for p, y in enumerate(lines):
                    start = (part * 2 + half) * N2
                    line = half * HALF + y
                    rows_ref[part, pl.ds((line // 8) * 8 * N2 + line % 8, N2, stride=8), :] = spectrum[
                        start : start + N2, p * 128 : (p + 1) * 128
                    ]
        if lines[1] % 8 == 7:
            for part in range(2):
                for half in range(2):
                    out_copy(part, half * (HALF // 8) + lines[1] // 8).start()
    for part in range(2):
        for group in range(S // 8):
            out_copy(part, group).wait()


def shards(visibilities, coordinates, block_index, counts, col_offset):
    band_count = lax.axis_size("band")
    group_count = lax.axis_size("wgrp")
    peers = 2 * band_count
    vmem = pl.BlockSpec(memory_space=pltpu.VMEM)
    hbm = pl.BlockSpec(memory_space=pltpu.HBM)
    inputs = (visibilities[0], coordinates[0], block_index, counts, col_offset)
    message = pl.pallas_call(
        functools.partial(pack_kernel, band_count, group_count),
        out_shape=jax.ShapeDtypeStruct((peers, CAP, ROW), jnp.bfloat16),
        in_specs=[hbm] * 5,
        out_specs=vmem,
        scratch_shapes=[pltpu.VMEM(a.shape, a.dtype) for a in inputs]
        + [pltpu.SemaphoreType.DMA((len(inputs),))],
        name="pack_blocks",
    )(*inputs)
    groups = [
        [b * group_count + q for b in range(band_count)]
        + [b * group_count + group_count - 1 - q for b in range(band_count)]
        for q in range(group_count // 2)
    ]
    received = lax.all_to_all(
        message, ("band", "wgrp"), 0, 0, axis_index_groups=groups, tiled=True
    )
    outer, inner, twist = transform_tables()
    slots = peers * CAP
    base = pltpu.VMEM((2 * K // 128 * 8 * CAP, 128), jnp.float32)
    step = pltpu.VMEM((CAP, 2 * K), jnp.float32)
    phasors = (base, base, step, step)
    rows = pl.pallas_call(
        functools.partial(grid_kernel, band_count, group_count),
        out_shape=jax.ShapeDtypeStruct((2, S * N2, N1), jnp.float32),
        in_specs=[vmem] + [hbm] * 3,
        out_specs=pl.BlockSpec(memory_space=pl.ANY),
        scratch_shapes=[
            pltpu.VMEM(outer.shape, outer.dtype),
            pltpu.VMEM(inner.shape, inner.dtype),
            pltpu.VMEM(twist.shape, twist.dtype),
            pltpu.VMEM((8, slots), jnp.int32),
            pltpu.SMEM((8, slots), jnp.int32),
            phasors,
            phasors,
            pltpu.VMEM((CAP * S, 128), jnp.float32),
            pltpu.VMEM((CAP * S, 128), jnp.float32),
            pltpu.VMEM((S // 8, (N1 + 2) * 8, 128), jnp.float32),
            pltpu.VMEM((2, S * N2, N1), jnp.float32),
            pltpu.SemaphoreType.DMA(()),
            pltpu.SemaphoreType.DMA((3,)),
            pltpu.SemaphoreType.DMA((2, S // 8)),
        ],
        name="grid_and_transform",
    )(received, outer, inner, twist)
    lines = rows.reshape(1, 2, S // 8, N2, 8, N1).transpose(0, 1, 2, 4, 3, 5)
    return lines.reshape(1, 2, S, G)


def solution(mesh):
    placed = (
        P("wgrp", "band", None),
        P("wgrp", "band", None),
        P("wgrp", "band"),
        P("wgrp", "band"),
        P("wgrp", "band"),
    )
    return jax.shard_map(
        shards, mesh=mesh, in_specs=placed, out_specs=P("wgrp", None, "band", None), check_vma=False
    )
```

```python
import functools
import math

import jax
import jax.numpy as jnp
from jax import lax
from jax.experimental import pallas as pl
from jax.experimental.pallas import tpu as pltpu
from jax.sharding import PartitionSpec as P

S = 32
G = 8192
K = 256
GROUP = 4
CAP = 8
HALF = S // 2
N1 = 128
N2 = 64
DATA = 4 * K
ROW = DATA + 128
LIVE = 32
LO = 64
PI = math.pi

SIN_TERMS = (1.0, -1 / 6, 1 / 120, -1 / 5040, 1 / 362880, -1 / 39916800)
COS_TERMS = (1.0, -1 / 2, 1 / 24, -1 / 720, 1 / 40320, -1 / 3628800, 1 / 479001600)


def dot_last(left, right):
    return lax.dot_general(
        left, right, (((1,), (1,)), ((), ())), preferred_element_type=jnp.float32
    )


def dot_first(left, right):
    return lax.dot_general(
        left, right, (((0,), (0,)), ((), ())), preferred_element_type=jnp.float32
    )


def own_base(band_count, group_count):
    low = lax.axis_index("wgrp") < group_count // 2
    return jnp.where(low, 0, band_count), jnp.where(low, band_count, 0)


def pack_kernel(band_count, group_count, *refs):
    sources, out_ref, targets, sems = refs[:5], refs[5], refs[6:11], refs[11]
    copies = [
        pltpu.make_async_copy(source, target, sems.at[i])
        for i, (source, target) in enumerate(zip(sources, targets))
    ]
    for copy in copies:
        copy.start()
    vis_ref, coord_ref, block_ref, count_ref, offset_ref = targets
    own, mirror = own_base(band_count, group_count)
    for copy in copies:
        copy.wait()
    slots = block_ref.shape[1]
    blocks = vis_ref.shape[0]
    lane = lax.broadcasted_iota(jnp.int32, (1, slots), 1)
    list_of = lane // CAP
    within = lane % CAP
    band_row = lax.broadcasted_iota(jnp.int32, (band_count, slots), 0)
    in_list = (band_row == list_of).astype(jnp.float32)
    counts = jnp.broadcast_to(count_ref[...].astype(jnp.float32), (8, band_count))
    live_count = jnp.dot(counts, in_list, preferred_element_type=jnp.float32)[0:1]
    live = (within.astype(jnp.float32) < live_count).astype(jnp.float32)
    chosen = (
        lax.broadcasted_iota(jnp.int32, (blocks, slots), 0) == block_ref[...]
    ).astype(jnp.float32)
    vis = dot_first((chosen * live).astype(jnp.bfloat16), vis_ref[...])
    coord = dot_first(chosen.astype(jnp.bfloat16), coord_ref[...])
    offsets = offset_ref[...]
    here = lax.broadcasted_iota(jnp.int32, (CAP, slots), 0) == within
    high = jnp.where(here, (offsets >> 7).astype(jnp.float32), 0.0).astype(jnp.bfloat16)
    low = jnp.where(here, (offsets & 127).astype(jnp.float32), 0.0).astype(jnp.bfloat16)
    slot_row = lax.broadcasted_iota(jnp.int32, (slots, 128), 0) // CAP
    column = lax.broadcasted_iota(jnp.int32, (slots, 128), 1)
    to_high = (slot_row == column).astype(jnp.bfloat16)
    to_low = (slot_row + LO == column).astype(jnp.bfloat16)
    to_live = (slot_row + LIVE == column).astype(jnp.bfloat16)
    alive = jnp.where(here, live, 0.0).astype(jnp.bfloat16)
    meta = (
        jnp.dot(high, to_high, preferred_element_type=jnp.float32)
        + jnp.dot(low, to_low, preferred_element_type=jnp.float32)
        + jnp.dot(alive, to_live, preferred_element_type=jnp.float32)
    )
    for d in range(band_count):
        rows = slice(d * CAP, (d + 1) * CAP)
        message = jnp.concatenate([vis[rows], coord[rows], meta], axis=1).astype(jnp.bfloat16)
        out_ref[own + d] = message
        out_ref[mirror + band_count - 1 - d] = message


def square(z):
    re, im = z
    return re * re - im * im, 2.0 * (re * im)


def times(z, w):
    return z[0] * w[0] - z[1] * w[1], z[0] * w[1] + z[1] * w[0]


def unit_phasor(cycles):
    half = (cycles - jnp.round(cycles)) * PI
    x = half * half
    sine = jnp.full_like(x, SIN_TERMS[-1])
    for term in SIN_TERMS[-2::-1]:
        sine = sine * x + term
    cosine = jnp.full_like(x, COS_TERMS[-1])
    for term in COS_TERMS[-2::-1]:
        cosine = cosine * x + term
    sine = sine * half
    return 1.0 - 2.0 * (sine * sine), 2.0 * (sine * cosine)


def turns(rows, columns, length):
    return unit_phasor(((rows * columns) & (length - 1)).astype(jnp.float32) * (1.0 / length))


def fill_tables(outer_ref, inner_ref, twist_ref):
    row = lax.broadcasted_iota(jnp.int32, (N1, 128), 0)
    column = lax.broadcasted_iota(jnp.int32, (N1, 128), 1)
    row_in, column_in = row & (N2 - 1), column & (N2 - 1)
    outer = turns(row, column, N1)
    same = (row ^ column) < N2
    inner = [jnp.where(same, z, 0.0) for z in turns(row_in, column_in, N2)]
    for ref, (cosine, sine) in ((outer_ref, outer), (inner_ref, inner)):
        cosine, sine = cosine.astype(jnp.bfloat16), sine.astype(jnp.bfloat16)
        ref[:N1, :128] = cosine
        ref[:N1, 128:] = sine
        ref[N1:, :128] = -sine
        ref[N1:, 128:] = cosine
    scale = 1.0 / math.sqrt(G * K)
    twist = turns(row, column_in, G)
    twist_ref[0] = twist[0] * scale
    twist_ref[1] = twist[1] * -scale


def grid_kernel(
    band_count,
    group_count,
    recv_ref,
    out_ref,
    outer_ref,
    inner_ref,
    twist_ref,
    offset_vmem,
    offset_smem,
    data_ref,
    tab_re,
    tab_im,
    eight_re,
    eight_im,
    cells_ref,
    grid_ref,
    rows_ref,
    offset_sem,
    out_sem,
):
    own, _ = own_base(band_count, group_count)
    band = lax.axis_index("band")

    slots = 2 * band_count * CAP
    flat = recv_ref[...].astype(jnp.float32).reshape(slots, ROW).astype(jnp.bfloat16)
    pick_row = lax.broadcasted_iota(jnp.int32, (8, 128), 0)
    pick_col = lax.broadcasted_iota(jnp.int32, (8, 128), 1)
    flipped = band_count - 1 - band
    wanted = jnp.full((8, 128), -1, jnp.int32)
    for i, at in enumerate((0, LO, LIVE)):
        wanted = jnp.where(pick_row == i, band + at, wanted)
        wanted = jnp.where(pick_row == i + 3, flipped + at, wanted)
    picked = dot_last((pick_col == wanted).astype(jnp.bfloat16), flat[:, DATA:])
    slot = lax.broadcasted_iota(jnp.int32, (1, slots), 1)
    mine = (slot >= own * CAP) & (slot < (own + band_count) * CAP)
    high, low, live = (jnp.where(mine, picked[i : i + 1], picked[i + 3 : i + 4]) for i in range(3))
    offsets = (high * 128.0 + low).astype(jnp.int32)
    offsets = jnp.where(mine, offsets, (G - S) - offsets)

    live_own = jnp.where(mine, live, 0.0)
    live_mirror = live - live_own
    nothing = jnp.zeros((6, slots), jnp.float32)
    kinds = jnp.concatenate([live_own, live_mirror, nothing], axis=0).astype(jnp.bfloat16)
    earlier = (
        lax.broadcasted_iota(jnp.int32, (slots, slots), 0)
        < lax.broadcasted_iota(jnp.int32, (slots, slots), 1)
    ).astype(jnp.bfloat16)
    before = jnp.dot(kinds, earlier, preferred_element_type=jnp.float32)
    own_groups, mirror_groups = (
        jnp.floor((jnp.sum(z, axis=1, keepdims=True) + (CAP - 1)) * (1.0 / CAP))
        for z in (live_own, live_mirror)
    )
    position = jnp.where(mine, before[0:1], before[1:2] + CAP * own_groups)
    position = jnp.where(live > 0.5, position, -1.0).astype(jnp.int32)
    moves = (
        lax.broadcasted_iota(jnp.int32, (slots, slots), 0) == position
    ).astype(jnp.bfloat16)
    data_ref[...] = jnp.dot(moves, flat[:, :DATA], preferred_element_type=jnp.float32)
    parts = jnp.concatenate(
        [(offsets >> 7).astype(jnp.float32), (offsets & 127).astype(jnp.float32), nothing], axis=0
    )
    moved = dot_last(parts.astype(jnp.bfloat16), moves)
    offset_vmem[0:1] = (moved[0:1] * 128.0 + moved[1:2]).astype(jnp.int32)
    offset_vmem[1:2] = jnp.broadcast_to(own_groups, (1, slots)).astype(jnp.int32)
    offset_vmem[2:3] = jnp.broadcast_to(own_groups + mirror_groups, (1, slots)).astype(jnp.int32)
    to_smem = pltpu.make_async_copy(offset_vmem, offset_smem, offset_sem)
    to_smem.start()

    def clear(step, _):
        for block in range(S // 8):
            grid_ref[block, pl.ds(pl.multiple_of(step * 16, 16), 16), :] = jnp.zeros(
                (16, 128), jnp.float32
            )
        return 0

    lax.fori_loop(0, (N1 + 2) // 2, clear, 0)

    lane = lax.broadcasted_iota(jnp.int32, (8, 128), 1)
    first_half = lane < N2
    lane_in = lane & (N2 - 1)
    chunks = 2 * K // 128

    def add_cells(cells, start, offset):
        row = pl.multiple_of((offset >> 6) * 8, 8)
        shift = offset & (N2 - 1)
        near, far = (shift + 128 - start) & 127, (shift + N2 - start) & 127
        stays = (lane_in >= shift) & (lane_in < shift + S)
        wraps = lane_in < shift - (N2 - S)
        for block in range(HALF // 8):
            upper = cells[block * 8 : block * 8 + 8]
            lower = cells[HALF + block * 8 : HALF + block * 8 + 8]
            even = jnp.where(first_half, pltpu.roll(upper, near, 1), pltpu.roll(lower, far, 1))
            odd = jnp.where(first_half, pltpu.roll(upper, far, 1), pltpu.roll(lower, near, 1))
            for part, here, over in ((0, even, odd), (1, odd, even)):
                for at, piece in ((row, jnp.where(stays, here, 0.0)), (row + 8, jnp.where(wraps, over, 0.0))):
                    rows = pl.ds(at, 8)
                    grid_ref[part * (HALF // 8) + block, rows, :] += piece

    def make_tables(group, mirrored):
        block = data_ref[pl.ds(pl.multiple_of(group * CAP, CAP), CAP), :]
        flip = jnp.where(mirrored == 1, -1.0, 1.0)
        vis = (block[:, 0:K], block[:, K : 2 * K] * flip)
        e1 = unit_phasor(block[:, 2 * K : 4 * K] * (1.0 / S))
        e2 = square(e1)
        e3 = times(e2, e1)
        e4 = square(e2)
        e8 = square(e4)
        edge = tuple(jnp.where(mirrored == 1, z, one) for z, one in zip(e8, (1.0, 0.0)))
        for b, e in enumerate((edge, e1, e2, e3, e4, times(e4, e1), square(e3), times(e4, e3))):
            at = 7 * mirrored if b == 0 else b - mirrored
            weighted = times(vis, (e[0][:, :K], e[1][:, :K]))
            for tab, z, e_part in ((tab_re, weighted[0], e[0]), (tab_im, weighted[1], e[1])):
                whole = jnp.concatenate([z, e_part[:, K:]], axis=1)
                for q in range(chunks):
                    tab[pl.ds(q * 8 * CAP + at, CAP, stride=8), :] = whole[:, q * 128 : (q + 1) * 128]
        eight_re[...] = e8[0]
        eight_im[...] = e8[1]

    def multiply():
        for first in range(0, CAP, GROUP):
            left, real, imag = [], [], []
            for c in range(first, first + GROUP):
                base = tuple(
                    jnp.concatenate(
                        [tab[(q * CAP + c) * 8 : (q * CAP + c + 1) * 8, :] for q in range(chunks)],
                        axis=1,
                    )
                    for tab in (tab_re, tab_im)
                )
                c8 = jnp.broadcast_to(eight_re[c : c + 1, :], (8, 2 * K))
                s8 = jnp.broadcast_to(eight_im[c : c + 1, :], (8, 2 * K))
                cc, ss, cs, sc = base[0] * c8, base[1] * s8, base[0] * s8, base[1] * c8
                up = (cc - ss, sc + cs)
                down = (cc + ss, sc - cs)
                down2 = (down[0] * c8 + down[1] * s8, down[1] * c8 - down[0] * s8)
                order = (down2, down, base, up)
                re = jnp.concatenate([z[0] for z in order], axis=0).astype(jnp.bfloat16)
                im = jnp.concatenate([z[1] for z in order], axis=0).astype(jnp.bfloat16)
                left.append(jnp.concatenate([re[:, K:], im[:, K:]], axis=1))
                real.append(jnp.concatenate([re[:, :K], -im[:, :K]], axis=1))
                imag.append(jnp.concatenate([im[:, :K], re[:, :K]], axis=1))
            right = []
            for c in range(0, GROUP, 2):
                right += real[c : c + 2] + imag[c : c + 2]
            cells = dot_last(jnp.concatenate(left, axis=0), jnp.concatenate(right, axis=0))
            for c in range(GROUP):
                tile = c // 2 * 128
                cells_ref[(first + c) * S : (first + c + 1) * S, :] = cells[
                    c * S : (c + 1) * S, tile : tile + 128
                ]

    def add_group(group):
        for c in range(CAP):
            add_cells(cells_ref[c * S : (c + 1) * S, :], c % 2 * S, offset_smem[0, group * CAP + c])

    make_tables(0, jnp.int32(0))
    fill_tables(outer_ref, inner_ref, twist_ref)
    cells_ref[...] = jnp.zeros_like(cells_ref)
    to_smem.wait()
    first_mirrored, groups = offset_smem[1, 0], offset_smem[2, 0]

    def turn(group, _):
        add_group(jnp.maximum(group - 1, 0))
        multiply()
        later = jnp.minimum(group + 1, groups - 1)
        make_tables(later, (later >= first_mirrored).astype(jnp.int32))
        return 0

    lax.fori_loop(0, groups, turn, 0)
    add_group(groups - 1)

    def out_copy(part, group):
        rows = pl.ds(group * 8 * N2, 8 * N2)
        return pltpu.make_async_copy(
            rows_ref.at[part, rows, :], out_ref.at[part, rows, :], out_sem.at[part, group]
        )

    twist_re, twist_im = twist_ref[0], twist_ref[1]
    for pair in range(HALF // 2):
        lines = (2 * pair, 2 * pair + 1)
        field = jnp.concatenate(
            [
                jnp.concatenate(
                    [
                        grid_ref[
                            part * (HALF // 8) + y // 8, pl.ds(y % 8, N1, stride=8), :
                        ].astype(jnp.bfloat16)
                        for y in lines
                    ],
                    axis=1,
                )
                for part in range(2)
            ],
            axis=0,
        )
        section = jnp.dot(outer_ref[...], field, preferred_element_type=jnp.float32)
        twisted = []
        for p in range(2):
            re = section[:N1, p * 128 : (p + 1) * 128]
            im = section[N1:, p * 128 : (p + 1) * 128]
            twisted.append(
                jnp.concatenate(
                    [re * twist_re - im * twist_im, re * twist_im + im * twist_re], axis=1
                ).astype(jnp.bfloat16)
            )
        spectrum = dot_last(inner_ref[...], jnp.concatenate(twisted, axis=0))
        for part in range(2):
            for half in range(2):
                for p, y in enumerate(lines):
                    start = (part * 2 + half) * N2
                    line = half * HALF + y
                    rows_ref[part, pl.ds((line // 8) * 8 * N2 + line % 8, N2, stride=8), :] = spectrum[
                        start : start + N2, p * 128 : (p + 1) * 128
                    ]
        if lines[1] % 8 == 7:
            for part in range(2):
                for half in range(2):
                    out_copy(part, half * (HALF // 8) + lines[1] // 8).start()
    for part in range(2):
        for group in range(S // 8):
            out_copy(part, group).wait()


def shards(visibilities, coordinates, block_index, counts, col_offset):
    band_count = lax.axis_size("band")
    group_count = lax.axis_size("wgrp")
    peers = 2 * band_count
    vmem = pl.BlockSpec(memory_space=pltpu.VMEM)
    hbm = pl.BlockSpec(memory_space=pltpu.HBM)
    inputs = (visibilities[0], coordinates[0], block_index, counts, col_offset)
    message = pl.pallas_call(
        functools.partial(pack_kernel, band_count, group_count),
        out_shape=jax.ShapeDtypeStruct((peers, CAP, ROW), jnp.bfloat16),
        in_specs=[hbm] * 5,
        out_specs=vmem,
        scratch_shapes=[pltpu.VMEM(a.shape, a.dtype) for a in inputs]
        + [pltpu.SemaphoreType.DMA((len(inputs),))],
        name="pack_blocks",
    )(*inputs)
    groups = [
        [b * group_count + q for b in range(band_count)]
        + [b * group_count + group_count - 1 - q for b in range(band_count)]
        for q in range(group_count // 2)
    ]
    received = lax.all_to_all(
        message, ("band", "wgrp"), 0, 0, axis_index_groups=groups, tiled=True
    )
    slots = peers * CAP
    base = pltpu.VMEM((2 * K // 128 * 8 * CAP, 128), jnp.float32)
    step = pltpu.VMEM((CAP, 2 * K), jnp.float32)
    rows = pl.pallas_call(
        functools.partial(grid_kernel, band_count, group_count),
        out_shape=jax.ShapeDtypeStruct((2, S * N2, N1), jnp.float32),
        in_specs=[vmem],
        out_specs=pl.BlockSpec(memory_space=pl.ANY),
        scratch_shapes=[
            pltpu.VMEM((2 * N1, 256), jnp.bfloat16),
            pltpu.VMEM((2 * N1, 256), jnp.bfloat16),
            pltpu.VMEM((2, N1, 128), jnp.float32),
            pltpu.VMEM((8, slots), jnp.int32),
            pltpu.SMEM((8, slots), jnp.int32),
            pltpu.VMEM((slots, DATA), jnp.float32),
            base,
            base,
            step,
            step,
            pltpu.VMEM((CAP * S, 128), jnp.float32),
            pltpu.VMEM((S // 8, (N1 + 2) * 8, 128), jnp.float32),
            pltpu.VMEM((2, S * N2, N1), jnp.float32),
            pltpu.SemaphoreType.DMA(()),
            pltpu.SemaphoreType.DMA((2, S // 8)),
        ],
        compiler_params=pltpu.CompilerParams(vmem_limit_bytes=48 * 2**20),
        name="grid_and_transform",
    )(received)
    lines = rows.reshape(1, 2, S // 8, N2, 8, N1).transpose(0, 1, 2, 4, 3, 5)
    return lines.reshape(1, 2, S, G)


def solution(mesh):
    placed = (
        P("wgrp", "band", None),
        P("wgrp", "band", None),
        P("wgrp", "band"),
        P("wgrp", "band"),
        P("wgrp", "band"),
    )
    return jax.shard_map(
        shards, mesh=mesh, in_specs=placed, out_specs=P("wgrp", None, "band", None), check_vma=False
    )
```

```python
import functools
import math

import jax
import jax.numpy as jnp
from jax import lax
from jax.experimental import pallas as pl
from jax.experimental.pallas import tpu as pltpu
from jax.sharding import PartitionSpec as P

S = 32
G = 8192
K = 256
GROUP = 2
CAP = 8
HALF = S // 2
N1 = 128
N2 = 64
DATA = 4 * K
ROW = DATA + 128
LIVE = 32
LO = 64
PI = math.pi

SIN_TERMS = (0.99999999572, -0.1666665797, 0.0083330506173, -0.00019809046357, 2.6051662762e-06)
COS_TERMS = (0.99999995325, -0.49999905063, 0.041663578931, -0.0013853666933, 2.3153174156e-05)


def dot_last(left, right):
    return lax.dot_general(
        left, right, (((1,), (1,)), ((), ())), preferred_element_type=jnp.float32
    )


def dot_first(left, right):
    return lax.dot_general(
        left, right, (((0,), (0,)), ((), ())), preferred_element_type=jnp.float32
    )


def own_base(band_count, group_count):
    low = lax.axis_index("wgrp") < group_count // 2
    return jnp.where(low, 0, band_count), jnp.where(low, band_count, 0)


def pack_kernel(band_count, group_count, data_ref, whole_ref, out_ref):
    own, mirror = own_base(band_count, group_count)
    slots = band_count * CAP
    block_index = whole_ref[:, :slots]
    offsets = whole_ref[:, slots : 2 * slots]
    count = whole_ref[:, 2 * slots :]
    blocks = data_ref.shape[0]
    lane = lax.broadcasted_iota(jnp.int32, (1, slots), 1)
    list_of = lane // CAP
    within = lane % CAP
    band_row = lax.broadcasted_iota(jnp.int32, (band_count, slots), 0)
    in_list = (band_row == list_of).astype(jnp.float32)
    counts = jnp.broadcast_to(count.astype(jnp.float32), (8, band_count))
    live_count = jnp.dot(counts, in_list, preferred_element_type=jnp.float32)[0:1]
    live = (within.astype(jnp.float32) < live_count).astype(jnp.float32)
    chosen = (
        lax.broadcasted_iota(jnp.int32, (blocks, slots), 0) == block_index
    ).astype(jnp.float32)
    vis = dot_first((chosen * live).astype(jnp.bfloat16), data_ref[:, : 2 * K])
    coord = dot_first(chosen.astype(jnp.bfloat16), data_ref[:, 2 * K :])
    here = lax.broadcasted_iota(jnp.int32, (CAP, slots), 0) == within
    high = jnp.where(here, (offsets >> 7).astype(jnp.float32), 0.0).astype(jnp.bfloat16)
    low = jnp.where(here, (offsets & 127).astype(jnp.float32), 0.0).astype(jnp.bfloat16)
    slot_row = lax.broadcasted_iota(jnp.int32, (slots, 128), 0) // CAP
    column = lax.broadcasted_iota(jnp.int32, (slots, 128), 1)
    to_high = (slot_row == column).astype(jnp.bfloat16)
    to_low = (slot_row + LO == column).astype(jnp.bfloat16)
    to_live = (slot_row + LIVE == column).astype(jnp.bfloat16)
    alive = jnp.where(here, live, 0.0).astype(jnp.bfloat16)
    meta = (
        jnp.dot(high, to_high, preferred_element_type=jnp.float32)
        + jnp.dot(low, to_low, preferred_element_type=jnp.float32)
        + jnp.dot(alive, to_live, preferred_element_type=jnp.float32)
    )
    for d in range(band_count):
        rows = slice(d * CAP, (d + 1) * CAP)
        message = jnp.concatenate([vis[rows], coord[rows], meta], axis=1).astype(jnp.bfloat16)
        out_ref[own + d] = message
        out_ref[mirror + band_count - 1 - d] = message


def square(z):
    re, im = z
    return re * re - im * im, 2.0 * (re * im)


def times(z, w):
    return z[0] * w[0] - z[1] * w[1], z[0] * w[1] + z[1] * w[0]


def unit_phasor(cycles):
    half = (cycles - jnp.round(cycles)) * PI
    x = half * half
    sine = jnp.full_like(x, SIN_TERMS[-1])
    for term in SIN_TERMS[-2::-1]:
        sine = sine * x + term
    cosine = jnp.full_like(x, COS_TERMS[-1])
    for term in COS_TERMS[-2::-1]:
        cosine = cosine * x + term
    sine = sine * half
    return 1.0 - 2.0 * (sine * sine), 2.0 * (sine * cosine)


def turn_table(rows, column, length):
    row = lax.broadcasted_iota(jnp.int32, column.shape, 0)

    def turns(factor):
        return unit_phasor(((factor * column) & (length - 1)).astype(jnp.float32) * (1.0 / length))

    parts = [turns(row)]
    step = turns(jnp.full_like(row, 8))
    for _ in range(rows // 8 - 1):
        parts.append(times(parts[-1], step))
    return tuple(jnp.concatenate([z[i] for z in parts], axis=0) for i in range(2))


def fill_tables(outer_ref, inner_ref, twist_ref):
    column = lax.broadcasted_iota(jnp.int32, (8, 128), 1)
    column_in = column & (N2 - 1)
    outer = turn_table(N1, column, N1)
    left = lax.broadcasted_iota(jnp.int32, (N2, 128), 1) < N2
    inner = [
        jnp.concatenate([jnp.where(left, z, 0.0), jnp.where(left, 0.0, z)], axis=0)
        for z in turn_table(N2, column_in, N2)
    ]
    for ref, (cosine, sine) in ((outer_ref, outer), (inner_ref, inner)):
        cosine, sine = cosine.astype(jnp.bfloat16), sine.astype(jnp.bfloat16)
        ref[:N1, :128] = cosine
        ref[:N1, 128:] = sine
        ref[N1:, :128] = -sine
        ref[N1:, 128:] = cosine
    scale = 1.0 / math.sqrt(G * K)
    twist = turn_table(N1, column_in, G)
    twist_ref[0] = twist[0] * scale
    twist_ref[1] = twist[1] * -scale


def grid_kernel(
    band_count,
    group_count,
    recv_ref,
    out_ref,
    outer_ref,
    inner_ref,
    twist_ref,
    offset_vmem,
    offset_smem,
    data_ref,
    tab_re,
    tab_im,
    eight_re,
    eight_im,
    cells_ref,
    grid_ref,
    rows_ref,
    offset_sem,
    out_sem,
):
    own, _ = own_base(band_count, group_count)
    band = lax.axis_index("band")

    slots = 2 * band_count * CAP
    flat = recv_ref[...].astype(jnp.float32).reshape(slots, ROW).astype(jnp.bfloat16)
    pick_row = lax.broadcasted_iota(jnp.int32, (8, 128), 0)
    pick_col = lax.broadcasted_iota(jnp.int32, (8, 128), 1)
    flipped = band_count - 1 - band
    wanted = jnp.full((8, 128), -1, jnp.int32)
    for i, at in enumerate((0, LO, LIVE)):
        wanted = jnp.where(pick_row == i, band + at, wanted)
        wanted = jnp.where(pick_row == i + 3, flipped + at, wanted)
    picked = dot_last((pick_col == wanted).astype(jnp.bfloat16), flat[:, DATA:])
    slot = lax.broadcasted_iota(jnp.int32, (1, slots), 1)
    mine = (slot >= own * CAP) & (slot < (own + band_count) * CAP)
    high, low, live = (jnp.where(mine, picked[i : i + 1], picked[i + 3 : i + 4]) for i in range(3))
    offsets = (high * 128.0 + low).astype(jnp.int32)
    offsets = jnp.where(mine, offsets, (G - S) - offsets)

    live_own = jnp.where(mine, live, 0.0)
    live_mirror = live - live_own
    nothing = jnp.zeros((6, slots), jnp.float32)
    kinds = jnp.concatenate([live_own, live_mirror, nothing], axis=0).astype(jnp.bfloat16)
    earlier = (
        lax.broadcasted_iota(jnp.int32, (slots, slots), 0)
        < lax.broadcasted_iota(jnp.int32, (slots, slots), 1)
    ).astype(jnp.bfloat16)
    before = jnp.dot(kinds, earlier, preferred_element_type=jnp.float32)
    own_groups, mirror_groups = (
        jnp.floor((jnp.sum(z, axis=1, keepdims=True) + (CAP - 1)) * (1.0 / CAP))
        for z in (live_own, live_mirror)
    )
    position = jnp.where(mine, before[0:1], before[1:2] + CAP * own_groups)
    position = jnp.where(live > 0.5, position, -1.0).astype(jnp.int32)
    moves = (
        lax.broadcasted_iota(jnp.int32, (slots, slots), 0) == position
    ).astype(jnp.bfloat16)
    data_ref[...] = jnp.dot(moves, flat[:, :DATA], preferred_element_type=jnp.float32)
    parts = jnp.concatenate(
        [(offsets >> 7).astype(jnp.float32), (offsets & 127).astype(jnp.float32), nothing], axis=0
    )
    moved = dot_last(parts.astype(jnp.bfloat16), moves)
    offset_vmem[0:1] = (moved[0:1] * 128.0 + moved[1:2]).astype(jnp.int32)
    offset_vmem[1:2] = jnp.broadcast_to(own_groups, (1, slots)).astype(jnp.int32)
    offset_vmem[2:3] = jnp.broadcast_to(own_groups + mirror_groups, (1, slots)).astype(jnp.int32)
    to_smem = pltpu.make_async_copy(offset_vmem, offset_smem, offset_sem)
    to_smem.start()

    def clear(step, _):
        for block in range(S // 8):
            grid_ref[block, pl.ds(pl.multiple_of(step * 16, 16), 16), :] = jnp.zeros(
                (16, 128), jnp.float32
            )
        return 0

    lax.fori_loop(0, (N1 + 2) // 2, clear, 0)

    lane = lax.broadcasted_iota(jnp.int32, (8, 128), 1)
    first_half = lane < N2
    lane_in = lane & (N2 - 1)
    chunks = 2 * K // 128

    def add_cells(cells, start, offset):
        row = pl.multiple_of((offset >> 6) * 8, 8)
        shift = offset & (N2 - 1)
        near, far = (shift + 128 - start) & 127, (shift + N2 - start) & 127
        stays = (lane_in >= shift) & (lane_in < shift + S)
        wraps = lane_in < shift - (N2 - S)
        for block in range(HALF // 8):
            upper = cells[block * 8 : block * 8 + 8]
            lower = cells[HALF + block * 8 : HALF + block * 8 + 8]
            even = jnp.where(first_half, pltpu.roll(upper, near, 1), pltpu.roll(lower, far, 1))
            odd = jnp.where(first_half, pltpu.roll(upper, far, 1), pltpu.roll(lower, near, 1))
            for part, here, over in ((0, even, odd), (1, odd, even)):
                for at, piece in ((row, jnp.where(stays, here, 0.0)), (row + 8, jnp.where(wraps, over, 0.0))):
                    rows = pl.ds(at, 8)
                    grid_ref[part * (HALF // 8) + block, rows, :] += piece

    def make_tables(group, mirrored):
        block = data_ref[pl.ds(pl.multiple_of(group * CAP, CAP), CAP), :]
        flip = jnp.where(mirrored == 1, -1.0, 1.0)
        vis = (block[:, 0:K], block[:, K : 2 * K] * flip)
        e1 = unit_phasor(block[:, 2 * K : 4 * K] * (1.0 / S))
        e2 = square(e1)
        e4 = square(e2)
        cc, ss, cs, sc = e4[0] * e1[0], e4[1] * e1[1], e4[0] * e1[1], e4[1] * e1[0]
        e3, e5 = (cc + ss, sc - cs), (cc - ss, sc + cs)
        e8 = square(e4)
        edge = tuple(jnp.where(mirrored == 1, z, one) for z, one in zip(e8, (1.0, 0.0)))
        for b, e in enumerate((edge, e1, e2, e3, e4, e5, square(e3), times(e4, e3))):
            at = 7 * mirrored if b == 0 else b - mirrored
            weighted = times(vis, (e[0][:, :K], e[1][:, :K]))
            for tab, z, e_part in ((tab_re, weighted[0], e[0]), (tab_im, weighted[1], e[1])):
                whole = jnp.concatenate([z, e_part[:, K:]], axis=1)
                for q in range(chunks):
                    tab[pl.ds(q * 8 * CAP + at, CAP, stride=8), :] = whole[:, q * 128 : (q + 1) * 128]
        eight_re[...] = e8[0]
        eight_im[...] = e8[1]

    def multiply():
        products = []
        for first in range(0, CAP, GROUP):
            left, real, imag = [], [], []
            for c in range(first, first + GROUP):
                base = tuple(
                    jnp.concatenate(
                        [tab[(q * CAP + c) * 8 : (q * CAP + c + 1) * 8, :] for q in range(chunks)],
                        axis=1,
                    )
                    for tab in (tab_re, tab_im)
                )
                c8 = jnp.broadcast_to(eight_re[c : c + 1, :], (8, 2 * K))
                s8 = jnp.broadcast_to(eight_im[c : c + 1, :], (8, 2 * K))
                cc, ss, cs, sc = base[0] * c8, base[1] * s8, base[0] * s8, base[1] * c8
                up = (cc - ss, sc + cs)
                down = (cc + ss, sc - cs)
                down2 = (down[0] * c8 + down[1] * s8, down[1] * c8 - down[0] * s8)
                order = (down2, down, base, up)
                re = jnp.concatenate([z[0] for z in order], axis=0).astype(jnp.bfloat16)
                im = jnp.concatenate([z[1] for z in order], axis=0).astype(jnp.bfloat16)
                left.append(jnp.concatenate([re[:, K:], im[:, K:]], axis=1))
                real.append(jnp.concatenate([re[:, :K], -im[:, :K]], axis=1))
                imag.append(jnp.concatenate([im[:, :K], re[:, :K]], axis=1))
            right = []
            for c in range(0, GROUP, 2):
                right += real[c : c + 2] + imag[c : c + 2]
            cells = dot_last(jnp.concatenate(left, axis=0), jnp.concatenate(right, axis=0))
            products.append(cells)
        return products

    def keep(products):
        for c in range(CAP):
            row, tile = c % GROUP * S, c % GROUP // 2 * 128
            cells_ref[c * S : (c + 1) * S, :] = products[c // GROUP][row : row + S, tile : tile + 128]

    def add_group(group):
        for c in range(CAP):
            add_cells(cells_ref[c * S : (c + 1) * S, :], c % 2 * S, offset_smem[0, group * CAP + c])

    make_tables(0, jnp.int32(0))
    fill_tables(outer_ref, inner_ref, twist_ref)
    cells_ref[...] = jnp.zeros_like(cells_ref)
    to_smem.wait()
    first_mirrored, groups = offset_smem[1, 0], offset_smem[2, 0]

    def turn(group, _):
        products = multiply()
        add_group(jnp.maximum(group - 1, 0))
        keep(products)
        later = jnp.minimum(group + 1, groups - 1)
        make_tables(later, (later >= first_mirrored).astype(jnp.int32))
        return 0

    lax.fori_loop(0, groups, turn, 0)
    add_group(groups - 1)

    def out_copy(part, group):
        rows = pl.ds(group * 8 * N2, 8 * N2)
        return pltpu.make_async_copy(
            rows_ref.at[part, rows, :], out_ref.at[part, rows, :], out_sem.at[part, group]
        )

    twist_re, twist_im = twist_ref[0], twist_ref[1]
    for pair in range(HALF // 2):
        lines = (2 * pair, 2 * pair + 1)
        field = jnp.concatenate(
            [
                jnp.concatenate(
                    [
                        grid_ref[
                            part * (HALF // 8) + y // 8, pl.ds(y % 8, N1, stride=8), :
                        ].astype(jnp.bfloat16)
                        for y in lines
                    ],
                    axis=1,
                )
                for part in range(2)
            ],
            axis=0,
        )
        section = jnp.dot(outer_ref[...], field, preferred_element_type=jnp.float32)
        twisted = []
        for p in range(2):
            re = section[:N1, p * 128 : (p + 1) * 128]
            im = section[N1:, p * 128 : (p + 1) * 128]
            twisted.append(
                jnp.concatenate(
                    [re * twist_re - im * twist_im, re * twist_im + im * twist_re], axis=1
                ).astype(jnp.bfloat16)
            )
        spectrum = dot_last(inner_ref[...], jnp.concatenate(twisted, axis=0))
        for part in range(2):
            for half in range(2):
                for p, y in enumerate(lines):
                    start = (part * 2 + half) * N2
                    line = half * HALF + y
                    rows_ref[part, pl.ds((line // 8) * 8 * N2 + line % 8, N2, stride=8), :] = spectrum[
                        start : start + N2, p * 128 : (p + 1) * 128
                    ]
        if lines[1] % 8 == 7:
            for part in range(2):
                for half in range(2):
                    out_copy(part, half * (HALF // 8) + lines[1] // 8).start()
    for part in range(2):
        for group in range(S // 8):
            out_copy(part, group).wait()


def shards(visibilities, coordinates, block_index, counts, col_offset):
    band_count = lax.axis_size("band")
    group_count = lax.axis_size("wgrp")
    peers = 2 * band_count
    vmem = pl.BlockSpec(memory_space=pltpu.VMEM)
    hbm = pl.BlockSpec(memory_space=pltpu.HBM)
    blocks = jnp.concatenate([visibilities[0], coordinates[0]], axis=1)
    whole = jnp.concatenate([block_index, col_offset, counts], axis=1)
    message = pl.pallas_call(
        functools.partial(pack_kernel, band_count, group_count),
        out_shape=jax.ShapeDtypeStruct((peers, CAP, ROW), jnp.bfloat16),
        in_specs=[vmem] * 2,
        out_specs=vmem,
        compiler_params=pltpu.CompilerParams(vmem_limit_bytes=48 * 2**20),
        name="pack_blocks",
    )(blocks, whole)
    groups = [
        [b * group_count + q for b in range(band_count)]
        + [b * group_count + group_count - 1 - q for b in range(band_count)]
        for q in range(group_count // 2)
    ]
    received = lax.all_to_all(
        message, ("band", "wgrp"), 0, 0, axis_index_groups=groups, tiled=True
    )
    slots = peers * CAP
    base = pltpu.VMEM((2 * K // 128 * 8 * CAP, 128), jnp.float32)
    step = pltpu.VMEM((CAP, 2 * K), jnp.float32)
    rows = pl.pallas_call(
        functools.partial(grid_kernel, band_count, group_count),
        out_shape=jax.ShapeDtypeStruct((2, S * N2, N1), jnp.float32),
        in_specs=[vmem],
        out_specs=pl.BlockSpec(memory_space=pl.ANY),
        scratch_shapes=[
            pltpu.VMEM((2 * N1, 256), jnp.bfloat16),
            pltpu.VMEM((2 * N1, 256), jnp.bfloat16),
            pltpu.VMEM((2, N1, 128), jnp.float32),
            pltpu.VMEM((8, slots), jnp.int32),
            pltpu.SMEM((8, slots), jnp.int32),
            pltpu.VMEM((slots, DATA), jnp.float32),
            base,
            base,
            step,
            step,
            pltpu.VMEM((CAP * S, 128), jnp.float32),
            pltpu.VMEM((S // 8, (N1 + 2) * 8, 128), jnp.float32),
            pltpu.VMEM((2, S * N2, N1), jnp.float32),
            pltpu.SemaphoreType.DMA(()),
            pltpu.SemaphoreType.DMA((2, S // 8)),
        ],
        compiler_params=pltpu.CompilerParams(vmem_limit_bytes=48 * 2**20),
        name="grid_and_transform",
    )(received)
    lines = rows.reshape(1, 2, S // 8, N2, 8, N1).transpose(0, 1, 2, 4, 3, 5)
    return lines.reshape(1, 2, S, G)


def solution(mesh):
    placed = (
        P("wgrp", "band", None),
        P("wgrp", "band", None),
        P("wgrp", "band"),
        P("wgrp", "band"),
        P("wgrp", "band"),
    )
    return jax.shard_map(
        shards, mesh=mesh, in_specs=placed, out_specs=P("wgrp", None, "band", None), check_vma=False
    )
```

```python
import functools
import math

import jax
import jax.numpy as jnp
from jax import lax
from jax.experimental import pallas as pl
from jax.experimental.pallas import tpu as pltpu
from jax.sharding import PartitionSpec as P

S = 32
G = 8192
K = 256
GROUP = 2
STEP = 9
CAP = 8
HALF = S // 2
N1 = 128
N2 = 64
DATA = 4 * K
ROW = DATA + 128
LIVE = 32
LO = 64
PI = math.pi

SIN_TERMS = (0.99999999572, -0.1666665797, 0.0083330506173, -0.00019809046357, 2.6051662762e-06)
COS_TERMS = (0.99999995325, -0.49999905063, 0.041663578931, -0.0013853666933, 2.3153174156e-05)


def dot_last(left, right):
    return lax.dot_general(
        left, right, (((1,), (1,)), ((), ())), preferred_element_type=jnp.float32
    )


def dot_first(left, right):
    return lax.dot_general(
        left, right, (((0,), (0,)), ((), ())), preferred_element_type=jnp.float32
    )


def exchange_order(band_count):
    first = band_count * 5 // 8
    order = []
    for i in range(band_count):
        band = (first + i) % band_count
        order += [(band, 1), (band_count - 1 - band, 0)]
    return order


def in_low_half(group_count):
    return lax.axis_index("wgrp") < group_count // 2


def pack_kernel(band_count, group_count, data_ref, whole_ref, out_ref):
    below = in_low_half(group_count)
    order = exchange_order(band_count)
    slots = band_count * CAP
    block_index = whole_ref[:, :slots]
    offsets = whole_ref[:, slots : 2 * slots]
    count = whole_ref[:, 2 * slots :]
    blocks = data_ref.shape[0]
    lane = lax.broadcasted_iota(jnp.int32, (1, slots), 1)
    list_of = lane // CAP
    within = lane % CAP
    band_row = lax.broadcasted_iota(jnp.int32, (band_count, slots), 0)
    in_list = (band_row == list_of).astype(jnp.float32)
    counts = jnp.broadcast_to(count.astype(jnp.float32), (8, band_count))
    live_count = jnp.dot(counts, in_list, preferred_element_type=jnp.float32)[0:1]
    live = (within.astype(jnp.float32) < live_count).astype(jnp.float32)
    chosen = (
        lax.broadcasted_iota(jnp.int32, (blocks, slots), 0) == block_index
    ).astype(jnp.float32)
    vis = dot_first((chosen * live).astype(jnp.bfloat16), data_ref[:, : 2 * K])
    coord = dot_first(chosen.astype(jnp.bfloat16), data_ref[:, 2 * K :])
    here = lax.broadcasted_iota(jnp.int32, (CAP, slots), 0) == within
    high = jnp.where(here, (offsets >> 7).astype(jnp.float32), 0.0).astype(jnp.bfloat16)
    low = jnp.where(here, (offsets & 127).astype(jnp.float32), 0.0).astype(jnp.bfloat16)
    slot_row = lax.broadcasted_iota(jnp.int32, (slots, 128), 0) // CAP
    column = lax.broadcasted_iota(jnp.int32, (slots, 128), 1)
    to_high = (slot_row == column).astype(jnp.bfloat16)
    to_low = (slot_row + LO == column).astype(jnp.bfloat16)
    to_live = (slot_row + LIVE == column).astype(jnp.bfloat16)
    alive = jnp.where(here, live, 0.0).astype(jnp.bfloat16)
    meta = (
        jnp.dot(high, to_high, preferred_element_type=jnp.float32)
        + jnp.dot(low, to_low, preferred_element_type=jnp.float32)
        + jnp.dot(alive, to_live, preferred_element_type=jnp.float32)
    )
    for d in range(band_count):
        rows = slice(d * CAP, (d + 1) * CAP)
        message = jnp.concatenate([vis[rows], coord[rows], meta], axis=1).astype(jnp.bfloat16)
        flipped = band_count - 1 - d
        out_ref[jnp.where(below, order.index((d, 0)), order.index((d, 1)))] = message
        out_ref[jnp.where(below, order.index((flipped, 1)), order.index((flipped, 0)))] = message


def square(z):
    re, im = z
    return re * re - im * im, 2.0 * (re * im)


def times(z, w):
    return z[0] * w[0] - z[1] * w[1], z[0] * w[1] + z[1] * w[0]


def unit_phasor(cycles):
    half = (cycles - jnp.round(cycles)) * PI
    x = half * half
    sine = jnp.full_like(x, SIN_TERMS[-1])
    for term in SIN_TERMS[-2::-1]:
        sine = sine * x + term
    cosine = jnp.full_like(x, COS_TERMS[-1])
    for term in COS_TERMS[-2::-1]:
        cosine = cosine * x + term
    sine = sine * half
    return 1.0 - 2.0 * (sine * sine), 2.0 * (sine * cosine)


def turn_table(rows, column, length):
    row = lax.broadcasted_iota(jnp.int32, column.shape, 0)

    def turns(factor):
        return unit_phasor(((factor * column) & (length - 1)).astype(jnp.float32) * (1.0 / length))

    parts = [turns(row)]
    step = turns(jnp.full_like(row, 8))
    for _ in range(rows // 8 - 1):
        parts.append(times(parts[-1], step))
    return tuple(jnp.concatenate([z[i] for z in parts], axis=0) for i in range(2))


def fill_tables(outer_ref, inner_ref, twist_ref):
    column = lax.broadcasted_iota(jnp.int32, (8, 128), 1)
    column_in = column & (N2 - 1)
    outer = turn_table(N1, column, N1)
    left = lax.broadcasted_iota(jnp.int32, (N2, 128), 1) < N2
    inner = [
        jnp.concatenate([jnp.where(left, z, 0.0), jnp.where(left, 0.0, z)], axis=0)
        for z in turn_table(N2, column_in, N2)
    ]
    for ref, (cosine, sine) in ((outer_ref, outer), (inner_ref, inner)):
        cosine, sine = cosine.astype(jnp.bfloat16), sine.astype(jnp.bfloat16)
        ref[:N1, :128] = cosine
        ref[:N1, 128:] = sine
        ref[N1:, :128] = -sine
        ref[N1:, 128:] = cosine
    scale = 1.0 / math.sqrt(G * K)
    twist = turn_table(N1, column_in, G)
    twist_ref[0] = twist[0] * scale
    twist_ref[1] = twist[1] * -scale


def grid_kernel(
    band_count,
    group_count,
    recv_ref,
    out_ref,
    outer_ref,
    inner_ref,
    twist_ref,
    offset_vmem,
    offset_smem,
    data_ref,
    tab_re,
    tab_im,
    eight_re,
    eight_im,
    cells_ref,
    grid_ref,
    rows_ref,
    offset_sem,
    out_sem,
):
    below = in_low_half(group_count)
    band = lax.axis_index("band")

    slots = 2 * band_count * CAP
    flat = recv_ref[...].astype(jnp.float32).reshape(slots, ROW).astype(jnp.bfloat16)
    pick_row = lax.broadcasted_iota(jnp.int32, (8, 128), 0)
    pick_col = lax.broadcasted_iota(jnp.int32, (8, 128), 1)
    flipped = band_count - 1 - band
    wanted = jnp.full((8, 128), -1, jnp.int32)
    for i, at in enumerate((0, LO, LIVE)):
        wanted = jnp.where(pick_row == i, band + at, wanted)
        wanted = jnp.where(pick_row == i + 3, flipped + at, wanted)
    picked = dot_last((pick_col == wanted).astype(jnp.bfloat16), flat[:, DATA:])
    slot = lax.broadcasted_iota(jnp.int32, (1, slots), 1)
    from_low = jnp.zeros((1, slots), jnp.int32)
    for at, (_, half) in enumerate(exchange_order(band_count)):
        if half == 0:
            from_low = jnp.where(slot // CAP == at, 1, from_low)
    mine = from_low == below.astype(jnp.int32)
    high, low, live = (jnp.where(mine, picked[i : i + 1], picked[i + 3 : i + 4]) for i in range(3))
    offsets = (high * 128.0 + low).astype(jnp.int32)
    offsets = jnp.where(mine, offsets, (G - S) - offsets)

    live_own = jnp.where(mine, live, 0.0)
    live_mirror = live - live_own
    nothing = jnp.zeros((6, slots), jnp.float32)
    kinds = jnp.concatenate([live_own, live_mirror, nothing], axis=0).astype(jnp.bfloat16)
    earlier = (
        lax.broadcasted_iota(jnp.int32, (slots, slots), 0)
        < lax.broadcasted_iota(jnp.int32, (slots, slots), 1)
    ).astype(jnp.bfloat16)
    before = jnp.dot(kinds, earlier, preferred_element_type=jnp.float32)
    own_groups, mirror_groups = (
        jnp.floor((jnp.sum(z, axis=1, keepdims=True) + (CAP - 1)) * (1.0 / CAP))
        for z in (live_own, live_mirror)
    )
    position = jnp.where(mine, before[0:1], before[1:2] + CAP * own_groups)
    position = jnp.where(live > 0.5, position, -1.0).astype(jnp.int32)
    moves = (
        lax.broadcasted_iota(jnp.int32, (slots, slots), 0) == position
    ).astype(jnp.bfloat16)
    data_ref[...] = jnp.dot(moves, flat[:, :DATA], preferred_element_type=jnp.float32)
    parts = jnp.concatenate(
        [(offsets >> 7).astype(jnp.float32), (offsets & 127).astype(jnp.float32), nothing], axis=0
    )
    moved = dot_last(parts.astype(jnp.bfloat16), moves)
    offset_vmem[0:1] = (moved[0:1] * 128.0 + moved[1:2]).astype(jnp.int32)
    offset_vmem[1:2] = jnp.broadcast_to(own_groups, (1, slots)).astype(jnp.int32)
    offset_vmem[2:3] = jnp.broadcast_to(own_groups + mirror_groups, (1, slots)).astype(jnp.int32)
    to_smem = pltpu.make_async_copy(offset_vmem, offset_smem, offset_sem)
    to_smem.start()

    def clear(step, _):
        rows = pl.ds(pl.multiple_of(step * 24, 24), 24)
        for block in range(S // 8):
            grid_ref[block, rows, :] = jnp.zeros((24, 128), jnp.float32)
        return 0

    lax.fori_loop(0, grid_ref.shape[1] // 24, clear, 0)

    lane = lax.broadcasted_iota(jnp.int32, (8, 128), 1)
    first_half = lane < N2
    lane_in = lane & (N2 - 1)
    turn_sign = jnp.where(lax.broadcasted_iota(jnp.int32, (S, 128), 1) < N2, -1.0, 1.0)
    chunks = 2 * K // 128

    def add_cells(cells, start, offset):
        row = (offset >> 6) * STEP
        shift = offset & (N2 - 1)
        near, far = (shift + 128 - start) & 127, (shift + N2 - start) & 127
        stays = (lane_in >= shift) & (lane_in < shift + S)
        wraps = lane_in < shift - (N2 - S)
        for block in range(HALF // 8):
            upper = cells[block * 8 : block * 8 + 8]
            lower = cells[HALF + block * 8 : HALF + block * 8 + 8]
            even = jnp.where(first_half, pltpu.roll(upper, near, 1), pltpu.roll(lower, far, 1))
            odd = jnp.where(first_half, pltpu.roll(upper, far, 1), pltpu.roll(lower, near, 1))
            for part, here, over in ((0, even, odd), (1, odd, even)):
                for at, piece in ((row, jnp.where(stays, here, 0.0)), (row + STEP, jnp.where(wraps, over, 0.0))):
                    rows = pl.ds(at, 8)
                    grid_ref[part * (HALF // 8) + block, rows, :] += piece

    def make_tables(group, mirrored):
        block = data_ref[pl.ds(pl.multiple_of(group * CAP, CAP), CAP), :]
        flip = jnp.where(mirrored == 1, -1.0, 1.0)
        vis = (block[:, 0:K], block[:, K : 2 * K] * flip)
        e1 = unit_phasor(block[:, 2 * K : 4 * K] * (1.0 / S))
        e2 = square(e1)
        e4 = square(e2)
        cc, ss, cs, sc = e4[0] * e1[0], e4[1] * e1[1], e4[0] * e1[1], e4[1] * e1[0]
        e3, e5 = (cc + ss, sc - cs), (cc - ss, sc + cs)
        e8 = square(e4)
        edge = tuple(jnp.where(mirrored == 1, z, one) for z, one in zip(e8, (1.0, 0.0)))
        for b, e in enumerate((edge, e1, e2, e3, e4, e5, square(e3), times(e4, e3))):
            at = 7 * mirrored if b == 0 else b - mirrored
            weighted = times(vis, (e[0][:, :K], e[1][:, :K]))
            for tab, z, e_part in ((tab_re, weighted[0], e[0]), (tab_im, weighted[1], e[1])):
                whole = jnp.concatenate([z, e_part[:, K:]], axis=1)
                for q in range(chunks):
                    tab[pl.ds(q * STEP * CAP + at, CAP, stride=STEP), :] = whole[:, q * 128 : (q + 1) * 128]
        eight_re[...] = e8[0]
        eight_im[...] = e8[1]

    def multiply():
        products = []
        for first in range(0, CAP, GROUP):
            left, real, imag = [], [], []
            for c in range(first, first + GROUP):
                base = tuple(
                    jnp.concatenate(
                        [tab[(q * CAP + c) * STEP : (q * CAP + c) * STEP + 8, :] for q in range(chunks)],
                        axis=1,
                    )
                    for tab in (tab_re, tab_im)
                )
                c8 = jnp.broadcast_to(eight_re[c : c + 1, :], (8, 2 * K))
                s8 = jnp.broadcast_to(eight_im[c : c + 1, :], (8, 2 * K))
                cc, ss, cs, sc = base[0] * c8, base[1] * s8, base[0] * s8, base[1] * c8
                up = (cc - ss, sc + cs)
                down = (cc + ss, sc - cs)
                down2 = (down[0] * c8 + down[1] * s8, down[1] * c8 - down[0] * s8)
                order = (down2, down, base, up)
                re = jnp.concatenate([z[0] for z in order], axis=0).astype(jnp.bfloat16)
                im = jnp.concatenate([z[1] for z in order], axis=0).astype(jnp.bfloat16)
                left += [re[:, K:], im[:, K:]]
                real.append(re[:, :K])
                imag.append(im[:, :K])
            right = []
            for c in range(0, GROUP, 2):
                right += real[c : c + 2] + imag[c : c + 2]
            cells = dot_last(jnp.concatenate(left, axis=0), jnp.concatenate(right, axis=0))
            products.append(cells)
        return products

    def keep(products):
        for c in range(CAP):
            row, tile = 2 * (c % GROUP) * S, c % GROUP // 2 * 128
            cells_ref[2 * c * S : 2 * (c + 1) * S, :] = products[c // GROUP][
                row : row + 2 * S, tile : tile + 128
            ]

    def add_group(group):
        for c in range(CAP):
            by_cos = cells_ref[2 * c * S : (2 * c + 1) * S, :]
            by_sin = pltpu.roll(cells_ref[(2 * c + 1) * S : (2 * c + 2) * S, :], N2, 1)
            add_cells(by_cos + turn_sign * by_sin, c % 2 * S, offset_smem[0, group * CAP + c])

    make_tables(0, jnp.int32(0))
    fill_tables(outer_ref, inner_ref, twist_ref)
    keep(multiply())
    to_smem.wait()
    first_mirrored, groups = offset_smem[1, 0], offset_smem[2, 0]

    def tables_of(group):
        group = jnp.minimum(group, groups - 1)
        make_tables(group, (group >= first_mirrored).astype(jnp.int32))

    tables_of(1)

    def turn(group, _):
        products = multiply()
        add_group(group - 1)
        keep(products)
        tables_of(group + 1)
        return 0

    lax.fori_loop(1, groups, turn, 0)
    add_group(groups - 1)

    def out_copy(part, group):
        rows = pl.ds(group * 8 * N2, 8 * N2)
        return pltpu.make_async_copy(
            rows_ref.at[part, rows, :], out_ref.at[part, rows, :], out_sem.at[part, group]
        )

    twist_re, twist_im = twist_ref[0], twist_ref[1]
    for pair in range(HALF // 2):
        lines = (2 * pair, 2 * pair + 1)
        field = jnp.concatenate(
            [
                jnp.concatenate(
                    [
                        grid_ref[
                            part * (HALF // 8) + y // 8, pl.ds(y % 8, N1, stride=STEP), :
                        ].astype(jnp.bfloat16)
                        for y in lines
                    ],
                    axis=1,
                )
                for part in range(2)
            ],
            axis=0,
        )
        section = jnp.dot(outer_ref[...], field, preferred_element_type=jnp.float32)
        twisted = []
        for p in range(2):
            re = section[:N1, p * 128 : (p + 1) * 128]
            im = section[N1:, p * 128 : (p + 1) * 128]
            twisted.append(
                jnp.concatenate(
                    [re * twist_re - im * twist_im, re * twist_im + im * twist_re], axis=1
                ).astype(jnp.bfloat16)
            )
        spectrum = dot_last(inner_ref[...], jnp.concatenate(twisted, axis=0))
        for part in range(2):
            for half in range(2):
                for p, y in enumerate(lines):
                    start = (part * 2 + half) * N2
                    line = half * HALF + y
                    rows_ref[part, pl.ds((line // 8) * 8 * N2 + line % 8, N2, stride=8), :] = spectrum[
                        start : start + N2, p * 128 : (p + 1) * 128
                    ]
        if lines[1] % 8 == 7:
            for part in range(2):
                for half in range(2):
                    out_copy(part, half * (HALF // 8) + lines[1] // 8).start()
    for part in range(2):
        for group in range(S // 8):
            out_copy(part, group).wait()


def shards(visibilities, coordinates, block_index, counts, col_offset):
    band_count = lax.axis_size("band")
    group_count = lax.axis_size("wgrp")
    peers = 2 * band_count
    vmem = pl.BlockSpec(memory_space=pltpu.VMEM)
    hbm = pl.BlockSpec(memory_space=pltpu.HBM)
    blocks = jnp.concatenate([visibilities[0], coordinates[0]], axis=1)
    whole = jnp.concatenate([block_index, col_offset, counts], axis=1)
    message = pl.pallas_call(
        functools.partial(pack_kernel, band_count, group_count),
        out_shape=jax.ShapeDtypeStruct((peers, CAP, ROW), jnp.bfloat16),
        in_specs=[vmem] * 2,
        out_specs=vmem,
        compiler_params=pltpu.CompilerParams(vmem_limit_bytes=48 * 2**20),
        name="pack_blocks",
    )(blocks, whole)
    groups = [
        [b * group_count + (q if half == 0 else group_count - 1 - q) for b, half in exchange_order(band_count)]
        for q in range(group_count // 2)
    ]
    received = lax.all_to_all(
        message, ("band", "wgrp"), 0, 0, axis_index_groups=groups, tiled=True
    )
    slots = peers * CAP
    base = pltpu.VMEM((2 * K // 128 * STEP * CAP, 128), jnp.float32)
    step = pltpu.VMEM((CAP, 2 * K), jnp.float32)
    rows = pl.pallas_call(
        functools.partial(grid_kernel, band_count, group_count),
        out_shape=jax.ShapeDtypeStruct((2, S * N2, N1), jnp.float32),
        in_specs=[vmem],
        out_specs=pl.BlockSpec(memory_space=pl.ANY),
        scratch_shapes=[
            pltpu.VMEM((2 * N1, 256), jnp.bfloat16),
            pltpu.VMEM((2 * N1, 256), jnp.bfloat16),
            pltpu.VMEM((2, N1, 128), jnp.float32),
            pltpu.VMEM((8, slots), jnp.int32),
            pltpu.SMEM((8, slots), jnp.int32),
            pltpu.VMEM((slots, DATA), jnp.float32),
            base,
            base,
            step,
            step,
            pltpu.VMEM((CAP * 2 * S, 128), jnp.float32),
            pltpu.VMEM((S // 8, pl.cdiv((N1 + 2) * STEP, 24) * 24, 128), jnp.float32),
            pltpu.VMEM((2, S * N2, N1), jnp.float32),
            pltpu.SemaphoreType.DMA(()),
            pltpu.SemaphoreType.DMA((2, S // 8)),
        ],
        compiler_params=pltpu.CompilerParams(vmem_limit_bytes=48 * 2**20),
        name="grid_and_transform",
    )(received)
    lines = rows.reshape(1, 2, S // 8, N2, 8, N1).transpose(0, 1, 2, 4, 3, 5)
    return lines.reshape(1, 2, S, G)


def solution(mesh):
    placed = (
        P("wgrp", "band", None),
        P("wgrp", "band", None),
        P("wgrp", "band"),
        P("wgrp", "band"),
        P("wgrp", "band"),
    )
    return jax.shard_map(
        shards, mesh=mesh, in_specs=placed, out_specs=P("wgrp", None, "band", None), check_vma=False
    )
```

```python
import functools
import math

import jax
import jax.numpy as jnp
from jax import lax
from jax.experimental import pallas as pl
from jax.experimental.pallas import tpu as pltpu
from jax.sharding import PartitionSpec as P

S = 32
G = 8192
K = 256
GROUP = 2
STEP = 9
CAP = 8
HALF = S // 2
N1 = 128
N2 = 64
DATA = 4 * K
ROW = DATA + 128
LIVE = 32
LO = 64
PI = math.pi

SIN_TERMS = (0.99999999572, -0.1666665797, 0.0083330506173, -0.00019809046357, 2.6051662762e-06)
COS_TERMS = (0.99999995325, -0.49999905063, 0.041663578931, -0.0013853666933, 2.3153174156e-05)


def dot_last(left, right):
    return lax.dot_general(
        left, right, (((1,), (1,)), ((), ())), preferred_element_type=jnp.float32
    )


def dot_first(left, right):
    return lax.dot_general(
        left, right, (((0,), (0,)), ((), ())), preferred_element_type=jnp.float32
    )


def exchange_order(band_count):
    first = band_count * 5 // 8
    order = []
    for i in range(band_count):
        band = (first + i) % band_count
        order += [(band, 1), (band_count - 1 - band, 0)]
    return order


def in_low_half(group_count):
    return lax.axis_index("wgrp") < group_count // 2


def pack_kernel(band_count, group_count, *refs):
    sources, out_ref, targets, sems = refs[:5], refs[5], refs[6:11], refs[11]
    copies = [
        pltpu.make_async_copy(source, target, sems.at[i])
        for i, (source, target) in enumerate(zip(sources, targets))
    ]
    for copy in copies:
        copy.start()
    vis_ref, coord_ref, block_ref, count_ref, offset_ref = targets
    below = in_low_half(group_count)
    order = exchange_order(band_count)
    slots = band_count * CAP
    blocks = vis_ref.shape[0]
    for copy in copies:
        copy.wait()
    block_index, count, offsets = block_ref[...], count_ref[...], offset_ref[...]
    lane = lax.broadcasted_iota(jnp.int32, (1, slots), 1)
    list_of = lane // CAP
    within = lane % CAP
    band_row = lax.broadcasted_iota(jnp.int32, (band_count, slots), 0)
    in_list = (band_row == list_of).astype(jnp.float32)
    counts = jnp.broadcast_to(count.astype(jnp.float32), (8, band_count))
    live_count = jnp.dot(counts, in_list, preferred_element_type=jnp.float32)[0:1]
    live = (within.astype(jnp.float32) < live_count).astype(jnp.float32)
    chosen = (
        lax.broadcasted_iota(jnp.int32, (blocks, slots), 0) == block_index
    ).astype(jnp.float32)
    vis = dot_first((chosen * live).astype(jnp.bfloat16), vis_ref[...])
    coord = dot_first(chosen.astype(jnp.bfloat16), coord_ref[...])
    here = lax.broadcasted_iota(jnp.int32, (CAP, slots), 0) == within
    high = jnp.where(here, (offsets >> 7).astype(jnp.float32), 0.0).astype(jnp.bfloat16)
    low = jnp.where(here, (offsets & 127).astype(jnp.float32), 0.0).astype(jnp.bfloat16)
    slot_row = lax.broadcasted_iota(jnp.int32, (slots, 128), 0) // CAP
    column = lax.broadcasted_iota(jnp.int32, (slots, 128), 1)
    to_high = (slot_row == column).astype(jnp.bfloat16)
    to_low = (slot_row + LO == column).astype(jnp.bfloat16)
    to_live = (slot_row + LIVE == column).astype(jnp.bfloat16)
    alive = jnp.where(here, live, 0.0).astype(jnp.bfloat16)
    meta = (
        jnp.dot(high, to_high, preferred_element_type=jnp.float32)
        + jnp.dot(low, to_low, preferred_element_type=jnp.float32)
        + jnp.dot(alive, to_live, preferred_element_type=jnp.float32)
    )
    for d in range(band_count):
        rows = slice(d * CAP, (d + 1) * CAP)
        message = jnp.concatenate([vis[rows], coord[rows], meta], axis=1).astype(jnp.bfloat16)
        flipped = band_count - 1 - d
        out_ref[jnp.where(below, order.index((d, 0)), order.index((d, 1)))] = message
        out_ref[jnp.where(below, order.index((flipped, 1)), order.index((flipped, 0)))] = message


def square(z):
    re, im = z
    return re * re - im * im, 2.0 * (re * im)


def times(z, w):
    return z[0] * w[0] - z[1] * w[1], z[0] * w[1] + z[1] * w[0]


def unit_phasor(cycles):
    half = (cycles - jnp.round(cycles)) * PI
    x = half * half
    sine = jnp.full_like(x, SIN_TERMS[-1])
    for term in SIN_TERMS[-2::-1]:
        sine = sine * x + term
    cosine = jnp.full_like(x, COS_TERMS[-1])
    for term in COS_TERMS[-2::-1]:
        cosine = cosine * x + term
    sine = sine * half
    return 1.0 - 2.0 * (sine * sine), 2.0 * (sine * cosine)


def turn_table(rows, column, length):
    row = lax.broadcasted_iota(jnp.int32, column.shape, 0)

    def turns(factor):
        return unit_phasor(((factor * column) & (length - 1)).astype(jnp.float32) * (1.0 / length))

    parts = [turns(row)]
    step = turns(jnp.full_like(row, 8))
    for _ in range(rows // 8 - 1):
        parts.append(times(parts[-1], step))
    return tuple(jnp.concatenate([z[i] for z in parts], axis=0) for i in range(2))


def fill_tables(outer_ref, inner_ref, twist_ref):
    column = lax.broadcasted_iota(jnp.int32, (8, 128), 1)
    column_in = column & (N2 - 1)
    outer = turn_table(N1, column, N1)
    left = lax.broadcasted_iota(jnp.int32, (N2, 128), 1) < N2
    inner = [
        jnp.concatenate([jnp.where(left, z, 0.0), jnp.where(left, 0.0, z)], axis=0)
        for z in turn_table(N2, column_in, N2)
    ]
    for ref, (cosine, sine) in ((outer_ref, outer), (inner_ref, inner)):
        cosine, sine = cosine.astype(jnp.bfloat16), sine.astype(jnp.bfloat16)
        ref[:N1, :128] = cosine
        ref[:N1, 128:] = sine
        ref[N1:, :128] = -sine
        ref[N1:, 128:] = cosine
    scale = 1.0 / math.sqrt(G * K)
    twist = turn_table(N1, column_in, G)
    twist_ref[0] = twist[0] * scale
    twist_ref[1] = twist[1] * -scale


def grid_kernel(
    band_count,
    group_count,
    recv_ref,
    out_ref,
    outer_ref,
    inner_ref,
    twist_ref,
    offset_vmem,
    offset_smem,
    data_ref,
    tab_re,
    tab_im,
    eight_re,
    eight_im,
    cells_ref,
    grid_ref,
    rows_ref,
    offset_sem,
    out_sem,
):
    below = in_low_half(group_count)
    band = lax.axis_index("band")

    slots = 2 * band_count * CAP
    flat = recv_ref[...].astype(jnp.float32).reshape(slots, ROW).astype(jnp.bfloat16)
    pick_row = lax.broadcasted_iota(jnp.int32, (8, 128), 0)
    pick_col = lax.broadcasted_iota(jnp.int32, (8, 128), 1)
    flipped = band_count - 1 - band
    wanted = jnp.full((8, 128), -1, jnp.int32)
    for i, at in enumerate((0, LO, LIVE)):
        wanted = jnp.where(pick_row == i, band + at, wanted)
        wanted = jnp.where(pick_row == i + 3, flipped + at, wanted)
    picked = dot_last((pick_col == wanted).astype(jnp.bfloat16), flat[:, DATA:])
    slot = lax.broadcasted_iota(jnp.int32, (1, slots), 1)
    from_low = jnp.zeros((1, slots), jnp.int32)
    for at, (_, half) in enumerate(exchange_order(band_count)):
        if half == 0:
            from_low = jnp.where(slot // CAP == at, 1, from_low)
    mine = from_low == below.astype(jnp.int32)
    high, low, live = (jnp.where(mine, picked[i : i + 1], picked[i + 3 : i + 4]) for i in range(3))
    offsets = (high * 128.0 + low).astype(jnp.int32)
    offsets = jnp.where(mine, offsets, (G - S) - offsets)

    live_own = jnp.where(mine, live, 0.0)
    live_mirror = live - live_own
    nothing = jnp.zeros((6, slots), jnp.float32)
    kinds = jnp.concatenate([live_own, live_mirror, nothing], axis=0).astype(jnp.bfloat16)
    earlier = (
        lax.broadcasted_iota(jnp.int32, (slots, slots), 0)
        < lax.broadcasted_iota(jnp.int32, (slots, slots), 1)
    ).astype(jnp.bfloat16)
    before = jnp.dot(kinds, earlier, preferred_element_type=jnp.float32)
    own_groups, mirror_groups = (
        jnp.floor((jnp.sum(z, axis=1, keepdims=True) + (CAP - 1)) * (1.0 / CAP))
        for z in (live_own, live_mirror)
    )
    position = jnp.where(mine, before[0:1], before[1:2] + CAP * own_groups)
    position = jnp.where(live > 0.5, position, -1.0).astype(jnp.int32)
    moves = (
        lax.broadcasted_iota(jnp.int32, (slots, slots), 0) == position
    ).astype(jnp.bfloat16)
    data_ref[...] = jnp.dot(moves, flat[:, :DATA], preferred_element_type=jnp.float32)
    parts = jnp.concatenate(
        [(offsets >> 7).astype(jnp.float32), (offsets & 127).astype(jnp.float32), nothing], axis=0
    )
    moved = dot_last(parts.astype(jnp.bfloat16), moves)
    offset_vmem[0:1] = (moved[0:1] * 128.0 + moved[1:2]).astype(jnp.int32)
    offset_vmem[1:2] = jnp.broadcast_to(own_groups, (1, slots)).astype(jnp.int32)
    offset_vmem[2:3] = jnp.broadcast_to(own_groups + mirror_groups, (1, slots)).astype(jnp.int32)
    to_smem = pltpu.make_async_copy(offset_vmem, offset_smem, offset_sem)
    to_smem.start()

    def clear(step, _):
        rows = pl.ds(pl.multiple_of(step * 24, 24), 24)
        for block in range(S // 8):
            grid_ref[block, rows, :] = jnp.zeros((24, 128), jnp.float32)
        return 0

    lax.fori_loop(0, grid_ref.shape[1] // 24, clear, 0)

    lane = lax.broadcasted_iota(jnp.int32, (8, 128), 1)
    first_half = lane < N2
    lane_in = lane & (N2 - 1)
    turn_sign = jnp.where(lax.broadcasted_iota(jnp.int32, (S, 128), 1) < N2, -1.0, 1.0)
    chunks = 2 * K // 128

    def add_cells(cells, start, offset):
        row = (offset >> 6) * STEP
        shift = offset & (N2 - 1)
        near, far = (shift + 128 - start) & 127, (shift + N2 - start) & 127
        stays = (lane_in >= shift) & (lane_in < shift + S)
        wraps = lane_in < shift - (N2 - S)
        for block in range(HALF // 8):
            upper = cells[block * 8 : block * 8 + 8]
            lower = cells[HALF + block * 8 : HALF + block * 8 + 8]
            even = jnp.where(first_half, pltpu.roll(upper, near, 1), pltpu.roll(lower, far, 1))
            odd = jnp.where(first_half, pltpu.roll(upper, far, 1), pltpu.roll(lower, near, 1))
            for part, here, over in ((0, even, odd), (1, odd, even)):
                for at, piece in ((row, jnp.where(stays, here, 0.0)), (row + STEP, jnp.where(wraps, over, 0.0))):
                    rows = pl.ds(at, 8)
                    grid_ref[part * (HALF // 8) + block, rows, :] += piece

    def make_tables(group, mirrored):
        block = data_ref[pl.ds(pl.multiple_of(group * CAP, CAP), CAP), :]
        flip = jnp.where(mirrored == 1, -1.0, 1.0)
        vis = (block[:, 0:K], block[:, K : 2 * K] * flip)
        e1 = unit_phasor(block[:, 2 * K : 4 * K] * (1.0 / S))
        e2 = square(e1)
        e4 = square(e2)
        cc, ss, cs, sc = e4[0] * e1[0], e4[1] * e1[1], e4[0] * e1[1], e4[1] * e1[0]
        e3, e5 = (cc + ss, sc - cs), (cc - ss, sc + cs)
        e8 = square(e4)
        edge = tuple(jnp.where(mirrored == 1, z, one) for z, one in zip(e8, (1.0, 0.0)))
        for b, e in enumerate((edge, e1, e2, e3, e4, e5, square(e3), times(e4, e3))):
            at = 7 * mirrored if b == 0 else b - mirrored
            weighted = times(vis, (e[0][:, :K], e[1][:, :K]))
            for tab, z, e_part in ((tab_re, weighted[0], e[0]), (tab_im, weighted[1], e[1])):
                whole = jnp.concatenate([z, e_part[:, K:]], axis=1)
                for q in range(chunks):
                    tab[pl.ds(q * STEP * CAP + at, CAP, stride=STEP), :] = whole[:, q * 128 : (q + 1) * 128]
        eight_re[...] = e8[0]
        eight_im[...] = e8[1]

    def multiply():
        products = []
        for first in range(0, CAP, GROUP):
            left, real, imag = [], [], []
            for c in range(first, first + GROUP):
                base = tuple(
                    jnp.concatenate(
                        [tab[(q * CAP + c) * STEP : (q * CAP + c) * STEP + 8, :] for q in range(chunks)],
                        axis=1,
                    )
                    for tab in (tab_re, tab_im)
                )
                c8 = jnp.broadcast_to(eight_re[c : c + 1, :], (8, 2 * K))
                s8 = jnp.broadcast_to(eight_im[c : c + 1, :], (8, 2 * K))
                cc, ss, cs, sc = base[0] * c8, base[1] * s8, base[0] * s8, base[1] * c8
                up = (cc - ss, sc + cs)
                down = (cc + ss, sc - cs)
                down2 = (down[0] * c8 + down[1] * s8, down[1] * c8 - down[0] * s8)
                order = (down2, down, base, up)
                re = jnp.concatenate([z[0] for z in order], axis=0).astype(jnp.bfloat16)
                im = jnp.concatenate([z[1] for z in order], axis=0).astype(jnp.bfloat16)
                left += [re[:, K:], im[:, K:]]
                real.append(re[:, :K])
                imag.append(im[:, :K])
            right = []
            for c in range(0, GROUP, 2):
                right += real[c : c + 2] + imag[c : c + 2]
            cells = dot_last(jnp.concatenate(left, axis=0), jnp.concatenate(right, axis=0))
            products.append(cells)
        return products

    def keep(products):
        for c in range(CAP):
            row, tile = 2 * (c % GROUP) * S, c % GROUP // 2 * 128
            cells_ref[2 * c * S : 2 * (c + 1) * S, :] = products[c // GROUP][
                row : row + 2 * S, tile : tile + 128
            ]

    def add_group(group):
        for c in range(CAP):
            by_cos = cells_ref[2 * c * S : (2 * c + 1) * S, :]
            by_sin = pltpu.roll(cells_ref[(2 * c + 1) * S : (2 * c + 2) * S, :], N2, 1)
            add_cells(by_cos + turn_sign * by_sin, c % 2 * S, offset_smem[0, group * CAP + c])

    make_tables(0, jnp.int32(0))
    fill_tables(outer_ref, inner_ref, twist_ref)
    keep(multiply())
    to_smem.wait()
    first_mirrored, groups = offset_smem[1, 0], offset_smem[2, 0]

    def tables_of(group):
        group = jnp.minimum(group, groups - 1)
        make_tables(group, (group >= first_mirrored).astype(jnp.int32))

    tables_of(1)

    def turn(group, _):
        products = multiply()
        add_group(group - 1)
        keep(products)
        tables_of(group + 1)
        return 0

    lax.fori_loop(1, groups, turn, 0)
    add_group(groups - 1)

    def out_copy(part, group):
        rows = pl.ds(group * 8 * N2, 8 * N2)
        return pltpu.make_async_copy(
            rows_ref.at[part, rows, :], out_ref.at[part, rows, :], out_sem.at[part, group]
        )

    twist_re, twist_im = twist_ref[0], twist_ref[1]
    for pair in range(HALF // 2):
        lines = (2 * pair, 2 * pair + 1)
        field = jnp.concatenate(
            [
                jnp.concatenate(
                    [
                        grid_ref[
                            part * (HALF // 8) + y // 8, pl.ds(y % 8, N1, stride=STEP), :
                        ].astype(jnp.bfloat16)
                        for y in lines
                    ],
                    axis=1,
                )
                for part in range(2)
            ],
            axis=0,
        )
        section = jnp.dot(outer_ref[...], field, preferred_element_type=jnp.float32)
        twisted = []
        for p in range(2):
            re = section[:N1, p * 128 : (p + 1) * 128]
            im = section[N1:, p * 128 : (p + 1) * 128]
            twisted.append(
                jnp.concatenate(
                    [re * twist_re - im * twist_im, re * twist_im + im * twist_re], axis=1
                ).astype(jnp.bfloat16)
            )
        spectrum = dot_last(inner_ref[...], jnp.concatenate(twisted, axis=0))
        for part in range(2):
            for half in range(2):
                for p, y in enumerate(lines):
                    start = (part * 2 + half) * N2
                    line = half * HALF + y
                    rows_ref[part, pl.ds((line // 8) * 8 * N2 + line % 8, N2, stride=8), :] = spectrum[
                        start : start + N2, p * 128 : (p + 1) * 128
                    ]
        if lines[1] % 8 == 7:
            for part in range(2):
                for half in range(2):
                    out_copy(part, half * (HALF // 8) + lines[1] // 8).start()
    for part in range(2):
        for group in range(S // 8):
            out_copy(part, group).wait()


def shards(visibilities, coordinates, block_index, counts, col_offset):
    band_count = lax.axis_size("band")
    group_count = lax.axis_size("wgrp")
    peers = 2 * band_count
    vmem = pl.BlockSpec(memory_space=pltpu.VMEM)
    hbm = pl.BlockSpec(memory_space=pltpu.HBM)
    inputs = [
        pltpu.with_memory_space_constraint(a, pltpu.HBM)
        for a in (visibilities[0], coordinates[0], block_index, counts, col_offset)
    ]
    message = pl.pallas_call(
        functools.partial(pack_kernel, band_count, group_count),
        out_shape=jax.ShapeDtypeStruct((peers, CAP, ROW), jnp.bfloat16),
        in_specs=[pl.BlockSpec(memory_space=pltpu.HBM)] * len(inputs),
        out_specs=vmem,
        scratch_shapes=[pltpu.VMEM(a.shape, a.dtype) for a in inputs]
        + [pltpu.SemaphoreType.DMA((len(inputs),))],
        compiler_params=pltpu.CompilerParams(vmem_limit_bytes=48 * 2**20),
        name="pack_blocks",
    )(*inputs)
    groups = [
        [b * group_count + (q if half == 0 else group_count - 1 - q) for b, half in exchange_order(band_count)]
        for q in range(group_count // 2)
    ]
    received = lax.all_to_all(
        message, ("band", "wgrp"), 0, 0, axis_index_groups=groups, tiled=True
    )
    slots = peers * CAP
    base = pltpu.VMEM((2 * K // 128 * STEP * CAP, 128), jnp.float32)
    step = pltpu.VMEM((CAP, 2 * K), jnp.float32)
    rows = pl.pallas_call(
        functools.partial(grid_kernel, band_count, group_count),
        out_shape=jax.ShapeDtypeStruct((2, S * N2, N1), jnp.float32),
        in_specs=[vmem],
        out_specs=pl.BlockSpec(memory_space=pl.ANY),
        scratch_shapes=[
            pltpu.VMEM((2 * N1, 256), jnp.bfloat16),
            pltpu.VMEM((2 * N1, 256), jnp.bfloat16),
            pltpu.VMEM((2, N1, 128), jnp.float32),
            pltpu.VMEM((8, slots), jnp.int32),
            pltpu.SMEM((8, slots), jnp.int32),
            pltpu.VMEM((slots, DATA), jnp.float32),
            base,
            base,
            step,
            step,
            pltpu.VMEM((CAP * 2 * S, 128), jnp.float32),
            pltpu.VMEM((S // 8, pl.cdiv((N1 + 2) * STEP, 24) * 24, 128), jnp.float32),
            pltpu.VMEM((2, S * N2, N1), jnp.float32),
            pltpu.SemaphoreType.DMA(()),
            pltpu.SemaphoreType.DMA((2, S // 8)),
        ],
        compiler_params=pltpu.CompilerParams(vmem_limit_bytes=48 * 2**20),
        name="grid_and_transform",
    )(received)
    lines = rows.reshape(1, 2, S // 8, N2, 8, N1).transpose(0, 1, 2, 4, 3, 5)
    return lines.reshape(1, 2, S, G)


def solution(mesh):
    placed = (
        P("wgrp", "band", None),
        P("wgrp", "band", None),
        P("wgrp", "band"),
        P("wgrp", "band"),
        P("wgrp", "band"),
    )
    return jax.shard_map(
        shards, mesh=mesh, in_specs=placed, out_specs=P("wgrp", None, "band", None), check_vma=False
    )
```

```python
import functools
import math

import jax
import jax.numpy as jnp
from jax import lax
from jax.experimental import pallas as pl
from jax.experimental.pallas import tpu as pltpu
from jax.sharding import PartitionSpec as P

S = 32
G = 8192
K = 256
GROUP = 4
STEP = 9
CAP = 8
HALF = S // 2
N1 = 128
N2 = 64
DATA = 4 * K
ROW = DATA + 128
LIVE = 32
LO = 64
PI = math.pi

SIN_TERMS = (0.99999999572, -0.1666665797, 0.0083330506173, -0.00019809046357, 2.6051662762e-06)
COS_TERMS = (0.99999995325, -0.49999905063, 0.041663578931, -0.0013853666933, 2.3153174156e-05)


def dot_last(left, right):
    return lax.dot_general(
        left, right, (((1,), (1,)), ((), ())), preferred_element_type=jnp.float32
    )


def dot_first(left, right):
    return lax.dot_general(
        left, right, (((0,), (0,)), ((), ())), preferred_element_type=jnp.float32
    )


def exchange_order(band_count):
    first = band_count * 5 // 8
    order = []
    for i in range(band_count):
        band = (first + i) % band_count
        order += [(band, 1), (band_count - 1 - band, 0)]
    return order


def in_low_half(group_count):
    return lax.axis_index("wgrp") < group_count // 2


def pack_kernel(band_count, group_count, *refs):
    sources, out_ref, targets, sems = refs[:5], refs[5], refs[6:11], refs[11]
    copies = [
        pltpu.make_async_copy(source, target, sems.at[i])
        for i, (source, target) in enumerate(zip(sources, targets))
    ]
    for copy in copies:
        copy.start()
    vis_ref, coord_ref, block_ref, count_ref, offset_ref = targets
    below = in_low_half(group_count)
    order = exchange_order(band_count)
    slots = band_count * CAP
    blocks = vis_ref.shape[0]
    for copy in copies:
        copy.wait()
    block_index, count, offsets = block_ref[...], count_ref[...], offset_ref[...]
    lane = lax.broadcasted_iota(jnp.int32, (1, slots), 1)
    list_of = lane // CAP
    within = lane % CAP
    band_row = lax.broadcasted_iota(jnp.int32, (band_count, slots), 0)
    in_list = (band_row == list_of).astype(jnp.float32)
    counts = jnp.broadcast_to(count.astype(jnp.float32), (8, band_count))
    live_count = jnp.dot(counts, in_list, preferred_element_type=jnp.float32)[0:1]
    live = (within.astype(jnp.float32) < live_count).astype(jnp.float32)
    chosen = (
        lax.broadcasted_iota(jnp.int32, (blocks, slots), 0) == block_index
    ).astype(jnp.float32)
    vis = dot_first((chosen * live).astype(jnp.bfloat16), vis_ref[...])
    coord = dot_first(chosen.astype(jnp.bfloat16), coord_ref[...])
    here = lax.broadcasted_iota(jnp.int32, (CAP, slots), 0) == within
    high = jnp.where(here, (offsets >> 7).astype(jnp.float32), 0.0).astype(jnp.bfloat16)
    low = jnp.where(here, (offsets & 127).astype(jnp.float32), 0.0).astype(jnp.bfloat16)
    slot_row = lax.broadcasted_iota(jnp.int32, (slots, 128), 0) // CAP
    column = lax.broadcasted_iota(jnp.int32, (slots, 128), 1)
    to_high = (slot_row == column).astype(jnp.bfloat16)
    to_low = (slot_row + LO == column).astype(jnp.bfloat16)
    to_live = (slot_row + LIVE == column).astype(jnp.bfloat16)
    alive = jnp.where(here, live, 0.0).astype(jnp.bfloat16)
    meta = (
        jnp.dot(high, to_high, preferred_element_type=jnp.float32)
        + jnp.dot(low, to_low, preferred_element_type=jnp.float32)
        + jnp.dot(alive, to_live, preferred_element_type=jnp.float32)
    )
    for d in range(band_count):
        rows = slice(d * CAP, (d + 1) * CAP)
        message = jnp.concatenate([vis[rows], coord[rows], meta], axis=1).astype(jnp.bfloat16)
        flipped = band_count - 1 - d
        out_ref[jnp.where(below, order.index((d, 0)), order.index((d, 1)))] = message
        out_ref[jnp.where(below, order.index((flipped, 1)), order.index((flipped, 0)))] = message


def square(z):
    re, im = z
    return re * re - im * im, 2.0 * (re * im)


def times(z, w):
    return z[0] * w[0] - z[1] * w[1], z[0] * w[1] + z[1] * w[0]


def unit_phasor(cycles):
    half = (cycles - jnp.round(cycles)) * PI
    x = half * half
    sine = jnp.full_like(x, SIN_TERMS[-1])
    for term in SIN_TERMS[-2::-1]:
        sine = sine * x + term
    cosine = jnp.full_like(x, COS_TERMS[-1])
    for term in COS_TERMS[-2::-1]:
        cosine = cosine * x + term
    sine = sine * half
    return 1.0 - 2.0 * (sine * sine), 2.0 * (sine * cosine)


def turn_table(rows, column, length):
    row = lax.broadcasted_iota(jnp.int32, column.shape, 0)

    def turns(factor):
        return unit_phasor(((factor * column) & (length - 1)).astype(jnp.float32) * (1.0 / length))

    parts = [turns(row)]
    step = turns(jnp.full_like(row, 8))
    for _ in range(rows // 8 - 1):
        parts.append(times(parts[-1], step))
    return tuple(jnp.concatenate([z[i] for z in parts], axis=0) for i in range(2))


def fill_tables(outer_ref, inner_ref, twist_ref):
    column = lax.broadcasted_iota(jnp.int32, (8, 128), 1)
    column_in = column & (N2 - 1)
    outer = turn_table(N1, column, N1)
    left = lax.broadcasted_iota(jnp.int32, (N2, 128), 1) < N2
    inner = [
        jnp.concatenate([jnp.where(left, z, 0.0), jnp.where(left, 0.0, z)], axis=0)
        for z in turn_table(N2, column_in, N2)
    ]
    for ref, (cosine, sine) in ((outer_ref, outer), (inner_ref, inner)):
        cosine, sine = cosine.astype(jnp.bfloat16), sine.astype(jnp.bfloat16)
        ref[:N1, :128] = cosine
        ref[:N1, 128:] = sine
        ref[N1:, :128] = -sine
        ref[N1:, 128:] = cosine
    scale = 1.0 / math.sqrt(G * K)
    twist = turn_table(N1, column_in, G)
    twist_ref[0] = twist[0] * scale
    twist_ref[1] = twist[1] * -scale


def grid_kernel(
    band_count,
    group_count,
    recv_ref,
    out_ref,
    outer_ref,
    inner_ref,
    twist_ref,
    offset_vmem,
    offset_smem,
    data_ref,
    tab_re,
    tab_im,
    eight_re,
    eight_im,
    last_ref,
    cells_ref,
    ends_ref,
    lines_ref,
    grid_ref,
    rows_ref,
    offset_sem,
    out_sem,
):
    below = in_low_half(group_count)
    band = lax.axis_index("band")

    slots = 2 * band_count * CAP
    flat = recv_ref[...].astype(jnp.float32).reshape(slots, ROW).astype(jnp.bfloat16)
    pick_row = lax.broadcasted_iota(jnp.int32, (8, 128), 0)
    pick_col = lax.broadcasted_iota(jnp.int32, (8, 128), 1)
    flipped = band_count - 1 - band
    wanted = jnp.full((8, 128), -1, jnp.int32)
    for i, at in enumerate((0, LO, LIVE)):
        wanted = jnp.where(pick_row == i, band + at, wanted)
        wanted = jnp.where(pick_row == i + 3, flipped + at, wanted)
    picked = dot_last((pick_col == wanted).astype(jnp.bfloat16), flat[:, DATA:])
    slot = lax.broadcasted_iota(jnp.int32, (1, slots), 1)
    from_low = jnp.zeros((1, slots), jnp.int32)
    for at, (_, half) in enumerate(exchange_order(band_count)):
        if half == 0:
            from_low = jnp.where(slot // CAP == at, 1, from_low)
    mine = from_low == below.astype(jnp.int32)
    high, low, live = (jnp.where(mine, picked[i : i + 1], picked[i + 3 : i + 4]) for i in range(3))
    offsets = (high * 128.0 + low).astype(jnp.int32)
    offsets = jnp.where(mine, offsets, (G - S) - offsets)

    live_own = jnp.where(mine, live, 0.0)
    live_mirror = live - live_own
    nothing = jnp.zeros((6, slots), jnp.float32)
    kinds = jnp.concatenate([live_own, live_mirror, nothing], axis=0).astype(jnp.bfloat16)
    earlier = (
        lax.broadcasted_iota(jnp.int32, (slots, slots), 0)
        < lax.broadcasted_iota(jnp.int32, (slots, slots), 1)
    ).astype(jnp.bfloat16)
    before = jnp.dot(kinds, earlier, preferred_element_type=jnp.float32)
    own_groups, mirror_groups = (
        jnp.floor((jnp.sum(z, axis=1, keepdims=True) + (CAP - 1)) * (1.0 / CAP))
        for z in (live_own, live_mirror)
    )
    position = jnp.where(mine, before[0:1], before[1:2] + CAP * own_groups)
    position = jnp.where(live > 0.5, position, -1.0).astype(jnp.int32)
    moves = (
        lax.broadcasted_iota(jnp.int32, (slots, slots), 0) == position
    ).astype(jnp.bfloat16)
    data_ref[...] = jnp.dot(moves, flat[:, :DATA], preferred_element_type=jnp.float32)
    parts = jnp.concatenate(
        [(offsets >> 7).astype(jnp.float32), (offsets & 127).astype(jnp.float32), nothing], axis=0
    )
    moved = dot_last(parts.astype(jnp.bfloat16), moves)
    offset_vmem[...] = jnp.concatenate(
        [
            moved[0:1] * 128.0 + moved[1:2],
            jnp.broadcast_to(own_groups, (1, slots)),
            jnp.broadcast_to(own_groups + mirror_groups, (1, slots)),
            jnp.zeros((5, slots), jnp.float32),
        ],
        axis=0,
    ).astype(jnp.int32)
    to_smem = pltpu.make_async_copy(offset_vmem, offset_smem, offset_sem)
    to_smem.start()

    def clear(step, _):
        rows = pl.ds(pl.multiple_of(step * 24, 24), 24)
        for block in range(S // 8):
            grid_ref[block, rows, :] = jnp.zeros((24, 128), jnp.float32)
        return 0

    lax.fori_loop(0, grid_ref.shape[1] // 24, clear, 0)

    lane = lax.broadcasted_iota(jnp.int32, (8, 128), 1)
    first_half = lane < N2
    lane_in = lane & (N2 - 1)
    turn_sign = jnp.where(lax.broadcasted_iota(jnp.int32, (S, 128), 1) < N2, -1.0, 1.0)
    chunks = 2 * K // 128

    def add_cells(uppers, lowers, start, offset):
        row = (offset >> 6) * STEP
        shift = offset & (N2 - 1)
        near, far = (shift + 128 - start) & 127, (shift + N2 - start) & 127
        stays = (lane_in >= shift) & (lane_in < shift + S)
        wraps = lane_in < shift - (N2 - S)
        for block in range(HALF // 8):
            upper = uppers[block * 8 : block * 8 + 8]
            lower = lowers[block * 8 : block * 8 + 8]
            even = jnp.where(first_half, pltpu.roll(upper, near, 1), pltpu.roll(lower, far, 1))
            odd = jnp.where(first_half, pltpu.roll(upper, far, 1), pltpu.roll(lower, near, 1))
            for part, here, over in ((0, even, odd), (1, odd, even)):
                for at, piece in ((row, jnp.where(stays, here, 0.0)), (row + STEP, jnp.where(wraps, over, 0.0))):
                    rows = pl.ds(at, 8)
                    grid_ref[part * (HALF // 8) + block, rows, :] += piece

    def make_tables(group, mirrored):
        block = data_ref[pl.ds(pl.multiple_of(group * CAP, CAP), CAP), :]
        flip = jnp.where(mirrored == 1, -1.0, 1.0)
        vis = (block[:, 0:K], block[:, K : 2 * K] * flip)
        e1 = unit_phasor(block[:, 2 * K : 4 * K] * (1.0 / S))
        e2 = square(e1)
        e4 = square(e2)
        cc, ss, cs, sc = e4[0] * e1[0], e4[1] * e1[1], e4[0] * e1[1], e4[1] * e1[0]
        e3, e5 = (cc + ss, sc - cs), (cc - ss, sc + cs)
        e8 = square(e4)
        edge = tuple(jnp.where(mirrored == 1, z, one) for z, one in zip(e8, (1.0, 0.0)))
        for b, e in enumerate((edge, e1, e2, e3, e4, e5, square(e3), times(e4, e3))):
            at = 7 * mirrored if b == 0 else b - mirrored
            weighted = times(vis, (e[0][:, :K], e[1][:, :K]))
            for tab, z, y in ((tab_re, weighted[0], e[0][:, K:]), (tab_im, weighted[1], e[1][:, K:])):
                for q in range(chunks):
                    if q < chunks // 2:
                        tab[pl.ds(q * STEP * CAP + at, CAP, stride=STEP), :] = z[:, q * 128 : (q + 1) * 128]
                    elif b > 0:
                        column = (q - chunks // 2) * 128
                        tab[pl.ds(q * STEP * CAP + b, CAP, stride=STEP), :] = y[:, column : column + 128]
        eight_re[...] = e8[0]
        eight_im[...] = e8[1]
        last = square((e8[0][:, K:], e8[1][:, K:]))
        last_ref[...] = jnp.concatenate(last, axis=0).astype(jnp.bfloat16)

    def multiply():
        products = []
        for first in range(0, CAP, GROUP):
            left, real, imag = [], [], []
            for c in range(first, first + GROUP):
                base = tuple(
                    jnp.concatenate(
                        [tab[(q * CAP + c) * STEP : (q * CAP + c) * STEP + 8, :] for q in range(chunks)],
                        axis=1,
                    )
                    for tab in (tab_re, tab_im)
                )
                c8 = jnp.broadcast_to(eight_re[c : c + 1, :], (8, 2 * K))
                s8 = jnp.broadcast_to(eight_im[c : c + 1, :], (8, 2 * K))
                cc, ss, cs, sc = base[0] * c8, base[1] * s8, base[0] * s8, base[1] * c8
                up = (cc - ss, sc + cs)
                up_y = tuple(z[:, K:] for z in up)
                left += [
                    jnp.concatenate([z[:, K:], y], axis=0).astype(jnp.bfloat16) for z, y in zip(base, up_y)
                ]
                base, up, c8, s8 = (
                    tuple(z[:, :K] for z in base),
                    tuple(z[:, :K] for z in up),
                    c8[:, :K],
                    s8[:, :K],
                )
                down = (cc[:, :K] + ss[:, :K], sc[:, :K] - cs[:, :K])
                down2 = (down[0] * c8 + down[1] * s8, down[1] * c8 - down[0] * s8)
                order = (down2, down, base, up)
                real.append(jnp.concatenate([z[0] for z in order], axis=0).astype(jnp.bfloat16))
                imag.append(jnp.concatenate([z[1] for z in order], axis=0).astype(jnp.bfloat16))
            left.append(last_ref[...])
            right = []
            for c in range(0, GROUP, 2):
                right += real[c : c + 2] + imag[c : c + 2]
            cells = dot_last(jnp.concatenate(left, axis=0), jnp.concatenate(right, axis=0))
            products.append(cells)
        return products

    def keep(products):
        for c in range(CAP):
            row, tile = c % GROUP * S, c % GROUP // 2 * 128
            cells_ref[c * S : (c + 1) * S, :] = products[c // GROUP][row : row + S, tile : tile + 128]
        for i, product in enumerate(products):
            for tile in range(GROUP // 2):
                at = (i * (GROUP // 2) + tile) * 2 * CAP
                ends_ref[at : at + 2 * CAP, :] = product[GROUP * S :, tile * 128 : (tile + 1) * 128]

    def both_signs(by_cos, by_sin):
        by_sin = turn_sign[: by_sin.shape[0]] * pltpu.roll(by_sin, N2, 1)
        return by_cos + by_sin, by_cos - by_sin

    def add_group(group):
        mirrored = (group >= first_mirrored).astype(jnp.int32)
        for c in range(CAP):
            at = c // 2 * 2 * CAP
            if c % 2 == 0:
                end_right, end_left = both_signs(
                    ends_ref[at : at + CAP, :], ends_ref[at + CAP : at + 2 * CAP, :]
                )
            right, left = both_signs(
                cells_ref[c * S : c * S + HALF, :], cells_ref[c * S + HALF : (c + 1) * S, :]
            )
            line = c * 2 * S
            lines_ref[line : line + HALF, :] = right
            lines_ref[line + HALF : line + HALF + 1, :] = end_right[c : c + 1]
            lines_ref[line + S : line + S + HALF, :] = left
            lines_ref[line + S - 1 : line + S, :] = left[HALF - 1 :]
            lines_ref[line + S : line + S + 1, :] = jnp.where(mirrored == 1, left[0:1], end_left[c : c + 1])
            add_cells(
                lines_ref[pl.ds(line + S - mirrored, HALF), :],
                lines_ref[pl.ds(line + mirrored, HALF), :],
                c % 2 * S,
                offset_smem[0, group * CAP + c],
            )

    for tab, first in ((tab_re, 1.0), (tab_im, 0.0)):
        for q in range(chunks // 2, chunks):
            tab[pl.ds(q * STEP * CAP, CAP, stride=STEP), :] = jnp.full((CAP, 128), first, jnp.float32)
    make_tables(0, jnp.int32(0))
    fill_tables(outer_ref, inner_ref, twist_ref)
    keep(multiply())
    to_smem.wait()
    first_mirrored, groups = offset_smem[1, 0], offset_smem[2, 0]

    def tables_of(group):
        group = jnp.minimum(group, groups - 1)
        make_tables(group, (group >= first_mirrored).astype(jnp.int32))

    tables_of(1)

    def turn(group, _):
        products = multiply()
        add_group(group - 1)
        keep(products)
        tables_of(group + 1)
        return 0

    lax.fori_loop(1, groups, turn, 0)
    add_group(groups - 1)

    def out_copy(part, group):
        rows = pl.ds(group * 8 * N2, 8 * N2)
        return pltpu.make_async_copy(
            rows_ref.at[part, rows, :], out_ref.at[part, rows, :], out_sem.at[part, group]
        )

    twist_re, twist_im = twist_ref[0], twist_ref[1]
    for pair in range(HALF // 2):
        lines = (2 * pair, 2 * pair + 1)
        field = jnp.concatenate(
            [
                jnp.concatenate(
                    [
                        grid_ref[
                            part * (HALF // 8) + y // 8, pl.ds(y % 8, N1, stride=STEP), :
                        ].astype(jnp.bfloat16)
                        for y in lines
                    ],
                    axis=1,
                )
                for part in range(2)
            ],
            axis=0,
        )
        section = jnp.dot(outer_ref[...], field, preferred_element_type=jnp.float32)
        twisted = []
        for p in range(2):
            re = section[:N1, p * 128 : (p + 1) * 128]
            im = section[N1:, p * 128 : (p + 1) * 128]
            twisted.append(
                jnp.concatenate(
                    [re * twist_re - im * twist_im, re * twist_im + im * twist_re], axis=1
                ).astype(jnp.bfloat16)
            )
        spectrum = dot_last(inner_ref[...], jnp.concatenate(twisted, axis=0))
        for part in range(2):
            for half in range(2):
                for p, y in enumerate(lines):
                    start = (part * 2 + half) * N2
                    line = HALF + y if half else (HALF - y) % HALF
                    rows_ref[part, pl.ds((line // 8) * 8 * N2 + line % 8, N2, stride=8), :] = spectrum[
                        start : start + N2, p * 128 : (p + 1) * 128
                    ]
        done = {7: (2,), 9: (1,), 15: (0, 3)}.get(lines[1], ())
        for part in range(2):
            for group in done:
                out_copy(part, group).start()
    for part in range(2):
        for group in range(S // 8):
            out_copy(part, group).wait()


def shards(visibilities, coordinates, block_index, counts, col_offset):
    band_count = lax.axis_size("band")
    group_count = lax.axis_size("wgrp")
    peers = 2 * band_count
    vmem = pl.BlockSpec(memory_space=pltpu.VMEM)
    hbm = pl.BlockSpec(memory_space=pltpu.HBM)
    inputs = [
        pltpu.with_memory_space_constraint(a, pltpu.HBM)
        for a in (visibilities[0], coordinates[0], block_index, counts, col_offset)
    ]
    message = pl.pallas_call(
        functools.partial(pack_kernel, band_count, group_count),
        out_shape=jax.ShapeDtypeStruct((peers, CAP, ROW), jnp.bfloat16),
        in_specs=[pl.BlockSpec(memory_space=pltpu.HBM)] * len(inputs),
        out_specs=vmem,
        scratch_shapes=[pltpu.VMEM(a.shape, a.dtype) for a in inputs]
        + [pltpu.SemaphoreType.DMA((len(inputs),))],
        compiler_params=pltpu.CompilerParams(vmem_limit_bytes=48 * 2**20),
        name="pack_blocks",
    )(*inputs)
    groups = [
        [b * group_count + (q if half == 0 else group_count - 1 - q) for b, half in exchange_order(band_count)]
        for q in range(group_count // 2)
    ]
    received = lax.all_to_all(
        message, ("band", "wgrp"), 0, 0, axis_index_groups=groups, tiled=True
    )
    slots = peers * CAP
    base = pltpu.VMEM((2 * K // 128 * STEP * CAP + 8, 128), jnp.float32)
    step = pltpu.VMEM((CAP, 2 * K), jnp.float32)
    rows = pl.pallas_call(
        functools.partial(grid_kernel, band_count, group_count),
        out_shape=jax.ShapeDtypeStruct((2, S * N2, N1), jnp.float32),
        in_specs=[vmem],
        out_specs=pl.BlockSpec(memory_space=pl.ANY),
        scratch_shapes=[
            pltpu.VMEM((2 * N1, 256), jnp.bfloat16),
            pltpu.VMEM((2 * N1, 256), jnp.bfloat16),
            pltpu.VMEM((2, N1, 128), jnp.float32),
            pltpu.VMEM((8, slots), jnp.int32),
            pltpu.SMEM((8, slots), jnp.int32),
            pltpu.VMEM((slots, DATA), jnp.float32),
            base,
            base,
            step,
            step,
            pltpu.VMEM((2 * CAP, K), jnp.bfloat16),
            pltpu.VMEM((CAP * S, 128), jnp.float32),
            pltpu.VMEM((CAP // 2 * 2 * CAP, 128), jnp.float32),
            pltpu.VMEM((CAP * 2 * S, 128), jnp.float32),
            pltpu.VMEM((S // 8, pl.cdiv((N1 + 2) * STEP, 24) * 24, 128), jnp.float32),
            pltpu.VMEM((2, S * N2 + 8, N1), jnp.float32),
            pltpu.SemaphoreType.DMA(()),
            pltpu.SemaphoreType.DMA((2, S // 8)),
        ],
        compiler_params=pltpu.CompilerParams(vmem_limit_bytes=48 * 2**20),
        name="grid_and_transform",
    )(received)
    lines = rows.reshape(1, 2, S // 8, N2, 8, N1).transpose(0, 1, 2, 4, 3, 5)
    return lines.reshape(1, 2, S, G)


def solution(mesh):
    placed = (
        P("wgrp", "band", None),
        P("wgrp", "band", None),
        P("wgrp", "band"),
        P("wgrp", "band"),
        P("wgrp", "band"),
    )
    return jax.shard_map(
        shards, mesh=mesh, in_specs=placed, out_specs=P("wgrp", None, "band", None), check_vma=False
    )
```

```python
import functools
import math

import jax
import jax.numpy as jnp
from jax import lax
from jax.experimental import pallas as pl
from jax.experimental.pallas import tpu as pltpu
from jax.sharding import PartitionSpec as P

S = 32
G = 8192
K = 256
GROUP = 4
STEP = 9
CAP = 8
HALF = S // 2
N1 = 128
N2 = 64
DATA = 4 * K
ROW = DATA + 128
LIVE = 32
LO = 64
PI = math.pi

SIN_TERMS = (0.99999999572, -0.1666665797, 0.0083330506173, -0.00019809046357, 2.6051662762e-06)
COS_TERMS = (0.99999995325, -0.49999905063, 0.041663578931, -0.0013853666933, 2.3153174156e-05)


def dot_last(left, right):
    return lax.dot_general(
        left, right, (((1,), (1,)), ((), ())), preferred_element_type=jnp.float32
    )


def dot_first(left, right):
    return lax.dot_general(
        left, right, (((0,), (0,)), ((), ())), preferred_element_type=jnp.float32
    )


def exchange_order(band_count):
    first = band_count * 5 // 8
    bands = [first] + [band for band in reversed(range(band_count)) if band != first]
    return [at for band in bands for at in ((band, 1), (band_count - 1 - band, 0))]


def in_low_half(group_count):
    return lax.axis_index("wgrp") < group_count // 2


def pack_kernel(band_count, group_count, *refs):
    sources, out_ref, targets, sems = refs[:5], refs[5], refs[6:11], refs[11]
    copies = [
        pltpu.make_async_copy(source, target, sems.at[i])
        for i, (source, target) in enumerate(zip(sources, targets))
    ]
    for copy in copies:
        copy.start()
    vis_ref, coord_ref, block_ref, count_ref, offset_ref = targets
    below = in_low_half(group_count)
    order = exchange_order(band_count)
    slots = band_count * CAP
    blocks = vis_ref.shape[0]
    for copy in copies:
        copy.wait()
    block_index, count, offsets = block_ref[...], count_ref[...], offset_ref[...]
    lane = lax.broadcasted_iota(jnp.int32, (1, slots), 1)
    list_of = lane // CAP
    within = lane % CAP
    chosen = (
        lax.broadcasted_iota(jnp.int32, (blocks, slots), 0) == block_index
    ).astype(jnp.float32)
    vis = dot_first(chosen.astype(jnp.bfloat16), vis_ref[...])
    coord = dot_first(chosen.astype(jnp.bfloat16), coord_ref[...])
    here = lax.broadcasted_iota(jnp.int32, (CAP, slots), 0) == within
    high = jnp.where(here, (offsets >> 7).astype(jnp.float32), 0.0).astype(jnp.bfloat16)
    low = jnp.where(here, (offsets & 127).astype(jnp.float32), 0.0).astype(jnp.bfloat16)
    slot_row = lax.broadcasted_iota(jnp.int32, (slots, 128), 0) // CAP
    column = lax.broadcasted_iota(jnp.int32, (slots, 128), 1)
    to_high = (slot_row == column).astype(jnp.bfloat16)
    to_low = (slot_row + LO == column).astype(jnp.bfloat16)
    meta = jnp.dot(high, to_high, preferred_element_type=jnp.float32) + jnp.dot(
        low, to_low, preferred_element_type=jnp.float32
    )
    count = count.astype(jnp.float32)
    spread = jnp.concatenate([count, jnp.zeros((1, 128 - band_count), jnp.float32)], axis=1)
    slot_in = lax.broadcasted_iota(jnp.int32, (CAP, 128), 0).astype(jnp.float32)
    meta = meta + (slot_in < pltpu.roll(jnp.broadcast_to(spread, (CAP, 128)), LIVE, 1)).astype(jnp.float32)
    slot_in = slot_in[:, :1]
    for d in range(band_count):
        rows = slice(d * CAP, (d + 1) * CAP)
        shown = jnp.where(slot_in < count[:, d : d + 1], vis[rows], 0.0)
        message = jnp.concatenate([shown, coord[rows], meta], axis=1).astype(jnp.bfloat16)
        flipped = band_count - 1 - d
        out_ref[jnp.where(below, order.index((d, 0)), order.index((d, 1)))] = message
        out_ref[jnp.where(below, order.index((flipped, 1)), order.index((flipped, 0)))] = message


def square(z):
    re, im = z
    return re * re - im * im, 2.0 * (re * im)


def times(z, w):
    return z[0] * w[0] - z[1] * w[1], z[0] * w[1] + z[1] * w[0]


def unit_phasor(cycles):
    half = (cycles - jnp.round(cycles)) * PI
    x = half * half
    sine = jnp.full_like(x, SIN_TERMS[-1])
    for term in SIN_TERMS[-2::-1]:
        sine = sine * x + term
    cosine = jnp.full_like(x, COS_TERMS[-1])
    for term in COS_TERMS[-2::-1]:
        cosine = cosine * x + term
    sine = sine * half
    return 1.0 - 2.0 * (sine * sine), 2.0 * (sine * cosine)


def turn_table(rows, column, length):
    row = lax.broadcasted_iota(jnp.int32, column.shape, 0)

    def turns(factor):
        return unit_phasor(((factor * column) & (length - 1)).astype(jnp.float32) * (1.0 / length))

    parts = [turns(row)]
    step = turns(jnp.full_like(row, 8))
    for _ in range(rows // 8 - 1):
        parts.append(times(parts[-1], step))
    return tuple(jnp.concatenate([z[i] for z in parts], axis=0) for i in range(2))


def fill_tables(outer_ref, inner_ref, twist_ref):
    column = lax.broadcasted_iota(jnp.int32, (8, 128), 1)
    column_in = column & (N2 - 1)
    outer = turn_table(N1, column, N1)
    left = lax.broadcasted_iota(jnp.int32, (N2, 128), 1) < N2
    inner = [
        jnp.concatenate([jnp.where(left, z, 0.0), jnp.where(left, 0.0, z)], axis=0)
        for z in turn_table(N2, column_in, N2)
    ]
    for ref, (cosine, sine) in ((outer_ref, outer), (inner_ref, inner)):
        cosine, sine = cosine.astype(jnp.bfloat16), sine.astype(jnp.bfloat16)
        ref[:N1, :128] = cosine
        ref[:N1, 128:] = sine
        ref[N1:, :128] = -sine
        ref[N1:, 128:] = cosine
    scale = 1.0 / math.sqrt(G * K)
    twist = turn_table(N1, column_in, G)
    twist_ref[0] = twist[0] * scale
    twist_ref[1] = twist[1] * -scale


def grid_kernel(
    band_count,
    group_count,
    recv_ref,
    out_ref,
    outer_ref,
    inner_ref,
    twist_ref,
    offset_vmem,
    offset_smem,
    data_ref,
    tab_re,
    tab_im,
    eight_re,
    eight_im,
    last_ref,
    cells_ref,
    ends_ref,
    lines_ref,
    grid_ref,
    rows_ref,
    offset_sem,
    out_sem,
):
    below = in_low_half(group_count)
    band = lax.axis_index("band")

    slots = 2 * band_count * CAP
    flat = recv_ref[...].astype(jnp.float32).reshape(slots, ROW).astype(jnp.bfloat16)
    pick_row = lax.broadcasted_iota(jnp.int32, (8, 128), 0)
    pick_col = lax.broadcasted_iota(jnp.int32, (8, 128), 1)
    flipped = band_count - 1 - band
    wanted = jnp.full((8, 128), -1, jnp.int32)
    for i, at in enumerate((0, LO, LIVE)):
        wanted = jnp.where(pick_row == i, band + at, wanted)
        wanted = jnp.where(pick_row == i + 3, flipped + at, wanted)
    picked = dot_last((pick_col == wanted).astype(jnp.bfloat16), flat[:, DATA:])
    slot = lax.broadcasted_iota(jnp.int32, (1, slots), 1)
    from_low = jnp.zeros((1, slots), jnp.int32)
    for at, (_, half) in enumerate(exchange_order(band_count)):
        if half == 0:
            from_low = jnp.where(slot // CAP == at, 1, from_low)
    mine = from_low == below.astype(jnp.int32)
    high, low, live = (jnp.where(mine, picked[i : i + 1], picked[i + 3 : i + 4]) for i in range(3))
    offsets = (high * 128.0 + low).astype(jnp.int32)
    offsets = jnp.where(mine, offsets, (G - S) - offsets)

    live_own = jnp.where(mine, live, 0.0)
    live_mirror = live - live_own
    nothing = jnp.zeros((6, slots), jnp.float32)
    kinds = jnp.concatenate([live_own, live_mirror, nothing], axis=0).astype(jnp.bfloat16)
    earlier = (
        lax.broadcasted_iota(jnp.int32, (slots, slots), 0)
        < lax.broadcasted_iota(jnp.int32, (slots, slots), 1)
    ).astype(jnp.bfloat16)
    before = jnp.dot(kinds, earlier, preferred_element_type=jnp.float32)
    own_count, mirror_count = (jnp.sum(z, axis=1, keepdims=True) for z in (live_own, live_mirror))
    position = jnp.where(mine, before[0:1], before[1:2] + own_count)
    position = jnp.where(live > 0.5, position, -1.0).astype(jnp.int32)
    moves = (
        lax.broadcasted_iota(jnp.int32, (slots, slots), 0) == position
    ).astype(jnp.bfloat16)
    data_ref[...] = jnp.dot(moves, flat[:, :DATA], preferred_element_type=jnp.float32)
    parts = jnp.concatenate(
        [(offsets >> 7).astype(jnp.float32), (offsets & 127).astype(jnp.float32), nothing], axis=0
    )
    moved = dot_last(parts.astype(jnp.bfloat16), moves)
    offset_vmem[...] = jnp.concatenate(
        [
            moved[0:1] * 128.0 + moved[1:2],
            jnp.broadcast_to(own_count, (1, slots)),
            jnp.broadcast_to(own_count + mirror_count, (1, slots)),
            jnp.zeros((5, slots), jnp.float32),
        ],
        axis=0,
    ).astype(jnp.int32)
    to_smem = pltpu.make_async_copy(offset_vmem, offset_smem, offset_sem)
    to_smem.start()

    def clear(step, _):
        rows = pl.ds(pl.multiple_of(step * 24, 24), 24)
        for block in range(S // 8):
            grid_ref[block, rows, :] = jnp.zeros((24, 128), jnp.float32)
        return 0

    lax.fori_loop(0, grid_ref.shape[1] // 24, clear, 0)

    lane = lax.broadcasted_iota(jnp.int32, (8, 128), 1)
    first_half = lane < N2
    lane_in = lane & (N2 - 1)
    turn_sign = jnp.where(lax.broadcasted_iota(jnp.int32, (S, 128), 1) < N2, -1.0, 1.0)
    chunks = 2 * K // 128
    slot_in = lax.broadcasted_iota(jnp.int32, (CAP, K), 0)

    def add_cells(uppers, lowers, start, offset):
        row = (offset >> 6) * STEP
        shift = offset & (N2 - 1)
        near, far = (shift + 128 - start) & 127, (shift + N2 - start) & 127
        stays = (lane_in >= shift) & (lane_in < shift + S)
        wraps = lane_in < shift - (N2 - S)
        for block in range(HALF // 8):
            upper = uppers[block * 8 : block * 8 + 8]
            lower = lowers[block * 8 : block * 8 + 8]
            even = jnp.where(first_half, pltpu.roll(upper, near, 1), pltpu.roll(lower, far, 1))
            odd = jnp.where(first_half, pltpu.roll(upper, far, 1), pltpu.roll(lower, near, 1))
            for part, here, over in ((0, even, odd), (1, odd, even)):
                for at, piece in ((row, jnp.where(stays, here, 0.0)), (row + STEP, jnp.where(wraps, over, 0.0))):
                    rows = pl.ds(at, 8)
                    grid_ref[part * (HALF // 8) + block, rows, :] += piece

    def make_tables(group, own_slots):
        block = data_ref[pl.ds(pl.multiple_of(group * CAP, CAP), CAP), :]
        mirrored = slot_in >= own_slots - group * CAP
        vis = (block[:, 0:K], jnp.where(mirrored, -block[:, K : 2 * K], block[:, K : 2 * K]))
        e1 = unit_phasor(block[:, 2 * K : 4 * K] * (1.0 / S))
        e2 = square(e1)
        e4 = square(e2)
        cc, ss, cs, sc = e4[0] * e1[0], e4[1] * e1[1], e4[0] * e1[1], e4[1] * e1[0]
        e3, e5 = (cc + ss, sc - cs), (cc - ss, sc + cs)
        e8 = square(e4)
        one = (jnp.ones_like(e1[0]), jnp.zeros_like(e1[0]))
        steps = (one, e1, e2, e3, e4, e5, square(e3), times(e4, e3), e8)
        for b in range(8):
            x = tuple(jnp.where(mirrored, n[:, :K], z[:, :K]) for z, n in zip(steps[b], steps[b + 1]))
            weighted = times(vis, x)
            for tab, z, y in zip((tab_re, tab_im), weighted, steps[b]):
                for q in range(chunks):
                    piece = z if q < chunks // 2 else y
                    if b > 0 or q < chunks // 2:
                        tab[pl.ds(q * STEP * CAP + b, CAP, stride=STEP), :] = piece[:, q * 128 : (q + 1) * 128]
        eight_re[...] = e8[0]
        eight_im[...] = e8[1]
        last = square((e8[0][:, K:], e8[1][:, K:]))
        last_ref[...] = jnp.concatenate(last, axis=0).astype(jnp.bfloat16)

    def multiply():
        products = []
        for first in range(0, CAP, GROUP):
            left, real, imag = [], [], []
            for c in range(first, first + GROUP):
                base = tuple(
                    jnp.concatenate(
                        [tab[(q * CAP + c) * STEP : (q * CAP + c) * STEP + 8, :] for q in range(chunks)],
                        axis=1,
                    )
                    for tab in (tab_re, tab_im)
                )
                c8 = jnp.broadcast_to(eight_re[c : c + 1, :], (8, 2 * K))
                s8 = jnp.broadcast_to(eight_im[c : c + 1, :], (8, 2 * K))
                cc, ss, cs, sc = base[0] * c8, base[1] * s8, base[0] * s8, base[1] * c8
                up = (cc - ss, sc + cs)
                up_y = tuple(z[:, K:] for z in up)
                left += [
                    jnp.concatenate([z[:, K:], y], axis=0).astype(jnp.bfloat16) for z, y in zip(base, up_y)
                ]
                base, up, c8, s8 = (
                    tuple(z[:, :K] for z in base),
                    tuple(z[:, :K] for z in up),
                    c8[:, :K],
                    s8[:, :K],
                )
                down = (cc[:, :K] + ss[:, :K], sc[:, :K] - cs[:, :K])
                down2 = (down[0] * c8 + down[1] * s8, down[1] * c8 - down[0] * s8)
                order = (down2, down, base, up)
                real.append(jnp.concatenate([z[0] for z in order], axis=0).astype(jnp.bfloat16))
                imag.append(jnp.concatenate([z[1] for z in order], axis=0).astype(jnp.bfloat16))
            left.append(last_ref[...])
            right = []
            for c in range(0, GROUP, 2):
                right += real[c : c + 2] + imag[c : c + 2]
            cells = dot_last(jnp.concatenate(left, axis=0), jnp.concatenate(right, axis=0))
            products.append(cells)
        return products

    def keep(products):
        for c in range(CAP):
            row, tile = c % GROUP * S, c % GROUP // 2 * 128
            cells_ref[c * S : (c + 1) * S, :] = products[c // GROUP][row : row + S, tile : tile + 128]
        for i, product in enumerate(products):
            for tile in range(GROUP // 2):
                at = (i * (GROUP // 2) + tile) * 2 * CAP
                ends_ref[at : at + 2 * CAP, :] = product[GROUP * S :, tile * 128 : (tile + 1) * 128]

    def both_signs(by_cos, by_sin):
        by_sin = turn_sign[: by_sin.shape[0]] * pltpu.roll(by_sin, N2, 1)
        return by_cos + by_sin, by_cos - by_sin

    def add_group(group):
        for c in range(CAP):
            mirrored = (group * CAP + c >= own_slots).astype(jnp.int32)
            at = c // 2 * 2 * CAP
            if c % 2 == 0:
                end_right, end_left = both_signs(
                    ends_ref[at : at + CAP, :], ends_ref[at + CAP : at + 2 * CAP, :]
                )
            right, left = both_signs(
                cells_ref[c * S : c * S + HALF, :], cells_ref[c * S + HALF : (c + 1) * S, :]
            )
            line = c * 2 * S
            lines_ref[line : line + HALF, :] = right
            lines_ref[line + HALF : line + HALF + 1, :] = end_right[c : c + 1]
            lines_ref[line + S : line + S + HALF, :] = left
            lines_ref[line + S - 1 : line + S, :] = left[HALF - 1 :]
            lines_ref[line + S : line + S + 1, :] = jnp.where(mirrored == 1, left[0:1], end_left[c : c + 1])
            add_cells(
                lines_ref[pl.ds(line + S - mirrored, HALF), :],
                lines_ref[pl.ds(line + mirrored, HALF), :],
                c % 2 * S,
                offset_smem[0, group * CAP + c],
            )

    for tab, first in ((tab_re, 1.0), (tab_im, 0.0)):
        for q in range(chunks // 2, chunks):
            tab[pl.ds(q * STEP * CAP, CAP, stride=STEP), :] = jnp.full((CAP, 128), first, jnp.float32)
    make_tables(0, jnp.int32(CAP))
    fill_tables(outer_ref, inner_ref, twist_ref)
    keep(multiply())
    to_smem.wait()
    own_slots, groups = offset_smem[1, 0], pl.cdiv(offset_smem[2, 0], CAP)

    def tables_of(group):
        make_tables(jnp.minimum(group, groups - 1), own_slots)

    tables_of(1)

    def turn(group, _):
        products = multiply()
        add_group(group - 1)
        keep(products)
        tables_of(group + 1)
        return 0

    lax.fori_loop(1, groups, turn, 0)
    add_group(groups - 1)

    def out_copy(part, group):
        rows = pl.ds(group * 8 * N2, 8 * N2)
        return pltpu.make_async_copy(
            rows_ref.at[part, rows, :], out_ref.at[part, rows, :], out_sem.at[part, group]
        )

    twist_re, twist_im = twist_ref[0], twist_ref[1]
    for pair in range(HALF // 2):
        lines = (2 * pair, 2 * pair + 1)
        field = jnp.concatenate(
            [
                jnp.concatenate(
                    [
                        grid_ref[
                            part * (HALF // 8) + y // 8, pl.ds(y % 8, N1, stride=STEP), :
                        ].astype(jnp.bfloat16)
                        for y in lines
                    ],
                    axis=1,
                )
                for part in range(2)
            ],
            axis=0,
        )
        section = jnp.dot(outer_ref[...], field, preferred_element_type=jnp.float32)
        twisted = []
        for p in range(2):
            re = section[:N1, p * 128 : (p + 1) * 128]
            im = section[N1:, p * 128 : (p + 1) * 128]
            twisted.append(
                jnp.concatenate(
                    [re * twist_re - im * twist_im, re * twist_im + im * twist_re], axis=1
                ).astype(jnp.bfloat16)
            )
        spectrum = dot_last(inner_ref[...], jnp.concatenate(twisted, axis=0))
        for part in range(2):
            for half in range(2):
                for p, y in enumerate(lines):
                    start = (part * 2 + half) * N2
                    line = HALF + y if half else (HALF - y) % HALF
                    rows_ref[part, pl.ds((line // 8) * 8 * N2 + line % 8, N2, stride=8), :] = spectrum[
                        start : start + N2, p * 128 : (p + 1) * 128
                    ]
        done = {7: (2,), 9: (1,), 15: (0, 3)}.get(lines[1], ())
        for part in range(2):
            for group in done:
                out_copy(part, group).start()
    for part in range(2):
        for group in range(S // 8):
            out_copy(part, group).wait()


def shards(visibilities, coordinates, block_index, counts, col_offset):
    band_count = lax.axis_size("band")
    group_count = lax.axis_size("wgrp")
    peers = 2 * band_count
    vmem = pl.BlockSpec(memory_space=pltpu.VMEM)
    hbm = pl.BlockSpec(memory_space=pltpu.HBM)
    inputs = [
        pltpu.with_memory_space_constraint(a, pltpu.HBM)
        for a in (visibilities[0], coordinates[0], block_index, counts, col_offset)
    ]
    message = pl.pallas_call(
        functools.partial(pack_kernel, band_count, group_count),
        out_shape=jax.ShapeDtypeStruct((peers, CAP, ROW), jnp.bfloat16),
        in_specs=[pl.BlockSpec(memory_space=pltpu.HBM)] * len(inputs),
        out_specs=vmem,
        scratch_shapes=[pltpu.VMEM(a.shape, a.dtype) for a in inputs]
        + [pltpu.SemaphoreType.DMA((len(inputs),))],
        compiler_params=pltpu.CompilerParams(vmem_limit_bytes=48 * 2**20),
        name="pack_blocks",
    )(*inputs)
    groups = [
        [b * group_count + (q if half == 0 else group_count - 1 - q) for b, half in exchange_order(band_count)]
        for q in range(group_count // 2)
    ]
    received = lax.all_to_all(
        message, ("band", "wgrp"), 0, 0, axis_index_groups=groups, tiled=True
    )
    slots = peers * CAP
    base = pltpu.VMEM((2 * K // 128 * STEP * CAP + 8, 128), jnp.float32)
    step = pltpu.VMEM((CAP, 2 * K), jnp.float32)
    rows = pl.pallas_call(
        functools.partial(grid_kernel, band_count, group_count),
        out_shape=jax.ShapeDtypeStruct((2, S * N2, N1), jnp.float32),
        in_specs=[vmem],
        out_specs=pl.BlockSpec(memory_space=pl.ANY),
        scratch_shapes=[
            pltpu.VMEM((2 * N1, 256), jnp.bfloat16),
            pltpu.VMEM((2 * N1, 256), jnp.bfloat16),
            pltpu.VMEM((2, N1, 128), jnp.float32),
            pltpu.VMEM((8, slots), jnp.int32),
            pltpu.SMEM((8, slots), jnp.int32),
            pltpu.VMEM((slots, DATA), jnp.float32),
            base,
            base,
            step,
            step,
            pltpu.VMEM((2 * CAP, K), jnp.bfloat16),
            pltpu.VMEM((CAP * S, 128), jnp.float32),
            pltpu.VMEM((CAP // 2 * 2 * CAP, 128), jnp.float32),
            pltpu.VMEM((CAP * 2 * S, 128), jnp.float32),
            pltpu.VMEM((S // 8, pl.cdiv((N1 + 2) * STEP, 24) * 24, 128), jnp.float32),
            pltpu.VMEM((2, S * N2 + 8, N1), jnp.float32),
            pltpu.SemaphoreType.DMA(()),
            pltpu.SemaphoreType.DMA((2, S // 8)),
        ],
        compiler_params=pltpu.CompilerParams(vmem_limit_bytes=48 * 2**20),
        name="grid_and_transform",
    )(received)
    lines = rows.reshape(1, 2, S // 8, N2, 8, N1).transpose(0, 1, 2, 4, 3, 5)
    return lines.reshape(1, 2, S, G)


def solution(mesh):
    placed = (
        P("wgrp", "band", None),
        P("wgrp", "band", None),
        P("wgrp", "band"),
        P("wgrp", "band"),
        P("wgrp", "band"),
    )
    return jax.shard_map(
        shards, mesh=mesh, in_specs=placed, out_specs=P("wgrp", None, "band", None), check_vma=False
    )
```

```python
import functools
import math

import jax
import jax.numpy as jnp
from jax import lax
from jax.experimental import pallas as pl
from jax.experimental.pallas import tpu as pltpu
from jax.sharding import PartitionSpec as P

S = 32
G = 8192
K = 256
GROUP = 4
STEP = 9
CAP = 8
HALF = S // 2
N1 = 128
N2 = 64
DATA = 4 * K
ROW = DATA + 128
LIVE = 32
LO = 64
PI = math.pi

SIN_TERMS = (0.99999999572, -0.1666665797, 0.0083330506173, -0.00019809046357, 2.6051662762e-06)
COS_TERMS = (0.99999995325, -0.49999905063, 0.041663578931, -0.0013853666933, 2.3153174156e-05)


def dot_last(left, right):
    return lax.dot_general(
        left, right, (((1,), (1,)), ((), ())), preferred_element_type=jnp.float32
    )


def dot_first(left, right):
    return lax.dot_general(
        left, right, (((0,), (0,)), ((), ())), preferred_element_type=jnp.float32
    )


def exchange_order(band_count):
    middle = band_count * 5 // 8
    quarter = band_count // 4
    ends = [band for z in (3, 0, 1, 2) for band in reversed(range(z * quarter, (z + 1) * quarter))]
    bands = [middle] + [band for band in ends if band != middle]
    return [at for band in bands for at in ((band, 1), (band, 0))]


def in_low_half(group_count):
    return lax.axis_index("wgrp") < group_count // 2


def pack_kernel(band_count, group_count, *refs):
    sources, out_ref, targets, sems = refs[:5], refs[5], refs[6:11], refs[11]
    copies = [
        pltpu.make_async_copy(source, target, sems.at[i])
        for i, (source, target) in enumerate(zip(sources, targets))
    ]
    for copy in copies:
        copy.start()
    vis_ref, coord_ref, block_ref, count_ref, offset_ref = targets
    below = in_low_half(group_count)
    order = exchange_order(band_count)
    slots = band_count * CAP
    blocks = vis_ref.shape[0]
    for copy in copies:
        copy.wait()
    block_index, count, offsets = block_ref[...], count_ref[...], offset_ref[...]
    lane = lax.broadcasted_iota(jnp.int32, (1, slots), 1)
    list_of = lane // CAP
    within = lane % CAP
    chosen = (
        lax.broadcasted_iota(jnp.int32, (blocks, slots), 0) == block_index
    ).astype(jnp.float32)
    vis = dot_first(chosen.astype(jnp.bfloat16), vis_ref[...])
    coord = dot_first(chosen.astype(jnp.bfloat16), coord_ref[...])
    here = lax.broadcasted_iota(jnp.int32, (CAP, slots), 0) == within
    high = jnp.where(here, (offsets >> 7).astype(jnp.float32), 0.0).astype(jnp.bfloat16)
    low = jnp.where(here, (offsets & 127).astype(jnp.float32), 0.0).astype(jnp.bfloat16)
    slot_row = lax.broadcasted_iota(jnp.int32, (slots, 128), 0) // CAP
    column = lax.broadcasted_iota(jnp.int32, (slots, 128), 1)
    to_high = (slot_row == column).astype(jnp.bfloat16)
    to_low = (slot_row + LO == column).astype(jnp.bfloat16)
    meta = jnp.dot(high, to_high, preferred_element_type=jnp.float32) + jnp.dot(
        low, to_low, preferred_element_type=jnp.float32
    )
    count = count.astype(jnp.float32)
    spread = jnp.concatenate([count, jnp.zeros((1, 128 - band_count), jnp.float32)], axis=1)
    slot_in = lax.broadcasted_iota(jnp.int32, (CAP, 128), 0).astype(jnp.float32)
    meta = meta + (slot_in < pltpu.roll(jnp.broadcast_to(spread, (CAP, 128)), LIVE, 1)).astype(jnp.float32)
    slot_in = slot_in[:, :1]
    for d in range(band_count):
        rows = slice(d * CAP, (d + 1) * CAP)
        shown = jnp.where(slot_in < count[:, d : d + 1], vis[rows], 0.0)
        message = jnp.concatenate([shown, coord[rows], meta], axis=1).astype(jnp.bfloat16)
        flipped = band_count - 1 - d
        out_ref[jnp.where(below, order.index((d, 0)), order.index((d, 1)))] = message
        out_ref[jnp.where(below, order.index((flipped, 1)), order.index((flipped, 0)))] = message


def square(z):
    re, im = z
    return re * re - im * im, 2.0 * (re * im)


def times(z, w):
    return z[0] * w[0] - z[1] * w[1], z[0] * w[1] + z[1] * w[0]


def unit_phasor(cycles):
    half = (cycles - jnp.round(cycles)) * PI
    x = half * half
    sine = jnp.full_like(x, SIN_TERMS[-1])
    for term in SIN_TERMS[-2::-1]:
        sine = sine * x + term
    cosine = jnp.full_like(x, COS_TERMS[-1])
    for term in COS_TERMS[-2::-1]:
        cosine = cosine * x + term
    sine = sine * half
    return 1.0 - 2.0 * (sine * sine), 2.0 * (sine * cosine)


def turn_table(rows, column, length):
    row = lax.broadcasted_iota(jnp.int32, column.shape, 0)

    def turns(factor):
        return unit_phasor(((factor * column) & (length - 1)).astype(jnp.float32) * (1.0 / length))

    parts = [turns(row)]
    step = turns(jnp.full_like(row, 8))
    for _ in range(rows // 8 - 1):
        parts.append(times(parts[-1], step))
    return tuple(jnp.concatenate([z[i] for z in parts], axis=0) for i in range(2))


def fill_tables(outer_ref, inner_ref, twist_ref):
    column = lax.broadcasted_iota(jnp.int32, (8, 128), 1)
    column_in = column & (N2 - 1)
    outer = turn_table(N1, column, N1)
    left = lax.broadcasted_iota(jnp.int32, (N2, 128), 1) < N2
    inner = [
        jnp.concatenate([jnp.where(left, z, 0.0), jnp.where(left, 0.0, z)], axis=0)
        for z in turn_table(N2, column_in, N2)
    ]
    for ref, (cosine, sine) in ((outer_ref, outer), (inner_ref, inner)):
        cosine, sine = cosine.astype(jnp.bfloat16), sine.astype(jnp.bfloat16)
        ref[:N1, :128] = cosine
        ref[:N1, 128:] = sine
        ref[N1:, :128] = -sine
        ref[N1:, 128:] = cosine
    scale = 1.0 / math.sqrt(G * K)
    twist = turn_table(N1, column_in, G)
    twist_ref[0] = twist[0] * scale
    twist_ref[1] = twist[1] * -scale


def grid_kernel(
    band_count,
    group_count,
    recv_ref,
    out_ref,
    outer_ref,
    inner_ref,
    twist_ref,
    offset_vmem,
    offset_smem,
    data_ref,
    tab_re,
    tab_im,
    eight_re,
    eight_im,
    last_ref,
    cells_ref,
    ends_ref,
    lines_ref,
    grid_ref,
    rows_ref,
    offset_sem,
    out_sem,
):
    below = in_low_half(group_count)
    band = lax.axis_index("band")

    slots = 2 * band_count * CAP
    flat = recv_ref[...].astype(jnp.float32).reshape(slots, ROW).astype(jnp.bfloat16)
    pick_row = lax.broadcasted_iota(jnp.int32, (8, 128), 0)
    pick_col = lax.broadcasted_iota(jnp.int32, (8, 128), 1)
    flipped = band_count - 1 - band
    wanted = jnp.full((8, 128), -1, jnp.int32)
    for i, at in enumerate((0, LO, LIVE)):
        wanted = jnp.where(pick_row == i, band + at, wanted)
        wanted = jnp.where(pick_row == i + 3, flipped + at, wanted)
    picked = dot_last((pick_col == wanted).astype(jnp.bfloat16), flat[:, DATA:])
    slot = lax.broadcasted_iota(jnp.int32, (1, slots), 1)
    from_low = jnp.zeros((1, slots), jnp.int32)
    for at, (_, half) in enumerate(exchange_order(band_count)):
        if half == 0:
            from_low = jnp.where(slot // CAP == at, 1, from_low)
    mine = from_low == below.astype(jnp.int32)
    high, low, live = (jnp.where(mine, picked[i : i + 1], picked[i + 3 : i + 4]) for i in range(3))
    offsets = (high * 128.0 + low).astype(jnp.int32)
    offsets = jnp.where(mine, offsets, (G - S) - offsets)

    live_own = jnp.where(mine, live, 0.0)
    live_mirror = live - live_own
    nothing = jnp.zeros((6, slots), jnp.float32)
    kinds = jnp.concatenate([live_own, live_mirror, nothing], axis=0).astype(jnp.bfloat16)
    earlier = (
        lax.broadcasted_iota(jnp.int32, (slots, slots), 0)
        < lax.broadcasted_iota(jnp.int32, (slots, slots), 1)
    ).astype(jnp.bfloat16)
    before = jnp.dot(kinds, earlier, preferred_element_type=jnp.float32)
    own_count, mirror_count = (jnp.sum(z, axis=1, keepdims=True) for z in (live_own, live_mirror))
    position = jnp.where(mine, before[0:1], before[1:2] + own_count)
    position = jnp.where(live > 0.5, position, -1.0).astype(jnp.int32)
    moves = (
        lax.broadcasted_iota(jnp.int32, (slots, slots), 0) == position
    ).astype(jnp.bfloat16)
    data_ref[...] = jnp.dot(moves, flat[:, :DATA], preferred_element_type=jnp.float32)
    parts = jnp.concatenate(
        [(offsets >> 7).astype(jnp.float32), (offsets & 127).astype(jnp.float32), nothing], axis=0
    )
    moved = dot_last(parts.astype(jnp.bfloat16), moves)
    offset_vmem[...] = jnp.concatenate(
        [
            moved[0:1] * 128.0 + moved[1:2],
            jnp.broadcast_to(own_count, (1, slots)),
            jnp.broadcast_to(own_count + mirror_count, (1, slots)),
            jnp.zeros((5, slots), jnp.float32),
        ],
        axis=0,
    ).astype(jnp.int32)
    to_smem = pltpu.make_async_copy(offset_vmem, offset_smem, offset_sem)
    to_smem.start()

    def clear(step, _):
        rows = pl.ds(pl.multiple_of(step * 24, 24), 24)
        for block in range(S // 8):
            grid_ref[block, rows, :] = jnp.zeros((24, 128), jnp.float32)
        return 0

    lax.fori_loop(0, grid_ref.shape[1] // 24, clear, 0)

    lane = lax.broadcasted_iota(jnp.int32, (8, 128), 1)
    first_half = lane < N2
    lane_in = lane & (N2 - 1)
    turn_sign = jnp.where(lax.broadcasted_iota(jnp.int32, (S, 128), 1) < N2, -1.0, 1.0)
    chunks = 2 * K // 128
    slot_in = lax.broadcasted_iota(jnp.int32, (CAP, K), 0)

    def add_cells(uppers, lowers, start, offset):
        row = (offset >> 6) * STEP
        shift = offset & (N2 - 1)
        near, far = (shift + 128 - start) & 127, (shift + N2 - start) & 127
        stays = (lane_in >= shift) & (lane_in < shift + S)
        wraps = lane_in < shift - (N2 - S)
        for block in range(HALF // 8):
            upper = uppers[block * 8 : block * 8 + 8]
            lower = lowers[block * 8 : block * 8 + 8]
            even = jnp.where(first_half, pltpu.roll(upper, near, 1), pltpu.roll(lower, far, 1))
            odd = jnp.where(first_half, pltpu.roll(upper, far, 1), pltpu.roll(lower, near, 1))
            for part, here, over in ((0, even, odd), (1, odd, even)):
                for at, piece in ((row, jnp.where(stays, here, 0.0)), (row + STEP, jnp.where(wraps, over, 0.0))):
                    rows = pl.ds(at, 8)
                    grid_ref[part * (HALF // 8) + block, rows, :] += piece

    def make_tables(group, own_slots):
        block = data_ref[pl.ds(pl.multiple_of(group * CAP, CAP), CAP), :]
        mirrored = slot_in >= own_slots - group * CAP
        vis = (block[:, 0:K], jnp.where(mirrored, -block[:, K : 2 * K], block[:, K : 2 * K]))
        e1 = unit_phasor(block[:, 2 * K : 4 * K] * (1.0 / S))
        e2 = square(e1)
        e4 = square(e2)
        cc, ss, cs, sc = e4[0] * e1[0], e4[1] * e1[1], e4[0] * e1[1], e4[1] * e1[0]
        e3, e5 = (cc + ss, sc - cs), (cc - ss, sc + cs)
        e8 = square(e4)
        one = (jnp.ones_like(e1[0]), jnp.zeros_like(e1[0]))
        steps = (one, e1, e2, e3, e4, e5, square(e3), times(e4, e3), e8)
        for b in range(8):
            x = tuple(jnp.where(mirrored, n[:, :K], z[:, :K]) for z, n in zip(steps[b], steps[b + 1]))
            weighted = times(vis, x)
            for tab, z, y in zip((tab_re, tab_im), weighted, steps[b]):
                for q in range(chunks):
                    piece = z if q < chunks // 2 else y
                    if b > 0 or q < chunks // 2:
                        tab[pl.ds(q * STEP * CAP + b, CAP, stride=STEP), :] = piece[:, q * 128 : (q + 1) * 128]
        eight_re[...] = e8[0]
        eight_im[...] = e8[1]
        last = square((e8[0][:, K:], e8[1][:, K:]))
        last_ref[...] = jnp.concatenate(last, axis=0).astype(jnp.bfloat16)

    def multiply():
        products = []
        for first in range(0, CAP, GROUP):
            left, real, imag = [], [], []
            for c in range(first, first + GROUP):
                base = tuple(
                    jnp.concatenate(
                        [tab[(q * CAP + c) * STEP : (q * CAP + c) * STEP + 8, :] for q in range(chunks)],
                        axis=1,
                    )
                    for tab in (tab_re, tab_im)
                )
                c8 = jnp.broadcast_to(eight_re[c : c + 1, :], (8, 2 * K))
                s8 = jnp.broadcast_to(eight_im[c : c + 1, :], (8, 2 * K))
                cc, ss, cs, sc = base[0] * c8, base[1] * s8, base[0] * s8, base[1] * c8
                up = (cc - ss, sc + cs)
                up_y = tuple(z[:, K:] for z in up)
                left += [
                    jnp.concatenate([z[:, K:], y], axis=0).astype(jnp.bfloat16) for z, y in zip(base, up_y)
                ]
                base, up, c8, s8 = (
                    tuple(z[:, :K] for z in base),
                    tuple(z[:, :K] for z in up),
                    c8[:, :K],
                    s8[:, :K],
                )
                down = (cc[:, :K] + ss[:, :K], sc[:, :K] - cs[:, :K])
                down2 = (down[0] * c8 + down[1] * s8, down[1] * c8 - down[0] * s8)
                order = (down2, down, base, up)
                real.append(jnp.concatenate([z[0] for z in order], axis=0).astype(jnp.bfloat16))
                imag.append(jnp.concatenate([z[1] for z in order], axis=0).astype(jnp.bfloat16))
            left.append(last_ref[...])
            right = []
            for c in range(0, GROUP, 2):
                right += real[c : c + 2] + imag[c : c + 2]
            cells = dot_last(jnp.concatenate(left, axis=0), jnp.concatenate(right, axis=0))
            products.append(cells)
        return products

    def keep(products):
        for c in range(CAP):
            row, tile = c % GROUP * S, c % GROUP // 2 * 128
            cells_ref[c * S : (c + 1) * S, :] = products[c // GROUP][row : row + S, tile : tile + 128]
        for i, product in enumerate(products):
            for tile in range(GROUP // 2):
                at = (i * (GROUP // 2) + tile) * 2 * CAP
                ends_ref[at : at + 2 * CAP, :] = product[GROUP * S :, tile * 128 : (tile + 1) * 128]

    def both_signs(by_cos, by_sin):
        by_sin = turn_sign[: by_sin.shape[0]] * pltpu.roll(by_sin, N2, 1)
        return by_cos + by_sin, by_cos - by_sin

    def add_group(group):
        for c in range(CAP):
            mirrored = (group * CAP + c >= own_slots).astype(jnp.int32)
            at = c // 2 * 2 * CAP
            if c % 2 == 0:
                end_right, end_left = both_signs(
                    ends_ref[at : at + CAP, :], ends_ref[at + CAP : at + 2 * CAP, :]
                )
            right, left = both_signs(
                cells_ref[c * S : c * S + HALF, :], cells_ref[c * S + HALF : (c + 1) * S, :]
            )
            line = c * 2 * S
            lines_ref[line : line + HALF, :] = right
            lines_ref[line + HALF : line + HALF + 1, :] = end_right[c : c + 1]
            lines_ref[line + S : line + S + HALF, :] = left
            lines_ref[line + S - 1 : line + S, :] = left[HALF - 1 :]
            lines_ref[line + S : line + S + 1, :] = jnp.where(mirrored == 1, left[0:1], end_left[c : c + 1])
            add_cells(
                lines_ref[pl.ds(line + S - mirrored, HALF), :],
                lines_ref[pl.ds(line + mirrored, HALF), :],
                c % 2 * S,
                offset_smem[0, group * CAP + c],
            )

    for tab, first in ((tab_re, 1.0), (tab_im, 0.0)):
        for q in range(chunks // 2, chunks):
            tab[pl.ds(q * STEP * CAP, CAP, stride=STEP), :] = jnp.full((CAP, 128), first, jnp.float32)
    make_tables(0, jnp.int32(CAP))
    fill_tables(outer_ref, inner_ref, twist_ref)
    keep(multiply())
    to_smem.wait()
    own_slots, groups = offset_smem[1, 0], pl.cdiv(offset_smem[2, 0], CAP)

    def tables_of(group):
        make_tables(jnp.minimum(group, groups - 1), own_slots)

    tables_of(1)

    def turn(group, _):
        products = multiply()
        add_group(group - 1)
        keep(products)
        tables_of(group + 1)
        return 0

    lax.fori_loop(1, groups, turn, 0)
    add_group(groups - 1)

    def out_copy(part, group):
        rows = pl.ds(group * 8 * N2, 8 * N2)
        return pltpu.make_async_copy(
            rows_ref.at[part, rows, :], out_ref.at[part, rows, :], out_sem.at[part, group]
        )

    twist_re, twist_im = twist_ref[0], twist_ref[1]
    for pair in range(HALF // 2):
        lines = (2 * pair, 2 * pair + 1)
        field = jnp.concatenate(
            [
                jnp.concatenate(
                    [
                        grid_ref[
                            part * (HALF // 8) + y // 8, pl.ds(y % 8, N1, stride=STEP), :
                        ].astype(jnp.bfloat16)
                        for y in lines
                    ],
                    axis=1,
                )
                for part in range(2)
            ],
            axis=0,
        )
        section = jnp.dot(outer_ref[...], field, preferred_element_type=jnp.float32)
        twisted = []
        for p in range(2):
            re = section[:N1, p * 128 : (p + 1) * 128]
            im = section[N1:, p * 128 : (p + 1) * 128]
            twisted.append(
                jnp.concatenate(
                    [re * twist_re - im * twist_im, re * twist_im + im * twist_re], axis=1
                ).astype(jnp.bfloat16)
            )
        spectrum = dot_last(inner_ref[...], jnp.concatenate(twisted, axis=0))
        for part in range(2):
            for half in range(2):
                for p, y in enumerate(lines):
                    start = (part * 2 + half) * N2
                    line = HALF + y if half else (HALF - y) % HALF
                    rows_ref[part, pl.ds((line // 8) * 8 * N2 + line % 8, N2, stride=8), :] = spectrum[
                        start : start + N2, p * 128 : (p + 1) * 128
                    ]
        done = {7: (2,), 9: (1,), 15: (0, 3)}.get(lines[1], ())
        for part in range(2):
            for group in done:
                out_copy(part, group).start()
    for part in range(2):
        for group in range(S // 8):
            out_copy(part, group).wait()


def shards(visibilities, coordinates, block_index, counts, col_offset):
    band_count = lax.axis_size("band")
    group_count = lax.axis_size("wgrp")
    peers = 2 * band_count
    vmem = pl.BlockSpec(memory_space=pltpu.VMEM)
    hbm = pl.BlockSpec(memory_space=pltpu.HBM)
    inputs = [
        pltpu.with_memory_space_constraint(a, pltpu.HBM)
        for a in (visibilities[0], coordinates[0], block_index, counts, col_offset)
    ]
    message = pl.pallas_call(
        functools.partial(pack_kernel, band_count, group_count),
        out_shape=jax.ShapeDtypeStruct((peers, CAP, ROW), jnp.bfloat16),
        in_specs=[pl.BlockSpec(memory_space=pltpu.HBM)] * len(inputs),
        out_specs=vmem,
        scratch_shapes=[pltpu.VMEM(a.shape, a.dtype) for a in inputs]
        + [pltpu.SemaphoreType.DMA((len(inputs),))],
        compiler_params=pltpu.CompilerParams(vmem_limit_bytes=48 * 2**20),
        name="pack_blocks",
    )(*inputs)
    groups = [
        [b * group_count + (q if half == 0 else group_count - 1 - q) for b, half in exchange_order(band_count)]
        for q in range(group_count // 2)
    ]
    received = lax.all_to_all(
        message, ("band", "wgrp"), 0, 0, axis_index_groups=groups, tiled=True
    )
    slots = peers * CAP
    base = pltpu.VMEM((2 * K // 128 * STEP * CAP + 8, 128), jnp.float32)
    step = pltpu.VMEM((CAP, 2 * K), jnp.float32)
    rows = pl.pallas_call(
        functools.partial(grid_kernel, band_count, group_count),
        out_shape=jax.ShapeDtypeStruct((2, S * N2, N1), jnp.float32),
        in_specs=[vmem],
        out_specs=pl.BlockSpec(memory_space=pl.ANY),
        scratch_shapes=[
            pltpu.VMEM((2 * N1, 256), jnp.bfloat16),
            pltpu.VMEM((2 * N1, 256), jnp.bfloat16),
            pltpu.VMEM((2, N1, 128), jnp.float32),
            pltpu.VMEM((8, slots), jnp.int32),
            pltpu.SMEM((8, slots), jnp.int32),
            pltpu.VMEM((slots, DATA), jnp.float32),
            base,
            base,
            step,
            step,
            pltpu.VMEM((2 * CAP, K), jnp.bfloat16),
            pltpu.VMEM((CAP * S, 128), jnp.float32),
            pltpu.VMEM((CAP // 2 * 2 * CAP, 128), jnp.float32),
            pltpu.VMEM((CAP * 2 * S, 128), jnp.float32),
            pltpu.VMEM((S // 8, pl.cdiv((N1 + 2) * STEP, 24) * 24, 128), jnp.float32),
            pltpu.VMEM((2, S * N2 + 8, N1), jnp.float32),
            pltpu.SemaphoreType.DMA(()),
            pltpu.SemaphoreType.DMA((2, S // 8)),
        ],
        compiler_params=pltpu.CompilerParams(vmem_limit_bytes=48 * 2**20),
        name="grid_and_transform",
    )(received)
    lines = rows.reshape(1, 2, S // 8, N2, 8, N1).transpose(0, 1, 2, 4, 3, 5)
    return lines.reshape(1, 2, S, G)


def solution(mesh):
    placed = (
        P("wgrp", "band", None),
        P("wgrp", "band", None),
        P("wgrp", "band"),
        P("wgrp", "band"),
        P("wgrp", "band"),
    )
    return jax.shard_map(
        shards, mesh=mesh, in_specs=placed, out_specs=P("wgrp", None, "band", None), check_vma=False
    )
```

```python
import functools
import math

import jax
import jax.numpy as jnp
from jax import lax
from jax.experimental import pallas as pl
from jax.experimental.pallas import tpu as pltpu
from jax.sharding import PartitionSpec as P

S = 32
G = 8192
K = 256
GROUP = 4
STEP = 9
CAP = 8
HALF = S // 2
N1 = 128
N2 = 64
DATA = 4 * K
ROW = DATA + 128
LIVE = 32
LO = 64
PI = math.pi

SIN_TERMS = (0.99999999572, -0.1666665797, 0.0083330506173, -0.00019809046357, 2.6051662762e-06)
COS_TERMS = (0.99999995325, -0.49999905063, 0.041663578931, -0.0013853666933, 2.3153174156e-05)


def dot_last(left, right):
    return lax.dot_general(
        left, right, (((1,), (1,)), ((), ())), preferred_element_type=jnp.float32
    )


def dot_first(left, right):
    return lax.dot_general(
        left, right, (((0,), (0,)), ((), ())), preferred_element_type=jnp.float32
    )


def exchange_order(band_count):
    first = band_count * 5 // 8
    bands = [first] + [band for band in reversed(range(band_count)) if band != first]
    return [at for band in bands for at in ((band, 1), (band_count - 1 - band, 0))]


def in_low_half(group_count):
    return lax.axis_index("wgrp") < group_count // 2


def pack_kernel(band_count, group_count, *refs):
    sources, out_ref, targets, sems = refs[:5], refs[5], refs[6:11], refs[11]
    copies = [
        pltpu.make_async_copy(source, target, sems.at[i])
        for i, (source, target) in enumerate(zip(sources, targets))
    ]
    for copy in copies:
        copy.start()
    vis_ref, coord_ref, block_ref, count_ref, offset_ref = targets
    below = in_low_half(group_count)
    order = exchange_order(band_count)
    slots = band_count * CAP
    blocks = vis_ref.shape[0]
    for copy in copies:
        copy.wait()
    block_index, count, offsets = block_ref[...], count_ref[...], offset_ref[...]
    lane = lax.broadcasted_iota(jnp.int32, (1, slots), 1)
    list_of = lane // CAP
    within = lane % CAP
    chosen = (
        lax.broadcasted_iota(jnp.int32, (blocks, slots), 0) == block_index
    ).astype(jnp.float32)
    vis = dot_first(chosen.astype(jnp.bfloat16), vis_ref[...])
    coord = dot_first(chosen.astype(jnp.bfloat16), coord_ref[...])
    here = lax.broadcasted_iota(jnp.int32, (CAP, slots), 0) == within
    high = jnp.where(here, (offsets >> 7).astype(jnp.float32), 0.0).astype(jnp.bfloat16)
    low = jnp.where(here, (offsets & 127).astype(jnp.float32), 0.0).astype(jnp.bfloat16)
    slot_row = lax.broadcasted_iota(jnp.int32, (slots, 128), 0) // CAP
    column = lax.broadcasted_iota(jnp.int32, (slots, 128), 1)
    to_high = (slot_row == column).astype(jnp.bfloat16)
    to_low = (slot_row + LO == column).astype(jnp.bfloat16)
    meta = jnp.dot(high, to_high, preferred_element_type=jnp.float32) + jnp.dot(
        low, to_low, preferred_element_type=jnp.float32
    )
    count = count.astype(jnp.float32)
    spread = jnp.concatenate([count, jnp.zeros((1, 128 - band_count), jnp.float32)], axis=1)
    slot_in = lax.broadcasted_iota(jnp.int32, (CAP, 128), 0).astype(jnp.float32)
    meta = meta + (slot_in < pltpu.roll(jnp.broadcast_to(spread, (CAP, 128)), LIVE, 1)).astype(jnp.float32)
    slot_in = slot_in[:, :1]
    for d in range(band_count):
        rows = slice(d * CAP, (d + 1) * CAP)
        shown = jnp.where(slot_in < count[:, d : d + 1], vis[rows], 0.0)
        message = jnp.concatenate([shown, coord[rows], meta], axis=1).astype(jnp.bfloat16)
        flipped = band_count - 1 - d
        out_ref[jnp.where(below, order.index((d, 0)), order.index((d, 1)))] = message
        out_ref[jnp.where(below, order.index((flipped, 1)), order.index((flipped, 0)))] = message


def square(z):
    re, im = z
    return re * re - im * im, 2.0 * (re * im)


def times(z, w):
    return z[0] * w[0] - z[1] * w[1], z[0] * w[1] + z[1] * w[0]


def unit_phasor(cycles):
    half = (cycles - jnp.round(cycles)) * PI
    x = half * half
    sine = jnp.full_like(x, SIN_TERMS[-1])
    for term in SIN_TERMS[-2::-1]:
        sine = sine * x + term
    cosine = jnp.full_like(x, COS_TERMS[-1])
    for term in COS_TERMS[-2::-1]:
        cosine = cosine * x + term
    sine = sine * half
    return 1.0 - 2.0 * (sine * sine), 2.0 * (sine * cosine)


def turn_table(rows, column, length):
    row = lax.broadcasted_iota(jnp.int32, column.shape, 0)

    def turns(factor):
        return unit_phasor(((factor * column) & (length - 1)).astype(jnp.float32) * (1.0 / length))

    parts = [turns(row)]
    step = turns(jnp.full_like(row, 8))
    for _ in range(rows // 8 - 1):
        parts.append(times(parts[-1], step))
    return tuple(jnp.concatenate([z[i] for z in parts], axis=0) for i in range(2))


def fill_tables(outer_ref, inner_ref, twist_ref):
    column = lax.broadcasted_iota(jnp.int32, (8, 128), 1)
    column_in = column & (N2 - 1)
    outer = turn_table(N1, column, N1)
    left = lax.broadcasted_iota(jnp.int32, (N2, 128), 1) < N2
    inner = [
        jnp.concatenate([jnp.where(left, z, 0.0), jnp.where(left, 0.0, z)], axis=0)
        for z in turn_table(N2, column_in, N2)
    ]
    for ref, (cosine, sine) in ((outer_ref, outer), (inner_ref, inner)):
        cosine, sine = cosine.astype(jnp.bfloat16), sine.astype(jnp.bfloat16)
        ref[:N1, :128] = cosine
        ref[:N1, 128:] = sine
        ref[N1:, :128] = -sine
        ref[N1:, 128:] = cosine
    scale = 1.0 / math.sqrt(G * K)
    twist = turn_table(N1, column_in, G)
    twist_ref[0] = twist[0] * scale
    twist_ref[1] = twist[1] * -scale


def grid_kernel(
    band_count,
    group_count,
    recv_ref,
    out_ref,
    outer_ref,
    inner_ref,
    twist_ref,
    offset_vmem,
    offset_smem,
    data_ref,
    tab_re,
    tab_im,
    eight_re,
    eight_im,
    last_ref,
    cells_ref,
    ends_ref,
    lines_ref,
    grid_ref,
    rows_ref,
    offset_sem,
    out_sem,
):
    below = in_low_half(group_count)
    band = lax.axis_index("band")

    slots = 2 * band_count * CAP
    flat = recv_ref[...].astype(jnp.float32).reshape(slots, ROW).astype(jnp.bfloat16)
    pick_row = lax.broadcasted_iota(jnp.int32, (8, 128), 0)
    pick_col = lax.broadcasted_iota(jnp.int32, (8, 128), 1)
    flipped = band_count - 1 - band
    wanted = jnp.full((8, 128), -1, jnp.int32)
    for i, at in enumerate((0, LO, LIVE)):
        wanted = jnp.where(pick_row == i, band + at, wanted)
        wanted = jnp.where(pick_row == i + 3, flipped + at, wanted)
    picked = dot_last((pick_col == wanted).astype(jnp.bfloat16), flat[:, DATA:])
    slot = lax.broadcasted_iota(jnp.int32, (1, slots), 1)
    from_low = jnp.zeros((1, slots), jnp.int32)
    for at, (_, half) in enumerate(exchange_order(band_count)):
        if half == 0:
            from_low = jnp.where(slot // CAP == at, 1, from_low)
    mine = from_low == below.astype(jnp.int32)
    high, low, live = (jnp.where(mine, picked[i : i + 1], picked[i + 3 : i + 4]) for i in range(3))
    offsets = (high * 128.0 + low).astype(jnp.int32)
    offsets = jnp.where(mine, offsets, (G - S) - offsets)

    live_own = jnp.where(mine, live, 0.0)
    live_mirror = live - live_own
    nothing = jnp.zeros((6, slots), jnp.float32)
    kinds = jnp.concatenate([live_own, live_mirror, nothing], axis=0).astype(jnp.bfloat16)
    earlier = (
        lax.broadcasted_iota(jnp.int32, (slots, slots), 0)
        < lax.broadcasted_iota(jnp.int32, (slots, slots), 1)
    ).astype(jnp.bfloat16)
    before = jnp.dot(kinds, earlier, preferred_element_type=jnp.float32)
    own_count, mirror_count = (jnp.sum(z, axis=1, keepdims=True) for z in (live_own, live_mirror))
    position = jnp.where(mine, before[0:1], before[1:2] + own_count)
    position = jnp.where(live > 0.5, position, -1.0).astype(jnp.int32)
    moves = (
        lax.broadcasted_iota(jnp.int32, (slots, slots), 0) == position
    ).astype(jnp.bfloat16)
    data_ref[...] = jnp.dot(moves, flat[:, :DATA], preferred_element_type=jnp.float32)
    parts = jnp.concatenate(
        [(offsets >> 7).astype(jnp.float32), (offsets & 127).astype(jnp.float32), nothing], axis=0
    )
    moved = dot_last(parts.astype(jnp.bfloat16), moves)
    offset_vmem[...] = jnp.concatenate(
        [
            moved[0:1] * 128.0 + moved[1:2],
            jnp.broadcast_to(own_count, (1, slots)),
            jnp.broadcast_to(own_count + mirror_count, (1, slots)),
            jnp.zeros((5, slots), jnp.float32),
        ],
        axis=0,
    ).astype(jnp.int32)
    to_smem = pltpu.make_async_copy(offset_vmem, offset_smem, offset_sem)
    to_smem.start()

    def clear(step, _):
        rows = pl.ds(pl.multiple_of(step * 168, 168), 168)
        for block in range(S // 8):
            grid_ref[block, rows, :] = jnp.zeros((168, 128), jnp.float32)
        return 0

    lax.fori_loop(0, grid_ref.shape[1] // 168, clear, 0)

    lane = lax.broadcasted_iota(jnp.int32, (8, 128), 1)
    first_half = lane < N2
    lane_in = lane & (N2 - 1)
    turn_sign = jnp.where(lax.broadcasted_iota(jnp.int32, (S, 128), 1) < N2, -1.0, 1.0)
    chunks = 2 * K // 128
    slot_in = lax.broadcasted_iota(jnp.int32, (CAP, K), 0)

    def add_cells(uppers, lowers, start, offset):
        row = (offset >> 6) * STEP
        shift = offset & (N2 - 1)
        near, far = (shift + 128 - start) & 127, (shift + N2 - start) & 127
        stays = (lane_in >= shift) & (lane_in < shift + S)
        wraps = lane_in < shift - (N2 - S)
        for block in range(HALF // 8):
            upper = uppers[block * 8 : block * 8 + 8]
            lower = lowers[block * 8 : block * 8 + 8]
            even = jnp.where(first_half, pltpu.roll(upper, near, 1), pltpu.roll(lower, far, 1))
            odd = jnp.where(first_half, pltpu.roll(upper, far, 1), pltpu.roll(lower, near, 1))
            for part, here, over in ((0, even, odd), (1, odd, even)):
                for at, piece in ((row, jnp.where(stays, here, 0.0)), (row + STEP, jnp.where(wraps, over, 0.0))):
                    rows = pl.ds(at, 8)
                    grid_ref[part * (HALF // 8) + block, rows, :] += piece

    def make_tables(group, own_slots):
        block = data_ref[pl.ds(pl.multiple_of(group * CAP, CAP), CAP), :]
        mirrored = slot_in >= own_slots - group * CAP
        vis = (block[:, 0:K], jnp.where(mirrored, -block[:, K : 2 * K], block[:, K : 2 * K]))
        e1 = unit_phasor(block[:, 2 * K : 4 * K] * (1.0 / S))
        e2 = square(e1)
        e4 = square(e2)
        cc, ss, cs, sc = e4[0] * e1[0], e4[1] * e1[1], e4[0] * e1[1], e4[1] * e1[0]
        e3, e5 = (cc + ss, sc - cs), (cc - ss, sc + cs)
        e8 = square(e4)
        one = (jnp.ones_like(e1[0]), jnp.zeros_like(e1[0]))
        steps = (one, e1, e2, e3, e4, e5, square(e3), times(e4, e3), e8)
        for b in range(8):
            x = tuple(jnp.where(mirrored, n[:, :K], z[:, :K]) for z, n in zip(steps[b], steps[b + 1]))
            weighted = times(vis, x)
            for tab, z, y in zip((tab_re, tab_im), weighted, steps[b]):
                for q in range(chunks):
                    piece = z if q < chunks // 2 else y
                    if b > 0 or q < chunks // 2:
                        tab[pl.ds(q * STEP * CAP + b, CAP, stride=STEP), :] = piece[:, q * 128 : (q + 1) * 128]
        eight_re[...] = e8[0]
        eight_im[...] = e8[1]
        last = square((e8[0][:, K:], e8[1][:, K:]))
        last_ref[...] = jnp.concatenate(last, axis=0).astype(jnp.bfloat16)

    def multiply():
        products = []
        for first in range(0, CAP, GROUP):
            left, real, imag = [], [], []
            for c in range(first, first + GROUP):
                base = tuple(
                    jnp.concatenate(
                        [tab[(q * CAP + c) * STEP : (q * CAP + c) * STEP + 8, :] for q in range(chunks)],
                        axis=1,
                    )
                    for tab in (tab_re, tab_im)
                )
                c8 = jnp.broadcast_to(eight_re[c : c + 1, :], (8, 2 * K))
                s8 = jnp.broadcast_to(eight_im[c : c + 1, :], (8, 2 * K))
                cc, ss, cs, sc = base[0] * c8, base[1] * s8, base[0] * s8, base[1] * c8
                up = (cc - ss, sc + cs)
                up_y = tuple(z[:, K:] for z in up)
                left += [
                    jnp.concatenate([z[:, K:], y], axis=0).astype(jnp.bfloat16) for z, y in zip(base, up_y)
                ]
                base, up, c8, s8 = (
                    tuple(z[:, :K] for z in base),
                    tuple(z[:, :K] for z in up),
                    c8[:, :K],
                    s8[:, :K],
                )
                down = (cc[:, :K] + ss[:, :K], sc[:, :K] - cs[:, :K])
                down2 = (down[0] * c8 + down[1] * s8, down[1] * c8 - down[0] * s8)
                order = (down2, down, base, up)
                real.append(jnp.concatenate([z[0] for z in order], axis=0).astype(jnp.bfloat16))
                imag.append(jnp.concatenate([z[1] for z in order], axis=0).astype(jnp.bfloat16))
            left.append(last_ref[...])
            right = []
            for c in range(0, GROUP, 2):
                right += real[c : c + 2] + imag[c : c + 2]
            cells = dot_last(jnp.concatenate(left, axis=0), jnp.concatenate(right, axis=0))
            products.append(cells)
        return products

    def keep(products):
        for c in range(CAP):
            row, tile = c % GROUP * S, c % GROUP // 2 * 128
            cells_ref[c * S : (c + 1) * S, :] = products[c // GROUP][row : row + S, tile : tile + 128]
        for i, product in enumerate(products):
            for tile in range(GROUP // 2):
                at = (i * (GROUP // 2) + tile) * 2 * CAP
                ends_ref[at : at + 2 * CAP, :] = product[GROUP * S :, tile * 128 : (tile + 1) * 128]

    def both_signs(by_cos, by_sin):
        by_sin = turn_sign[: by_sin.shape[0]] * pltpu.roll(by_sin, N2, 1)
        return by_cos + by_sin, by_cos - by_sin

    def add_group(group):
        for c in range(CAP):
            mirrored = (group * CAP + c >= own_slots).astype(jnp.int32)
            at = c // 2 * 2 * CAP
            if c % 2 == 0:
                end_right, end_left = both_signs(
                    ends_ref[at : at + CAP, :], ends_ref[at + CAP : at + 2 * CAP, :]
                )
            right, left = both_signs(
                cells_ref[c * S : c * S + HALF, :], cells_ref[c * S + HALF : (c + 1) * S, :]
            )
            line = c * 2 * S
            lines_ref[line : line + HALF, :] = right
            lines_ref[line + HALF : line + HALF + 1, :] = end_right[c : c + 1]
            lines_ref[line + S : line + S + HALF, :] = left
            lines_ref[line + S - 1 : line + S, :] = left[HALF - 1 :]
            lines_ref[line + S : line + S + 1, :] = jnp.where(mirrored == 1, left[0:1], end_left[c : c + 1])
            add_cells(
                lines_ref[pl.ds(line + S - mirrored, HALF), :],
                lines_ref[pl.ds(line + mirrored, HALF), :],
                c % 2 * S,
                offset_smem[0, group * CAP + c],
            )

    for tab, first in ((tab_re, 1.0), (tab_im, 0.0)):
        for q in range(chunks // 2, chunks):
            tab[pl.ds(q * STEP * CAP, CAP, stride=STEP), :] = jnp.full((CAP, 128), first, jnp.float32)
    make_tables(0, jnp.int32(CAP))
    fill_tables(outer_ref, inner_ref, twist_ref)
    keep(multiply())
    to_smem.wait()
    own_slots, groups = offset_smem[1, 0], pl.cdiv(offset_smem[2, 0], CAP)

    def tables_of(group):
        make_tables(jnp.minimum(group, groups - 1), own_slots)

    tables_of(1)

    def turn(group, _):
        products = multiply()
        add_group(group - 1)
        keep(products)
        tables_of(group + 1)
        return 0

    lax.fori_loop(1, groups, turn, 0)
    add_group(groups - 1)

    def out_copy(part, group):
        rows = pl.ds(group * 8 * N2, 8 * N2)
        return pltpu.make_async_copy(
            rows_ref.at[part, rows, :], out_ref.at[part, rows, :], out_sem.at[part, group]
        )

    twist_re, twist_im = twist_ref[0], twist_ref[1]
    for pair in range(HALF // 2):
        lines = (2 * pair, 2 * pair + 1)
        field = jnp.concatenate(
            [
                jnp.concatenate(
                    [
                        grid_ref[
                            part * (HALF // 8) + y // 8, pl.ds(y % 8, N1, stride=STEP), :
                        ].astype(jnp.bfloat16)
                        for y in lines
                    ],
                    axis=1,
                )
                for part in range(2)
            ],
            axis=0,
        )
        section = jnp.dot(outer_ref[...], field, preferred_element_type=jnp.float32)
        twisted = []
        for p in range(2):
            re = section[:N1, p * 128 : (p + 1) * 128]
            im = section[N1:, p * 128 : (p + 1) * 128]
            twisted.append(
                jnp.concatenate(
                    [re * twist_re - im * twist_im, re * twist_im + im * twist_re], axis=1
                ).astype(jnp.bfloat16)
            )
        spectrum = dot_last(inner_ref[...], jnp.concatenate(twisted, axis=0))
        for part in range(2):
            for half in range(2):
                for p, y in enumerate(lines):
                    start = (part * 2 + half) * N2
                    line = HALF + y if half else (HALF - y) % HALF
                    rows_ref[part, pl.ds((line // 8) * 8 * N2 + line % 8, N2, stride=8), :] = spectrum[
                        start : start + N2, p * 128 : (p + 1) * 128
                    ]
        done = {7: (2,), 9: (1,), 15: (0, 3)}.get(lines[1], ())
        for part in range(2):
            for group in done:
                out_copy(part, group).start()
    for part in range(2):
        for group in range(S // 8):
            out_copy(part, group).wait()


def shards(visibilities, coordinates, block_index, counts, col_offset):
    band_count = lax.axis_size("band")
    group_count = lax.axis_size("wgrp")
    peers = 2 * band_count
    vmem = pl.BlockSpec(memory_space=pltpu.VMEM)
    hbm = pl.BlockSpec(memory_space=pltpu.HBM)
    inputs = [
        pltpu.with_memory_space_constraint(a, pltpu.HBM)
        for a in (visibilities[0], coordinates[0], block_index, counts, col_offset)
    ]
    message = pl.pallas_call(
        functools.partial(pack_kernel, band_count, group_count),
        out_shape=jax.ShapeDtypeStruct((peers, CAP, ROW), jnp.bfloat16),
        in_specs=[pl.BlockSpec(memory_space=pltpu.HBM)] * len(inputs),
        out_specs=vmem,
        scratch_shapes=[pltpu.VMEM(a.shape, a.dtype) for a in inputs]
        + [pltpu.SemaphoreType.DMA((len(inputs),))],
        compiler_params=pltpu.CompilerParams(vmem_limit_bytes=48 * 2**20),
        name="pack_blocks",
    )(*inputs)
    groups = [
        [b * group_count + (q if half == 0 else group_count - 1 - q) for b, half in exchange_order(band_count)]
        for q in range(group_count // 2)
    ]
    received = lax.all_to_all(
        message, ("band", "wgrp"), 0, 0, axis_index_groups=groups, tiled=True
    )
    slots = peers * CAP
    base = pltpu.VMEM((2 * K // 128 * STEP * CAP + 8, 128), jnp.float32)
    step = pltpu.VMEM((CAP, 2 * K), jnp.float32)
    rows = pl.pallas_call(
        functools.partial(grid_kernel, band_count, group_count),
        out_shape=jax.ShapeDtypeStruct((2, S * N2, N1), jnp.float32),
        in_specs=[vmem],
        out_specs=pl.BlockSpec(memory_space=pl.ANY),
        scratch_shapes=[
            pltpu.VMEM((2 * N1, 256), jnp.bfloat16),
            pltpu.VMEM((2 * N1, 256), jnp.bfloat16),
            pltpu.VMEM((2, N1, 128), jnp.float32),
            pltpu.VMEM((8, slots), jnp.int32),
            pltpu.SMEM((8, slots), jnp.int32),
            pltpu.VMEM((slots, DATA), jnp.float32),
            base,
            base,
            step,
            step,
            pltpu.VMEM((2 * CAP, K), jnp.bfloat16),
            pltpu.VMEM((CAP * S, 128), jnp.float32),
            pltpu.VMEM((CAP // 2 * 2 * CAP, 128), jnp.float32),
            pltpu.VMEM((CAP * 2 * S, 128), jnp.float32),
            pltpu.VMEM((S // 8, pl.cdiv((N1 + 2) * STEP, 168) * 168, 128), jnp.float32),
            pltpu.VMEM((2, S * N2 + 8, N1), jnp.float32),
            pltpu.SemaphoreType.DMA(()),
            pltpu.SemaphoreType.DMA((2, S // 8)),
        ],
        compiler_params=pltpu.CompilerParams(vmem_limit_bytes=48 * 2**20),
        name="grid_and_transform",
    )(received)
    lines = rows.reshape(1, 2, S // 8, N2, 8, N1).transpose(0, 1, 2, 4, 3, 5)
    return lines.reshape(1, 2, S, G)


def solution(mesh):
    placed = (
        P("wgrp", "band", None),
        P("wgrp", "band", None),
        P("wgrp", "band"),
        P("wgrp", "band"),
        P("wgrp", "band"),
    )
    return jax.shard_map(
        shards, mesh=mesh, in_specs=placed, out_specs=P("wgrp", None, "band", None), check_vma=False
    )
```

```python
import functools
import math

import jax
import jax.numpy as jnp
from jax import lax
from jax.experimental import pallas as pl
from jax.experimental.pallas import tpu as pltpu
from jax.sharding import PartitionSpec as P

S = 32
G = 8192
K = 256
GROUP = 4
STEP = 9
CAP = 8
HALF = S // 2
N1 = 128
N2 = 64
DATA = 4 * K
ROW = DATA + 128
LIVE = 32
LO = 64
PI = math.pi

SIN_TERMS = (0.99999999572, -0.1666665797, 0.0083330506173, -0.00019809046357, 2.6051662762e-06)
COS_TERMS = (0.99999995325, -0.49999905063, 0.041663578931, -0.0013853666933, 2.3153174156e-05)


def dot_last(left, right):
    return lax.dot_general(
        left, right, (((1,), (1,)), ((), ())), preferred_element_type=jnp.float32
    )


def dot_first(left, right):
    return lax.dot_general(
        left, right, (((0,), (0,)), ((), ())), preferred_element_type=jnp.float32
    )


def exchange_order(band_count):
    first = band_count * 5 // 8
    bands = [first] + [band for band in reversed(range(band_count)) if band != first]
    return [at for band in bands for at in ((band, 1), (band_count - 1 - band, 0))]


def in_low_half(group_count):
    return lax.axis_index("wgrp") < group_count // 2


def pack_kernel(band_count, group_count, *refs):
    sources, out_ref, targets, sems = refs[:5], refs[5], refs[6:11], refs[11]
    copies = [
        pltpu.make_async_copy(source, target, sems.at[i])
        for i, (source, target) in enumerate(zip(sources, targets))
    ]
    for copy in copies:
        copy.start()
    vis_ref, coord_ref, block_ref, count_ref, offset_ref = targets
    below = in_low_half(group_count)
    order = exchange_order(band_count)
    slots = band_count * CAP
    blocks = vis_ref.shape[0]
    for copy in copies:
        copy.wait()
    block_index, count, offsets = block_ref[...], count_ref[...], offset_ref[...]
    lane = lax.broadcasted_iota(jnp.int32, (1, slots), 1)
    list_of = lane // CAP
    within = lane % CAP
    chosen = (
        lax.broadcasted_iota(jnp.int32, (blocks, slots), 0) == block_index
    ).astype(jnp.float32)
    vis = dot_first(chosen.astype(jnp.bfloat16), vis_ref[...])
    coord = dot_first(chosen.astype(jnp.bfloat16), coord_ref[...])
    here = lax.broadcasted_iota(jnp.int32, (CAP, slots), 0) == within
    high = jnp.where(here, (offsets >> 7).astype(jnp.float32), 0.0).astype(jnp.bfloat16)
    low = jnp.where(here, (offsets & 127).astype(jnp.float32), 0.0).astype(jnp.bfloat16)
    slot_row = lax.broadcasted_iota(jnp.int32, (slots, 128), 0) // CAP
    column = lax.broadcasted_iota(jnp.int32, (slots, 128), 1)
    to_high = (slot_row == column).astype(jnp.bfloat16)
    to_low = (slot_row + LO == column).astype(jnp.bfloat16)
    meta = jnp.dot(high, to_high, preferred_element_type=jnp.float32) + jnp.dot(
        low, to_low, preferred_element_type=jnp.float32
    )
    count = count.astype(jnp.float32)
    spread = jnp.concatenate([count, jnp.zeros((1, 128 - band_count), jnp.float32)], axis=1)
    slot_in = lax.broadcasted_iota(jnp.int32, (CAP, 128), 0).astype(jnp.float32)
    meta = meta + (slot_in < pltpu.roll(jnp.broadcast_to(spread, (CAP, 128)), LIVE, 1)).astype(jnp.float32)
    slot_in = slot_in[:, :1]
    for d in range(band_count):
        rows = slice(d * CAP, (d + 1) * CAP)
        shown = jnp.where(slot_in < count[:, d : d + 1], vis[rows], 0.0)
        message = jnp.concatenate([shown, coord[rows], meta], axis=1).astype(jnp.bfloat16)
        flipped = band_count - 1 - d
        out_ref[jnp.where(below, order.index((d, 0)), order.index((d, 1)))] = message
        out_ref[jnp.where(below, order.index((flipped, 1)), order.index((flipped, 0)))] = message


def square(z):
    re, im = z
    return re * re - im * im, 2.0 * (re * im)


def times(z, w):
    return z[0] * w[0] - z[1] * w[1], z[0] * w[1] + z[1] * w[0]


def unit_phasor(cycles):
    half = (cycles - jnp.round(cycles)) * PI
    x = half * half
    sine = jnp.full_like(x, SIN_TERMS[-1])
    for term in SIN_TERMS[-2::-1]:
        sine = sine * x + term
    cosine = jnp.full_like(x, COS_TERMS[-1])
    for term in COS_TERMS[-2::-1]:
        cosine = cosine * x + term
    sine = sine * half
    return 1.0 - 2.0 * (sine * sine), 2.0 * (sine * cosine)


def turn_table(rows, column, length):
    row = lax.broadcasted_iota(jnp.int32, column.shape, 0)

    def turns(factor):
        return unit_phasor(((factor * column) & (length - 1)).astype(jnp.float32) * (1.0 / length))

    parts = [turns(row)]
    step = turns(jnp.full_like(row, 8))
    for _ in range(rows // 8 - 1):
        parts.append(times(parts[-1], step))
    return tuple(jnp.concatenate([z[i] for z in parts], axis=0) for i in range(2))


def fill_tables(outer_ref, inner_ref, twist_ref):
    column = lax.broadcasted_iota(jnp.int32, (8, 128), 1)
    column_in = column & (N2 - 1)
    outer = turn_table(N1, column, N1)
    left = lax.broadcasted_iota(jnp.int32, (N2, 128), 1) < N2
    inner = [
        jnp.concatenate([jnp.where(left, z, 0.0), jnp.where(left, 0.0, z)], axis=0)
        for z in turn_table(N2, column_in, N2)
    ]
    for ref, (cosine, sine) in ((outer_ref, outer), (inner_ref, inner)):
        cosine, sine = cosine.astype(jnp.bfloat16), sine.astype(jnp.bfloat16)
        ref[:N1, :128] = cosine
        ref[:N1, 128:] = sine
        ref[N1:, :128] = -sine
        ref[N1:, 128:] = cosine
    scale = 1.0 / math.sqrt(G * K)
    twist = turn_table(N1, column_in, G)
    twist_ref[0] = twist[0] * scale
    twist_ref[1] = twist[1] * -scale


def grid_kernel(
    band_count,
    group_count,
    recv_ref,
    out_ref,
    outer_ref,
    inner_ref,
    twist_ref,
    offset_vmem,
    offset_smem,
    data_ref,
    tab_re,
    tab_im,
    eight_re,
    eight_im,
    last_ref,
    cells_ref,
    ends_ref,
    lines_ref,
    grid_ref,
    rows_ref,
    offset_sem,
    out_sem,
):
    below = in_low_half(group_count)
    band = lax.axis_index("band")

    slots = 2 * band_count * CAP
    flat = recv_ref[...].astype(jnp.float32).reshape(slots, ROW).astype(jnp.bfloat16)
    pick_row = lax.broadcasted_iota(jnp.int32, (8, 128), 0)
    pick_col = lax.broadcasted_iota(jnp.int32, (8, 128), 1)
    flipped = band_count - 1 - band
    wanted = jnp.full((8, 128), -1, jnp.int32)
    for i, at in enumerate((0, LO, LIVE)):
        wanted = jnp.where(pick_row == i, band + at, wanted)
        wanted = jnp.where(pick_row == i + 3, flipped + at, wanted)
    picked = dot_last((pick_col == wanted).astype(jnp.bfloat16), flat[:, DATA:])
    slot = lax.broadcasted_iota(jnp.int32, (1, slots), 1)
    from_low = jnp.zeros((1, slots), jnp.int32)
    for at, (_, half) in enumerate(exchange_order(band_count)):
        if half == 0:
            from_low = jnp.where(slot // CAP == at, 1, from_low)
    mine = from_low == below.astype(jnp.int32)
    high, low, live = (jnp.where(mine, picked[i : i + 1], picked[i + 3 : i + 4]) for i in range(3))
    offsets = (high * 128.0 + low).astype(jnp.int32)
    offsets = jnp.where(mine, offsets, (G - S) - offsets)

    live_own = jnp.where(mine, live, 0.0)
    live_mirror = live - live_own
    nothing = jnp.zeros((6, slots), jnp.float32)
    kinds = jnp.concatenate([live_own, live_mirror, nothing], axis=0).astype(jnp.bfloat16)
    earlier = (
        lax.broadcasted_iota(jnp.int32, (slots, slots), 0)
        < lax.broadcasted_iota(jnp.int32, (slots, slots), 1)
    ).astype(jnp.bfloat16)
    before = jnp.dot(kinds, earlier, preferred_element_type=jnp.float32)
    own_count, mirror_count = (jnp.sum(z, axis=1, keepdims=True) for z in (live_own, live_mirror))
    position = jnp.where(mine, before[0:1], before[1:2] + own_count)
    position = jnp.where(live > 0.5, position, -1.0).astype(jnp.int32)
    moves = (
        lax.broadcasted_iota(jnp.int32, (slots, slots), 0) == position
    ).astype(jnp.bfloat16)
    data_ref[...] = jnp.dot(moves, flat[:, :DATA], preferred_element_type=jnp.float32)
    parts = jnp.concatenate(
        [(offsets >> 7).astype(jnp.float32), (offsets & 127).astype(jnp.float32), nothing], axis=0
    )
    moved = dot_last(parts.astype(jnp.bfloat16), moves)
    offset_vmem[...] = jnp.concatenate(
        [
            moved[0:1] * 128.0 + moved[1:2],
            jnp.broadcast_to(own_count, (1, slots)),
            jnp.broadcast_to(own_count + mirror_count, (1, slots)),
            jnp.zeros((5, slots), jnp.float32),
        ],
        axis=0,
    ).astype(jnp.int32)
    to_smem = pltpu.make_async_copy(offset_vmem, offset_smem, offset_sem)
    to_smem.start()

    def clear(step, _):
        rows = pl.ds(pl.multiple_of(step * 24, 24), 24)
        for block in range(S // 8):
            grid_ref[block, rows, :] = jnp.zeros((24, 128), jnp.float32)
        return 0

    lax.fori_loop(0, grid_ref.shape[1] // 24, clear, 0)

    lane = lax.broadcasted_iota(jnp.int32, (8, 128), 1)
    first_half = lane < N2
    lane_in = lane & (N2 - 1)
    turn_sign = jnp.where(lax.broadcasted_iota(jnp.int32, (S, 128), 1) < N2, -1.0, 1.0)
    chunks = 2 * K // 128
    slot_in = lax.broadcasted_iota(jnp.int32, (CAP, K), 0)

    def add_cells(uppers, lowers, start, offset):
        row = (offset >> 6) * STEP
        shift = offset & (N2 - 1)
        near, far = (shift + 128 - start) & 127, (shift + N2 - start) & 127
        stays = (lane_in >= shift) & (lane_in < shift + S)
        wraps = lane_in < shift - (N2 - S)
        for block in range(HALF // 8):
            upper = uppers[block * 8 : block * 8 + 8]
            lower = lowers[block * 8 : block * 8 + 8]
            even = jnp.where(first_half, pltpu.roll(upper, near, 1), pltpu.roll(lower, far, 1))
            odd = jnp.where(first_half, pltpu.roll(upper, far, 1), pltpu.roll(lower, near, 1))
            for part, here, over in ((0, even, odd), (1, odd, even)):
                for at, piece in ((row, jnp.where(stays, here, 0.0)), (row + STEP, jnp.where(wraps, over, 0.0))):
                    rows = pl.ds(at, 8)
                    grid_ref[part * (HALF // 8) + block, rows, :] += piece

    def make_tables(group, own_slots):
        block = data_ref[pl.ds(pl.multiple_of(group * CAP, CAP), CAP), :]
        mirrored = slot_in >= own_slots - group * CAP
        vis = (block[:, 0:K], jnp.where(mirrored, -block[:, K : 2 * K], block[:, K : 2 * K]))
        e1 = unit_phasor(block[:, 2 * K : 4 * K] * (1.0 / S))
        e2 = square(e1)
        e4 = square(e2)
        cc, ss, cs, sc = e4[0] * e1[0], e4[1] * e1[1], e4[0] * e1[1], e4[1] * e1[0]
        e3, e5 = (cc + ss, sc - cs), (cc - ss, sc + cs)
        e8 = square(e4)
        one = (jnp.ones_like(e1[0]), jnp.zeros_like(e1[0]))
        steps = (one, e1, e2, e3, e4, e5, square(e3), times(e4, e3), e8)
        for b in range(8):
            x = tuple(jnp.where(mirrored, n[:, :K], z[:, :K]) for z, n in zip(steps[b], steps[b + 1]))
            weighted = times(vis, x)
            for tab, z, y in zip((tab_re, tab_im), weighted, steps[b]):
                for q in range(chunks):
                    piece = z if q < chunks // 2 else y
                    if b > 0 or q < chunks // 2:
                        tab[pl.ds(q * STEP * CAP + b, CAP, stride=STEP), :] = piece[:, q * 128 : (q + 1) * 128]
        eight_re[...] = e8[0]
        eight_im[...] = e8[1]
        last = square((e8[0][:, K:], e8[1][:, K:]))
        last_ref[...] = jnp.concatenate(last, axis=0).astype(jnp.bfloat16)

    def multiply():
        products = []
        for first in range(0, CAP, GROUP):
            left, real, imag = [], [], []
            for c in range(first, first + GROUP):
                base = tuple(
                    jnp.concatenate(
                        [tab[(q * CAP + c) * STEP : (q * CAP + c) * STEP + 8, :] for q in range(chunks)],
                        axis=1,
                    )
                    for tab in (tab_re, tab_im)
                )
                c8 = jnp.broadcast_to(eight_re[c : c + 1, :], (8, 2 * K))
                s8 = jnp.broadcast_to(eight_im[c : c + 1, :], (8, 2 * K))
                cc, ss, cs, sc = base[0] * c8, base[1] * s8, base[0] * s8, base[1] * c8
                up = (cc - ss, sc + cs)
                up_y = tuple(z[:, K:] for z in up)
                left += [
                    jnp.concatenate([z[:, K:], y], axis=0).astype(jnp.bfloat16) for z, y in zip(base, up_y)
                ]
                base, up, c8, s8 = (
                    tuple(z[:, :K] for z in base),
                    tuple(z[:, :K] for z in up),
                    c8[:, :K],
                    s8[:, :K],
                )
                down = (cc[:, :K] + ss[:, :K], sc[:, :K] - cs[:, :K])
                down2 = (down[0] * c8 + down[1] * s8, down[1] * c8 - down[0] * s8)
                order = (down2, down, base, up)
                real.append(jnp.concatenate([z[0] for z in order], axis=0).astype(jnp.bfloat16))
                imag.append(jnp.concatenate([z[1] for z in order], axis=0).astype(jnp.bfloat16))
            left.append(last_ref[...])
            right = []
            for c in range(0, GROUP, 2):
                right += real[c : c + 2] + imag[c : c + 2]
            cells = dot_last(jnp.concatenate(left, axis=0), jnp.concatenate(right, axis=0))
            products.append(cells)
        return products

    def keep(products):
        for c in range(CAP):
            row, tile = c % GROUP * S, c % GROUP // 2 * 128
            cells_ref[c * S : (c + 1) * S, :] = products[c // GROUP][row : row + S, tile : tile + 128]
        for i, product in enumerate(products):
            for tile in range(GROUP // 2):
                at = (i * (GROUP // 2) + tile) * 2 * CAP
                ends_ref[at : at + 2 * CAP, :] = product[GROUP * S :, tile * 128 : (tile + 1) * 128]

    def both_signs(by_cos, by_sin):
        by_sin = turn_sign[: by_sin.shape[0]] * pltpu.roll(by_sin, N2, 1)
        return by_cos + by_sin, by_cos - by_sin

    def add_group(group):
        for c in range(CAP):
            mirrored = (group * CAP + c >= own_slots).astype(jnp.int32)
            at = c // 2 * 2 * CAP
            if c % 2 == 0:
                end_right, end_left = both_signs(
                    ends_ref[at : at + CAP, :], ends_ref[at + CAP : at + 2 * CAP, :]
                )
            right, left = both_signs(
                cells_ref[c * S : c * S + HALF, :], cells_ref[c * S + HALF : (c + 1) * S, :]
            )
            line = c * 2 * S
            lines_ref[line : line + HALF, :] = right
            lines_ref[line + HALF : line + HALF + 1, :] = end_right[c : c + 1]
            lines_ref[line + S : line + S + HALF, :] = left
            lines_ref[line + S - 1 : line + S, :] = left[HALF - 1 :]
            lines_ref[line + S : line + S + 1, :] = jnp.where(mirrored == 1, left[0:1], end_left[c : c + 1])
            add_cells(
                lines_ref[pl.ds(line + S - mirrored, HALF), :],
                lines_ref[pl.ds(line + mirrored, HALF), :],
                c % 2 * S,
                offset_smem[0, group * CAP + c],
            )

    for tab, first in ((tab_re, 1.0), (tab_im, 0.0)):
        for q in range(chunks // 2, chunks):
            tab[pl.ds(q * STEP * CAP, CAP, stride=STEP), :] = jnp.full((CAP, 128), first, jnp.float32)
    make_tables(0, jnp.int32(CAP))
    keep(multiply())
    to_smem.wait()
    own_slots, groups = offset_smem[1, 0], pl.cdiv(offset_smem[2, 0], CAP)

    def tables_of(group):
        make_tables(jnp.minimum(group, groups - 1), own_slots)

    tables_of(1)

    def turn(group, _):
        products = multiply()
        add_group(group - 1)
        keep(products)
        tables_of(group + 1)
        return 0

    lax.fori_loop(1, groups, turn, 0)
    fill_tables(outer_ref, inner_ref, twist_ref)
    add_group(groups - 1)

    def out_copy(part, group):
        rows = pl.ds(group * 8 * N2, 8 * N2)
        return pltpu.make_async_copy(
            rows_ref.at[part, rows, :], out_ref.at[part, rows, :], out_sem.at[part, group]
        )

    twist_re, twist_im = twist_ref[0], twist_ref[1]
    for pair in range(HALF // 2):
        lines = (2 * pair, 2 * pair + 1)
        field = jnp.concatenate(
            [
                jnp.concatenate(
                    [
                        grid_ref[
                            part * (HALF // 8) + y // 8, pl.ds(y % 8, N1, stride=STEP), :
                        ].astype(jnp.bfloat16)
                        for y in lines
                    ],
                    axis=1,
                )
                for part in range(2)
            ],
            axis=0,
        )
        section = jnp.dot(outer_ref[...], field, preferred_element_type=jnp.float32)
        twisted = []
        for p in range(2):
            re = section[:N1, p * 128 : (p + 1) * 128]
            im = section[N1:, p * 128 : (p + 1) * 128]
            twisted.append(
                jnp.concatenate(
                    [re * twist_re - im * twist_im, re * twist_im + im * twist_re], axis=1
                ).astype(jnp.bfloat16)
            )
        spectrum = dot_last(inner_ref[...], jnp.concatenate(twisted, axis=0))
        for part in range(2):
            for half in range(2):
                for p, y in enumerate(lines):
                    start = (part * 2 + half) * N2
                    line = HALF + y if half else (HALF - y) % HALF
                    rows_ref[part, pl.ds((line // 8) * 8 * N2 + line % 8, N2, stride=8), :] = spectrum[
                        start : start + N2, p * 128 : (p + 1) * 128
                    ]
        done = {7: (2,), 9: (1,), 15: (0, 3)}.get(lines[1], ())
        for part in range(2):
            for group in done:
                out_copy(part, group).start()
    for part in range(2):
        for group in range(S // 8):
            out_copy(part, group).wait()


def shards(visibilities, coordinates, block_index, counts, col_offset):
    band_count = lax.axis_size("band")
    group_count = lax.axis_size("wgrp")
    peers = 2 * band_count
    vmem = pl.BlockSpec(memory_space=pltpu.VMEM)
    hbm = pl.BlockSpec(memory_space=pltpu.HBM)
    inputs = [
        pltpu.with_memory_space_constraint(a, pltpu.HBM)
        for a in (visibilities[0], coordinates[0], block_index, counts, col_offset)
    ]
    message = pl.pallas_call(
        functools.partial(pack_kernel, band_count, group_count),
        out_shape=jax.ShapeDtypeStruct((peers, CAP, ROW), jnp.bfloat16),
        in_specs=[pl.BlockSpec(memory_space=pltpu.HBM)] * len(inputs),
        out_specs=vmem,
        scratch_shapes=[pltpu.VMEM(a.shape, a.dtype) for a in inputs]
        + [pltpu.SemaphoreType.DMA((len(inputs),))],
        compiler_params=pltpu.CompilerParams(vmem_limit_bytes=48 * 2**20),
        name="pack_blocks",
    )(*inputs)
    groups = [
        [b * group_count + (q if half == 0 else group_count - 1 - q) for b, half in exchange_order(band_count)]
        for q in range(group_count // 2)
    ]
    received = lax.all_to_all(
        message, ("band", "wgrp"), 0, 0, axis_index_groups=groups, tiled=True
    )
    slots = peers * CAP
    base = pltpu.VMEM((2 * K // 128 * STEP * CAP + 8, 128), jnp.float32)
    step = pltpu.VMEM((CAP, 2 * K), jnp.float32)
    rows = pl.pallas_call(
        functools.partial(grid_kernel, band_count, group_count),
        out_shape=jax.ShapeDtypeStruct((2, S * N2, N1), jnp.float32),
        in_specs=[vmem],
        out_specs=pl.BlockSpec(memory_space=pl.ANY),
        scratch_shapes=[
            pltpu.VMEM((2 * N1, 256), jnp.bfloat16),
            pltpu.VMEM((2 * N1, 256), jnp.bfloat16),
            pltpu.VMEM((2, N1, 128), jnp.float32),
            pltpu.VMEM((8, slots), jnp.int32),
            pltpu.SMEM((8, slots), jnp.int32),
            pltpu.VMEM((slots, DATA), jnp.float32),
            base,
            base,
            step,
            step,
            pltpu.VMEM((2 * CAP, K), jnp.bfloat16),
            pltpu.VMEM((CAP * S, 128), jnp.float32),
            pltpu.VMEM((CAP // 2 * 2 * CAP, 128), jnp.float32),
            pltpu.VMEM((CAP * 2 * S, 128), jnp.float32),
            pltpu.VMEM((S // 8, pl.cdiv((N1 + 2) * STEP, 24) * 24, 128), jnp.float32),
            pltpu.VMEM((2, S * N2 + 8, N1), jnp.float32),
            pltpu.SemaphoreType.DMA(()),
            pltpu.SemaphoreType.DMA((2, S // 8)),
        ],
        compiler_params=pltpu.CompilerParams(vmem_limit_bytes=48 * 2**20),
        name="grid_and_transform",
    )(received)
    lines = rows.reshape(1, 2, S // 8, N2, 8, N1).transpose(0, 1, 2, 4, 3, 5)
    return lines.reshape(1, 2, S, G)


def solution(mesh):
    placed = (
        P("wgrp", "band", None),
        P("wgrp", "band", None),
        P("wgrp", "band"),
        P("wgrp", "band"),
        P("wgrp", "band"),
    )
    return jax.shard_map(
        shards, mesh=mesh, in_specs=placed, out_specs=P("wgrp", None, "band", None), check_vma=False
    )
```
